128 devices in a mesh: dp: 2 (over z_lo), ctx: 32 (over x, z_hi, y), tensor: 2 (over core).
Axes of the slice: x: 4, y: 4, z: 4 (z_hi: 2, z_lo: 2; z = z_hi * 2 + z_lo), core: 2. Of those that a mesh axis runs over, the one named last changes fastest.
Arguments:
- tokens: bfloat16 [4, 4096, 1536], P('dp', 'ctx'), may hold values from -6 to 6
- w_query: bfloat16 [1536, 1536], P('dp', 'tensor'), may hold values from -0.21875 to 0.21875
- key_projection_weight: bfloat16 [1536, 512], P('dp', 'tensor'), may hold values from -0.21875 to 0.21875
- value_projection_weight: bfloat16 [1536, 512], P('dp', 'tensor'), may hold values from -0.15625 to 0.15625
- w_out: bfloat16 [1536, 1536], P('tensor', 'dp'), may hold values from -3 to 3
- w_gate: bfloat16 [1536, 3840], P('dp', 'tensor'), may hold values from -0.15625 to 0.15625
- w_up: bfloat16 [1536, 3840], P('dp', 'tensor'), may hold values from -0.15625 to 0.15625
- w_down: bfloat16 [3840, 1536], P('tensor', 'dp'), may hold values from -0.75 to 0.75
- norm_attn: bfloat16 [1536], P('dp'), may hold values from 0.5 to 1.5
- norm_ffn: bfloat16 [1536], P('dp'), may hold values from 0.5 to 1.5
- doc_lengths: int32 [4, 4], P('dp'), may hold values from 1 to 4093, as said below
- valid_mask: int32 [4, 4096], P('dp', 'ctx'), may hold values from 0 to 1, as said below
- teacher: bfloat16 [4, 4096, 1536], P('dp', 'ctx'), may hold values from -6 to 6
Outputs:
- layer_out: bfloat16 [4, 4096, 1536], P('dp', 'ctx')
- loss_value: float32 [], replicated
- grad_tokens: float32 [4, 4096, 1536], P('dp', 'ctx')
- grad_query: float32 [1536, 1536], P('dp', 'tensor')
- grad_key: float32 [1536, 512], P('dp', 'tensor')
- grad_value: float32 [1536, 512], P('dp', 'tensor')
- grad_out: float32 [1536, 1536], P('tensor', 'dp')
- grad_gate: float32 [1536, 3840], P('dp', 'tensor')
- grad_up: float32 [1536, 3840], P('dp', 'tensor')
- down_weight_gradient: float32 [3840, 1536], P('tensor', 'dp')
- grad_norm_attn: float32 [1536], P('dp')
- grad_norm_ffn: float32 [1536], P('dp')
The draws below stay inside these ranges and needn't reach their ends.
Inputs may be any that keep to these rules, and one draw needn't show every extreme that they name: `doc_lengths`: the 4 lengths of a sequence sum to 4096; in each sequence one document starts within the first 128 tokens and ends within the last 128, and the other three have 1 to 32 tokens each; in exactly one of the four sequences those three have one token each. `valid_mask`: the last token of each sequence has a 1.
All inputs are finite; a program needn't handle non-finite values.
Results may differ from the reference program's by a relative error of at most 0.029.
Values may be sent and summed in bfloat16 or wider, within the bound.
No kernel may reach another device: no remote copies, remote signals or barrier semaphores. Data moves between devices by JAX's collectives and lax.ppermute only.
A program may use at most 192 MiB of HBM per device.

```python
import math
import jax
import jax.numpy as jnp
from jax import lax

MODEL_WIDTH = 1536
HEADS = 24
KV_HEADS = 8
HEAD = 64
FF = 3840
BLK = 128
WINDOW = 1024
NDOC = 4
SEQ_LEN = 4096
SEQS = 4
TOKENS = 16384
HQ = 1536
KEY_COLUMNS = 512
N_CTX = 32


def draw_doc_lengths(key, part):
    key = jax.random.fold_in(key, 11)
    short_key, place_key, single_key = jax.random.split(key, 3)
    shorts = jax.random.randint(short_key, (SEQS, NDOC), 1, BLK // NDOC + 1, dtype=jnp.int32)
    single_row = jax.random.randint(single_key, (1, 1), 0, SEQS, dtype=jnp.int32)
    row_ids = jnp.arange(SEQS, dtype=jnp.int32)[:, None]
    shorts = jnp.where(row_ids == single_row, 1, shorts)
    long_place = jax.random.randint(place_key, (SEQS, 1), 0, NDOC, dtype=jnp.int32)
    columns = jnp.arange(NDOC, dtype=jnp.int32)[None, :]
    is_long = columns == long_place
    others = jnp.sum(jnp.where(is_long, 0, shorts), axis=1, keepdims=True)
    return jnp.where(is_long, SEQ_LEN - others, shorts).astype(jnp.int32)


def draw_valid_mask(key, part):
    key = jax.random.fold_in(key, 23)
    positions = jnp.arange(SEQ_LEN, dtype=jnp.int32)[None, :]
    threshold = 25 + 60 * positions // SEQ_LEN
    dice_rolls = jax.random.randint(key, (SEQS, SEQ_LEN), 0, 100, dtype=jnp.int32)
    valid_flags = (dice_rolls < threshold).astype(jnp.int32)
    return jnp.where(positions == SEQ_LEN - 1, 1, valid_flags).astype(jnp.int32)


def level_of(key, shape, cuts, smallest, high):
    gain, own = 1.0, jax.random.fold_in(key, 6)
    for dim, parts in cuts:
        steps = jnp.exp(jax.random.uniform(jax.random.fold_in(own, dim), (parts,), jnp.float32, smallest / len(cuts), high / len(cuts)))
        gain = gain * jnp.repeat(steps, shape[dim] // parts).reshape([-1 if axis == dim else 1 for axis in range(len(shape))])
    return gain


def noise(key, extent, spread, reach, cuts=(), kind=jnp.bfloat16):
    entries = spread * jax.random.normal(key, extent, jnp.float32)
    if cuts:
        entries = entries * level_of(key, extent, cuts, -0.22, 0.18)
    return jnp.clip(entries, -reach, reach).astype(kind)


def setup_inputs(seed: int = 0) -> dict:
    seeds = jax.random.split(jax.random.key(seed), 14)
    tokens = noise(seeds[0], (SEQS, SEQ_LEN, MODEL_WIDTH), 1.0, 6.0, ((0, 2), (1, 32)))
    w_query = noise(seeds[1], (MODEL_WIDTH, HQ), (MODEL_WIDTH // 2) ** -0.5, 0.21875, ((0, 2), (1, 2)))
    key_projection_weight = noise(seeds[2], (MODEL_WIDTH, KEY_COLUMNS), (MODEL_WIDTH // 2) ** -0.5, 0.21875, ((0, 2), (1, 2)))
    value_projection_weight = noise(seeds[3], (MODEL_WIDTH, KEY_COLUMNS), MODEL_WIDTH ** -0.5, 0.15625, ((0, 2), (1, 2)))
    w_out = noise(seeds[4], (HQ, MODEL_WIDTH), 4 ** -0.5, 3.0, ((0, 2), (1, 2)))
    w_gate = noise(seeds[5], (MODEL_WIDTH, FF), MODEL_WIDTH ** -0.5, 0.15625, ((0, 2), (1, 2)))
    w_up = noise(seeds[6], (MODEL_WIDTH, FF), MODEL_WIDTH ** -0.5, 0.15625, ((0, 2), (1, 2)))
    w_down = noise(seeds[7], (FF, MODEL_WIDTH), (FF // 64) ** -0.5, 0.75, ((0, 2), (1, 2)))
    norm_attn = jnp.clip(1.0 + 0.1 * jax.random.normal(seeds[8], (MODEL_WIDTH,), jnp.float32), 0.5, 1.5).astype(jnp.bfloat16)
    norm_ffn = jnp.clip(1.0 + 0.1 * jax.random.normal(seeds[9], (MODEL_WIDTH,), jnp.float32), 0.5, 1.5).astype(jnp.bfloat16)
    doc_lengths = draw_doc_lengths(jax.random.fold_in(seeds[13], 71), 0)
    valid_mask = draw_valid_mask(jax.random.fold_in(seeds[13], 71), 0)
    teacher = noise(seeds[12], (SEQS, SEQ_LEN, MODEL_WIDTH), 1.0, 6.0, ((0, 2), (1, 32)))
    return {"tokens": tokens, "w_query": w_query, "key_projection_weight": key_projection_weight, "value_projection_weight": value_projection_weight, "w_out": w_out, "w_gate": w_gate, "w_up": w_up, "w_down": w_down, "norm_attn": norm_attn, "norm_ffn": norm_ffn, "doc_lengths": doc_lengths, "valid_mask": valid_mask, "teacher": teacher}


branch_scale = 1.4 / math.sqrt(52.0)
norm_epsilon = 1e-05
masked_score = -1e+30
top_precision = lax.Precision.HIGHEST

@jax.custom_vjp
def low(v):
    return lax.optimization_barrier(v.astype(jnp.bfloat16)).astype(jnp.float32)

@jax.custom_vjp
def low_back(v):
    return v

def low_keep(v):
    return (low(v), None)

def low_pass(kept, grad):
    return (grad,)

def back_keep(v):
    return (v, None)

def back_low(kept, grad):
    return (low(grad),)
low.defvjp(low_keep, low_pass)
low_back.defvjp(back_keep, back_low)

def matmul(left, right):
    return jnp.dot(left, right, precision=top_precision, preferred_element_type=jnp.float32)

def rms_scale(source, gain_vec):
    inverse = lax.rsqrt(lax.optimization_barrier(jnp.mean(source * source, axis=-1, keepdims=True)) + norm_epsilon)
    return source * inverse * gain_vec

def document_index(positions, bounds):
    return lax.optimization_barrier(jnp.sum((positions[:, None] >= bounds[None, :]).astype(jnp.int32), axis=1))

def attend(queries, keys_all, values_all, bounds):
    seq_len = queries.shape[0]
    block_rows = BLK * min(N_CTX, max(1, 512 // BLK))
    group_size = HEADS // KV_HEADS
    padding = jnp.zeros((WINDOW, KV_HEADS, HEAD), keys_all.dtype)
    keys_pad = jnp.concatenate([padding, keys_all.reshape(seq_len, KV_HEADS, HEAD)], axis=0)
    values_pad = jnp.concatenate([padding, values_all.reshape(seq_len, KV_HEADS, HEAD)], axis=0)
    query_groups = queries.reshape(seq_len, KV_HEADS, group_size, HEAD)
    scale_factor = 1.0 / math.sqrt(HEAD)

    def one_block(block_start):
        query_block = lax.dynamic_slice_in_dim(query_groups, block_start, block_rows, 0)
        key_block = lax.dynamic_slice_in_dim(keys_pad, block_start, WINDOW + block_rows, 0)
        value_block = lax.dynamic_slice_in_dim(values_pad, block_start, WINDOW + block_rows, 0)
        query_pos = block_start + jnp.arange(block_rows, dtype=jnp.int32)
        key_pos = block_start - WINDOW + jnp.arange(WINDOW + block_rows, dtype=jnp.int32)
        query_doc = document_index(query_pos, bounds)
        key_doc = document_index(key_pos, bounds)
        distance = query_pos[:, None] - key_pos[None, :]
        allowed = (distance >= 0) & (distance < WINDOW) & (key_pos[None, :] >= 0) & (query_doc[:, None] == key_doc[None, :])
        scores = jnp.einsum('rkge,ske->kgrs', query_block, key_block, precision=top_precision) * scale_factor
        scores = jnp.where(allowed, low_back(scores), masked_score)
        probabilities = low(jax.nn.softmax(scores, axis=-1))
        attended = jnp.einsum('kgrs,ske->rkge', probabilities, value_block, precision=top_precision)
        return low_back(low(attended.reshape(block_rows, HEADS * HEAD)))
    starts = jnp.arange(seq_len // block_rows, dtype=jnp.int32) * block_rows
    outputs = lax.map(jax.checkpoint(one_block), starts)
    return outputs.reshape(seq_len, HEADS * HEAD)

def forward(tokens, w_query, key_projection_weight, value_projection_weight, w_out, w_gate, w_up, w_down, norm_attn, norm_ffn, bounds):
    normed_one = low(rms_scale(tokens, norm_attn))
    queries = low_back(low(matmul(normed_one, w_query)))
    keys_all = low_back(low(matmul(normed_one, key_projection_weight)))
    values_all = low_back(low(matmul(normed_one, value_projection_weight)))
    attended = jnp.stack([attend(queries[seq_index], keys_all[seq_index], values_all[seq_index], bounds[seq_index]) for seq_index in range(SEQS)])
    mixed = low_back(matmul(attended, w_out))
    hidden_state = tokens + branch_scale * mixed
    normed_two = low(rms_scale(hidden_state, norm_ffn))
    gate_pre = low_back(matmul(normed_two, w_gate))
    up_pre = low_back(matmul(normed_two, w_up))
    activated = low_back(low(jax.nn.silu(gate_pre) * up_pre))
    branch_out = low_back(matmul(activated, w_down))
    return hidden_state + branch_scale * branch_out

def reference(tokens, w_query, key_projection_weight, value_projection_weight, w_out, w_gate, w_up, w_down, norm_attn, norm_ffn, doc_lengths, valid_mask, teacher):
    bounds = jnp.cumsum(doc_lengths, axis=1).astype(jnp.int32)

    def closed(*weights):
        return forward(*weights, bounds)
    inputs = (tokens, w_query, key_projection_weight, value_projection_weight, w_out, w_gate, w_up, w_down, norm_attn, norm_ffn)
    final_state, pullback = jax.vjp(closed, *[item.astype(jnp.float32) for item in inputs])
    mask_values = valid_mask.astype(jnp.float32)
    valid_count = jnp.sum(mask_values)
    deviation = final_state - teacher.astype(jnp.float32)
    loss_value = jnp.sum(mask_values * lax.optimization_barrier(jnp.mean(deviation * deviation, axis=-1))) / valid_count
    cotangent = deviation * mask_values[..., None] * (TOKENS / valid_count)
    grads = pullback(cotangent)
    return (final_state.astype(jnp.bfloat16), loss_value, grads[0], grads[1], grads[2], grads[3], grads[4], grads[5], grads[6], grads[7], grads[8], grads[9])
```

```python
import math

import jax
import jax.numpy as jnp
from jax import lax
from jax.sharding import Mesh
from jax.sharding import PartitionSpec as P

HEAD = 64
WINDOW = 1024
BLOCK = 128
GROUP = 3

branch_scale = 1.4 / math.sqrt(52.0)
norm_epsilon = 1e-05
masked_score = -1e30
scale_factor = 1.0 / math.sqrt(HEAD)
bf16 = jnp.bfloat16
f32 = jnp.float32


def dot(left, right):
    return jnp.dot(left, right, preferred_element_type=f32)


def dot_nt(left, right):
    return lax.dot_general(left, right, (((1,), (1,)), ((), ())), preferred_element_type=f32)


def dot_tn(left, right):
    return lax.dot_general(left, right, (((0,), (0,)), ((), ())), preferred_element_type=f32)


def z_move(value, distance):
    route = []
    for dp in range(2):
        for hi in range(2):
            z = (hi * 2 + dp + distance) % 4
            route.append((dp * 2 + hi, (z % 2) * 2 + z // 2))
    return lax.ppermute(value, ("dp", "z_hi"), route)


def ring_move(value, axis, distance):
    size = lax.axis_size(axis)
    return lax.ppermute(value, axis, [(i, (i + distance) % size) for i in range(size)])


def group_move(value, distance):
    return lax.ppermute(
        value, ("x", "z_hi"), [(i, i + distance) for i in range(8) if 0 <= i + distance < 8]
    )


def swap(value, axis):
    return lax.ppermute(value, axis, [(0, 1), (1, 0)])


PAIRS = {"even": ((0, 1), (1, 0), (2, 3), (3, 2)), "odd": ((0, 3), (3, 0), (1, 2), (2, 1))}


def pair_move(value, step):
    return lax.ppermute(value, step[0], PAIRS[step[1]])


def pair_bit(step):
    index = lax.axis_index(step[0])
    return (index // 2 + index) % 2 if step[1] == "even" else index // 2


def core_sum(part):
    return part.astype(f32) + swap(part, "tensor").astype(f32)


def total_sum(value):
    for step in (("x", "even"), ("x", "odd"), ("y", "even"), ("y", "odd")):
        value = value + pair_move(value, step)
    return value + swap(value, "z_hi")


ORDERS = (
    (("x", "even"), ("x", "odd"), ("y", "even"), ("y", "odd")),
    (("x", "odd"), ("x", "even"), ("y", "odd"), ("y", "even")),
    (("y", "even"), ("y", "odd"), ("x", "even"), ("x", "odd")),
    (("y", "odd"), ("y", "even"), ("x", "odd"), ("x", "even")),
)


def halve(value, step):
    bit = pair_bit(step)
    half = value.shape[0] // 2
    keep = lax.dynamic_slice_in_dim(value, bit * half, half, 0)
    send = lax.dynamic_slice_in_dim(value, (1 - bit) * half, half, 0)
    return (keep.astype(f32) + pair_move(send, step).astype(f32)).astype(bf16)


def double(value, step):
    other = pair_move(value, step)
    return jnp.where(
        pair_bit(step) == 0,
        jnp.concatenate([value, other], axis=0),
        jnp.concatenate([other, value], axis=0),
    )


def reduce_channels(channels):
    channels = list(channels)
    for level in range(4):
        channels = [halve(c, ORDERS[i][level]) for i, c in enumerate(channels)]
    channels = [(c.astype(f32) + swap(c, "z_hi").astype(f32)).astype(bf16) for c in channels]
    for level in (3, 2, 1, 0):
        channels = [double(c, ORDERS[i][level]) for i, c in enumerate(channels)]
    return channels


def inverse_rms(source):
    return lax.rsqrt(jnp.mean(source * source, axis=-1, keepdims=True) + norm_epsilon)


def norm_backward(source, inverse, gain_vec, grad_normed):
    weighted = grad_normed * gain_vec
    grad_source = inverse * weighted - source * (inverse * inverse * inverse) * jnp.mean(
        source * weighted, axis=-1, keepdims=True
    )
    grad_gain = jnp.sum(grad_normed * source * inverse, axis=0)
    return (grad_source, grad_gain)


def stack_heads(rows, group):
    first = group * GROUP * HEAD
    return jnp.concatenate(
        [rows[:, first + j * HEAD : first + (j + 1) * HEAD] for j in range(GROUP)], axis=0
    )


def unstack_heads(stacked):
    return jnp.concatenate([stacked[j * BLOCK : (j + 1) * BLOCK] for j in range(GROUP)], axis=1)


def masked_scores(q3, keys, allowed):
    scores = dot_nt(q3, keys) * scale_factor
    return jnp.where(allowed, scores, masked_score)


def attention_forward(queries, window, masks):
    rows, logs = [], []
    for r in range(4):
        q = queries[r * BLOCK : (r + 1) * BLOCK]
        keys_here = window[r * BLOCK : r * BLOCK + WINDOW + BLOCK]
        outs = []
        for g in range(2):
            keys = keys_here[:, g * HEAD : (g + 1) * HEAD]
            values = keys_here[:, 128 + g * HEAD : 128 + (g + 1) * HEAD]
            scores = masked_scores(stack_heads(q, g), keys, masks[r])
            top = jnp.max(scores, axis=-1, keepdims=True)
            log_total = top + jnp.log(jnp.sum(jnp.exp(scores - top), axis=-1, keepdims=True))
            probabilities = jnp.exp(scores - log_total).astype(bf16)
            outs.append(unstack_heads(dot(probabilities, values).astype(bf16)))
            logs.append(log_total)
        rows.append(jnp.concatenate(outs, axis=1))
    return jnp.concatenate(rows, axis=0), logs


def attention_backward(queries, window, masks, logs, grad_out):
    query_rows = []
    grad_window = [jnp.zeros((BLOCK, 256), f32) for _ in range(12)]
    for r in range(4):
        q = queries[r * BLOCK : (r + 1) * BLOCK]
        grad_rows = grad_out[r * BLOCK : (r + 1) * BLOCK]
        keys_here = window[r * BLOCK : r * BLOCK + WINDOW + BLOCK]
        outs, key_grads, value_grads = [], [], []
        for g in range(2):
            keys = keys_here[:, g * HEAD : (g + 1) * HEAD]
            values = keys_here[:, 128 + g * HEAD : 128 + (g + 1) * HEAD]
            q3, g3 = stack_heads(q, g), stack_heads(grad_rows, g)
            probs = jnp.exp(masked_scores(q3, keys, masks[r]) - logs[2 * r + g])
            grad_probs = dot_nt(g3, values)
            inner = jnp.sum(grad_probs * probs, axis=-1, keepdims=True)
            grad_scores = (probs * (grad_probs - inner)).astype(bf16)
            outs.append(unstack_heads((dot(grad_scores, keys) * scale_factor).astype(bf16)))
            key_grads.append(dot_tn(grad_scores, q3) * scale_factor)
            value_grads.append(dot_tn(probs.astype(bf16), g3))
        query_rows.append(jnp.concatenate(outs, axis=1))
        block = jnp.concatenate(key_grads + value_grads, axis=1)
        for b in range(9):
            grad_window[r + b] = grad_window[r + b] + block[b * BLOCK : (b + 1) * BLOCK]
    return jnp.concatenate(query_rows, axis=0), grad_window


def after(value, *others):
    return lax.optimization_barrier((value, *others))[0]


def local(
    tokens,
    w_query,
    key_projection_weight,
    value_projection_weight,
    w_out,
    w_gate,
    w_up,
    w_down,
    norm_attn,
    norm_ffn,
    doc_lengths,
    valid_mask,
    teacher,
):
    seq_count, row_count, width = tokens.shape
    rows = seq_count * row_count
    half = width // 2
    quarter = width // 4
    dp = lax.axis_index("dp")
    x_odd = lax.axis_index("x") % 2
    y_index = lax.axis_index("y")
    group_index = lax.axis_index("x") * 2 + lax.axis_index("z_hi")

    def to_local(value):
        own = jnp.where(dp == 0, value[..., :half], value[..., half:])
        other = jnp.where(dp == 0, value[..., half:], value[..., :half])
        first = jnp.where(x_odd == 0, other[..., :quarter], other[..., quarter:])
        second = jnp.where(x_odd == 0, other[..., quarter:], other[..., :quarter])
        return jnp.concatenate([own, first, second], axis=-1)

    def other_half(value):
        first, second = value[..., half : half + quarter], value[..., half + quarter :]
        return jnp.concatenate(
            [jnp.where(x_odd == 0, first, second), jnp.where(x_odd == 0, second, first)], axis=-1
        )

    def from_local(value):
        own, other = value[..., :half], other_half(value)
        return jnp.concatenate(
            [jnp.where(dp == 0, own, other), jnp.where(dp == 0, other, own)], axis=-1
        )

    def two_ways(first, second):
        return z_move(first, 1), z_move(second, -1)

    def fetch(piece):
        length = piece.shape[0] // 2
        one, two = two_ways(piece[:length], piece[length:])
        return (
            jnp.concatenate([one, two], axis=0),
            jnp.concatenate([ring_move(one, "x", 1), ring_move(two, "x", -1)], axis=0),
        )

    def to_neighbours(value):
        one, two = two_ways(value[:row_count], value[row_count:])
        return jnp.concatenate([one, two], axis=0)

    w_attn = jnp.concatenate(
        [
            part
            for p in range(2)
            for part in (
                w_query[:, p * 384 : (p + 1) * 384],
                key_projection_weight[:, p * 128 : (p + 1) * 128],
                value_projection_weight[:, p * 128 : (p + 1) * 128],
            )
        ],
        axis=1,
    )
    w_attn_send = jnp.where(
        x_odd == 0, w_attn, jnp.concatenate([w_attn[quarter:], w_attn[:quarter]], axis=0)
    )
    attn_one, attn_two = two_ways(w_attn_send[:quarter], w_attn_send[quarter:])
    attn_full = jnp.concatenate([w_attn, attn_one, attn_two], axis=0)
    gains = jnp.stack([norm_attn, norm_ffn])
    gains_other = swap(gains, "dp")
    gains_first = jnp.where(x_odd == 0, gains_other[:, :quarter], gains_other[:, quarter:])
    gains_second = jnp.where(x_odd == 0, gains_other[:, quarter:], gains_other[:, :quarter])
    gains_full = jnp.concatenate([gains, gains_first, gains_second], axis=1).astype(f32)
    gain_one, gain_two = gains_full[0], gains_full[1]

    mask_values = valid_mask.reshape(rows).astype(f32)
    local_count = jnp.full((8, 128), jnp.sum(mask_values), f32)
    count = total_sum(local_count + swap(local_count, "dp"))
    valid_count = count[0, 0]

    def column_piece(weight):
        return lax.dynamic_slice_in_dim(weight, x_odd * quarter, quarter, 1)

    def row_piece(weight):
        return lax.dynamic_slice_in_dim(weight, x_odd * quarter, quarter, 0)

    out_first, out_second = fetch(after(column_piece(w_out), attn_one, attn_two))
    gate_first, gate_second = fetch(after(row_piece(w_gate), out_first))
    up_first, up_second = fetch(after(row_piece(w_up), gate_first))
    down_first, down_second = fetch(after(column_piece(w_down), up_first))
    out_full = jnp.concatenate([w_out, out_first, out_second], axis=1)
    gate_full = jnp.concatenate([w_gate, gate_first, gate_second], axis=0)
    up_full = jnp.concatenate([w_up, up_first, up_second], axis=0)
    down_full = jnp.concatenate([w_down, down_first, down_second], axis=1)

    residual_in = to_local(tokens.reshape(rows, width)).astype(f32)
    inverse_one = inverse_rms(residual_in)
    normed_one = (residual_in * inverse_one * gain_one).astype(bf16)
    projected = jnp.concatenate(
        [dot(normed_one, attn_full[:, :640]), dot(normed_one, attn_full[:, 640:])], axis=0
    ).astype(bf16)
    mine = lax.all_to_all(projected, "y", 0, 0, tiled=True)
    queries, key_values = mine[:, :384], mine[:, 384:]
    window = jnp.concatenate(
        [group_move(key_values, 2), group_move(key_values, 1), key_values], axis=0
    )
    bounds = jnp.cumsum(
        lax.dynamic_index_in_dim(doc_lengths, y_index % 2, 0, keepdims=False)
    )
    masks = []
    for r in range(4):
        query_pos = group_index * 512 + r * BLOCK + jnp.arange(BLOCK, dtype=jnp.int32)
        key_pos = query_pos[0] - WINDOW + jnp.arange(WINDOW + BLOCK, dtype=jnp.int32)
        starts = jnp.max(
            jnp.where(query_pos[:, None] >= bounds[None, :], bounds[None, :], 0), axis=1
        )
        lowest = jnp.maximum(starts, query_pos - (WINDOW - 1))
        allowed = (key_pos[None, :] >= lowest[:, None]) & (key_pos[None, :] <= query_pos[:, None])
        masks.append(jnp.concatenate([allowed] * GROUP, axis=0))
    attended_mine, logs = attention_forward(queries, window, masks)
    returned = lax.all_to_all(attended_mine, "y", 0, 0, tiled=True)
    attended = jnp.concatenate([returned[:rows], returned[rows:]], axis=1)

    attn_total = core_sum(dot(attended, out_full).astype(bf16))
    hidden_state = residual_in + branch_scale * attn_total
    inverse_two = inverse_rms(hidden_state)
    normed_two = (hidden_state * inverse_two * gain_two).astype(bf16)
    gate_pre = dot(normed_two, gate_full)
    up_pre = dot(normed_two, up_full)
    sigmoid_gate = jax.nn.sigmoid(gate_pre)
    silu_gate = gate_pre * sigmoid_gate
    activated = (silu_gate * up_pre).astype(bf16)
    ffn_total = core_sum(dot(activated, down_full).astype(bf16))
    final_state = hidden_state + branch_scale * ffn_total
    deviation = final_state - to_local(teacher.reshape(rows, width)).astype(f32)
    local_square = jnp.sum(mask_values * jnp.mean(deviation * deviation, axis=-1))
    early = to_neighbours(
        jnp.concatenate([other_half(normed_one), attended, other_half(normed_two), activated], 1)
    )

    tokens_total = rows * lax.axis_size(("dp", "x", "z_hi", "y"))
    grad_final = deviation * mask_values[:, None] * (tokens_total / valid_count)
    branch_two = (branch_scale * grad_final).astype(bf16)
    grad_activated = dot_nt(branch_two, down_full).astype(bf16).astype(f32)
    grad_gate_pre = (
        grad_activated * up_pre * sigmoid_gate * (1.0 + gate_pre * (1.0 - sigmoid_gate))
    ).astype(bf16)
    grad_up_pre = (grad_activated * silu_gate).astype(bf16)
    late = to_neighbours(
        jnp.concatenate([other_half(branch_two), grad_gate_pre, grad_up_pre], axis=1)
    )
    part = dot_nt(grad_gate_pre, gate_full) + dot_nt(grad_up_pre, up_full)
    grad_normed_two = core_sum(part.astype(bf16))

    def both(own, received):
        return jnp.concatenate([own, received], axis=0)

    normed_two_all = both(normed_two[:, :half], early[:, 2 * half : 3 * half])
    activated_all = both(activated, early[:, 3 * half :])
    branch_two_all = both(branch_two[:, :half], late[:, :half])
    ff = grad_gate_pre.shape[1]
    ffn_grads = jnp.concatenate(
        [
            dot_tn(normed_two_all, both(grad_gate_pre, late[:, half : half + ff])).astype(bf16),
            dot_tn(normed_two_all, both(grad_up_pre, late[:, half + ff :])).astype(bf16),
            dot_tn(branch_two_all, activated_all).astype(bf16),
        ],
        axis=0,
    )
    ffn_share = lax.psum_scatter(ffn_grads, ("x", "y"), scatter_dimension=0, tiled=True)
    ffn_share = (ffn_share.astype(f32) + swap(ffn_share, "z_hi").astype(f32)).astype(bf16)
    ffn_total_grads = lax.all_gather(ffn_share, ("x", "y"), axis=0, tiled=True)

    grad_from_norm, grad_gain_two = norm_backward(
        hidden_state, inverse_two, gain_two, grad_normed_two
    )
    grad_hidden = grad_final + grad_from_norm
    branch_one = (branch_scale * grad_hidden).astype(bf16)
    grad_attended = jnp.concatenate(
        [dot_nt(branch_one, out_full[:384]), dot_nt(branch_one, out_full[384:])], axis=0
    ).astype(bf16)
    grad_mine = lax.all_to_all(grad_attended, "y", 0, 0, tiled=True)
    grad_queries, grad_window = attention_backward(queries, window, masks, logs, grad_mine)
    older = group_move(jnp.concatenate(grad_window[:4], axis=0).astype(bf16), -2)
    newer = group_move(jnp.concatenate(grad_window[4:8], axis=0).astype(bf16), -1)
    grad_key_values = (
        jnp.concatenate(grad_window[8:], axis=0) + newer.astype(f32) + older.astype(f32)
    ).astype(bf16)
    grad_projected = lax.all_to_all(
        jnp.concatenate([grad_queries, grad_key_values], axis=1), "y", 0, 0, tiled=True
    )
    grad_projected = jnp.concatenate([grad_projected[:rows], grad_projected[rows:]], axis=1)
    last = to_neighbours(jnp.concatenate([other_half(branch_one), grad_projected], axis=1))
    grad_normed_one = core_sum(dot_nt(grad_projected, attn_full).astype(bf16))
    gradient_via_first_norm, grad_gain_one = norm_backward(
        residual_in, inverse_one, gain_one, grad_normed_one
    )
    grad_tokens = from_local(grad_hidden + gradient_via_first_norm)

    normed_one_all = both(normed_one[:, :half], early[:, :half])
    attended_all = both(attended, early[:, half : 2 * half])
    branch_one_all = both(branch_one[:, :half], last[:, :half])
    projected_all = both(grad_projected, last[:, half:])
    attn_grads = dot_tn(normed_one_all, projected_all).astype(bf16)
    out_grads = dot_tn(attended_all, branch_one_all).astype(bf16)
    attn_out = jnp.concatenate([attn_grads, out_grads], axis=1)
    channels = reduce_channels([attn_out[:, c * 512 : (c + 1) * 512] for c in range(4)])
    reduced = jnp.concatenate(channels, axis=1).astype(f32)

    gain_grads = jnp.stack([grad_gain_one, grad_gain_two])
    gain_grads = gain_grads[:, :half] + swap(other_half(gain_grads), "dp")
    square = jnp.full((1, half), local_square, f32)
    square = square + swap(square, "dp")
    small = total_sum(jnp.concatenate([gain_grads, square], axis=0))
    loss_value = small[2, 0] / valid_count

    layer_out = from_local(final_state.astype(bf16)).reshape(seq_count, row_count, width)
    shard = w_gate.shape[0]
    return (
        layer_out,
        loss_value,
        grad_tokens.reshape(seq_count, row_count, width),
        jnp.concatenate([reduced[:, :384], reduced[:, 640:1024]], axis=1),
        jnp.concatenate([reduced[:, 384:512], reduced[:, 1024:1152]], axis=1),
        jnp.concatenate([reduced[:, 512:640], reduced[:, 1152:1280]], axis=1),
        reduced[:, 1280:],
        ffn_total_grads[:shard].astype(f32),
        ffn_total_grads[shard : 2 * shard].astype(f32),
        ffn_total_grads[2 * shard :].T.astype(f32),
        small[0],
        small[1],
    )


def solution(mesh):
    fine = Mesh(mesh.devices.reshape(2, 4, 2, 4, 2), ("dp", "x", "z_hi", "y", "tensor"))
    ctx = ("x", "z_hi", "y")
    return jax.shard_map(
        local,
        mesh=fine,
        in_specs=(
            P("dp", ctx, None),
            P("dp", "tensor"),
            P("dp", "tensor"),
            P("dp", "tensor"),
            P("tensor", "dp"),
            P("dp", "tensor"),
            P("dp", "tensor"),
            P("tensor", "dp"),
            P("dp"),
            P("dp"),
            P("dp", None),
            P("dp", ctx),
            P("dp", ctx, None),
        ),
        out_specs=(
            P("dp", ctx, None),
            P(),
            P("dp", ctx, None),
            P("dp", "tensor"),
            P("dp", "tensor"),
            P("dp", "tensor"),
            P("tensor", "dp"),
            P("dp", "tensor"),
            P("dp", "tensor"),
            P("tensor", "dp"),
            P("dp"),
            P("dp"),
        ),
        check_vma=False,
    )
```

```python
import math

import jax
import jax.numpy as jnp
from jax import lax
from jax.experimental import pallas as pl
from jax.experimental.pallas import tpu as pltpu
from jax.sharding import Mesh
from jax.sharding import PartitionSpec as P

HEAD = 64
WINDOW = 1024
BLOCK = 128
GROUP = 3
SPAN = WINDOW + BLOCK

branch_scale = 1.4 / math.sqrt(52.0)
norm_epsilon = 1e-05
masked_score = -1e30
scale_factor = 1.0 / math.sqrt(HEAD)
bf16 = jnp.bfloat16
f32 = jnp.float32


def dot(left, right):
    return jnp.dot(left, right, preferred_element_type=f32)


def dot_nt(left, right):
    return lax.dot_general(left, right, (((1,), (1,)), ((), ())), preferred_element_type=f32)


def dot_tn(left, right):
    return lax.dot_general(left, right, (((0,), (0,)), ((), ())), preferred_element_type=f32)


def z_move(value, distance):
    route = []
    for dp in range(2):
        for hi in range(2):
            z = (hi * 2 + dp + distance) % 4
            route.append((dp * 2 + hi, (z % 2) * 2 + z // 2))
    return lax.ppermute(value, ("dp", "z_hi"), route)


def ring_move(value, axis, distance):
    size = lax.axis_size(axis)
    return lax.ppermute(value, axis, [(i, (i + distance) % size) for i in range(size)])


def group_move(value, distance):
    return lax.ppermute(
        value, ("x", "z_hi"), [(i, i + distance) for i in range(8) if 0 <= i + distance < 8]
    )


def swap(value, axis):
    return lax.ppermute(value, axis, [(0, 1), (1, 0)])


PAIRS = {"even": ((0, 1), (1, 0), (2, 3), (3, 2)), "odd": ((0, 3), (3, 0), (1, 2), (2, 1))}


def pair_move(value, step):
    return lax.ppermute(value, step[0], PAIRS[step[1]])


def pair_bit(step):
    index = lax.axis_index(step[0])
    return (index // 2 + index) % 2 if step[1] == "even" else index // 2


def core_sum(part):
    return part.astype(f32) + swap(part, "tensor").astype(f32)


def nothing(value):
    return (value[0, 0] != value[0, 0]).astype(jnp.int32)


def held_by(value, *others):
    return jnp.where(sum(nothing(other) for other in others) == 0, value, 0)


def paired_heads(blocks):
    return [blocks[g * GROUP + j] for j in range(GROUP) for g in range(2)]


def plain_heads(blocks):
    return [blocks[j * 2 + g] for g in range(2) for j in range(GROUP)]


def column_heads(value, first):
    return [value[:, first + h * HEAD : first + (h + 1) * HEAD] for h in range(6)]


def row_heads(value, first):
    return [value[first + h * HEAD : first + (h + 1) * HEAD] for h in range(6)]


ORDERS = (
    (("x", "even"), ("x", "odd"), ("y", "even"), ("y", "odd")),
    (("x", "odd"), ("x", "even"), ("y", "odd"), ("y", "even")),
    (("y", "even"), ("y", "odd"), ("x", "even"), ("x", "odd")),
    (("y", "odd"), ("y", "even"), ("x", "odd"), ("x", "even")),
)


def halve(value, step):
    bit = pair_bit(step)
    half = value.shape[0] // 2
    keep = lax.dynamic_slice_in_dim(value, bit * half, half, 0)
    send = lax.dynamic_slice_in_dim(value, (1 - bit) * half, half, 0)
    return (keep.astype(f32) + pair_move(send, step).astype(f32)).astype(bf16)


def double(value, step):
    other = pair_move(value, step)
    return jnp.where(
        pair_bit(step) == 0,
        jnp.concatenate([value, other], axis=0),
        jnp.concatenate([other, value], axis=0),
    )


def reduce_first(channels):
    channels = list(channels)
    for level in range(2):
        channels = [halve(c, ORDERS[i][level]) for i, c in enumerate(channels)]
    return channels


def z_sum(value):
    return (value.astype(f32) + swap(value, "z_hi").astype(f32)).astype(bf16)


def reduce_rest(channels):
    for level in (2, 3):
        channels = [halve(c, ORDERS[i][level]) for i, c in enumerate(channels)]
    channels = [z_sum(c) for c in channels]
    for level in (3, 2, 1, 0):
        channels = [double(c, ORDERS[i][level]) for i, c in enumerate(channels)]
    return channels


def inverse_rms(source):
    return lax.rsqrt(jnp.mean(source * source, axis=-1, keepdims=True) + norm_epsilon)


def norm_backward(source, inverse, gain_vec, grad_normed):
    weighted = grad_normed * gain_vec
    grad_source = inverse * weighted - source * (inverse * inverse * inverse) * jnp.mean(
        source * weighted, axis=-1, keepdims=True
    )
    return (grad_source, grad_normed * source * inverse)


def allowed_keys(scalars, r):
    shape = (BLOCK, SPAN)
    query_pos = scalars[0] + r * BLOCK + lax.broadcasted_iota(jnp.int32, shape, 0)
    key_pos = scalars[0] + r * BLOCK - WINDOW + lax.broadcasted_iota(jnp.int32, shape, 1)
    lowest = jnp.maximum(query_pos - (WINDOW - 1), 0)
    for d in range(1, 5):
        lowest = jnp.maximum(lowest, jnp.where(query_pos >= scalars[d], scalars[d], 0))
    allowed = (key_pos >= lowest) & (key_pos <= query_pos)
    return jnp.concatenate([allowed] * GROUP, axis=0)


def head_rows(ref, lanes):
    return jnp.concatenate(
        [jnp.where(lanes, ref[:, j * 128 : (j + 1) * 128], 0) for j in range(GROUP)], axis=0
    )


def fill_window(window, older, newer, own):
    window[0:512] = older[...]
    window[512:1024] = newer[...]
    window[1024:1536] = own[...]


def attention_forward_kernel(scalars, q_ref, older, newer, own, *rest):
    out_ref, log_ref, window = rest[-3:]
    r = pl.program_id(0)

    @pl.when(r == 0)
    def _():
        fill_window(window, older, newer, own)

    span = pl.ds(pl.multiple_of(r * BLOCK, BLOCK), SPAN)
    keys = window[span, 0:128]
    values = window[span, 128:256]
    allowed = allowed_keys(scalars, r)
    low_lanes = lax.broadcasted_iota(jnp.int32, (BLOCK, 128), 1) < HEAD
    outs = []
    for g in range(2):
        q3 = head_rows(q_ref, low_lanes if g == 0 else jnp.logical_not(low_lanes))
        scores = jnp.where(allowed, dot_nt(q3, keys) * scale_factor, masked_score)
        top = jnp.max(scores, axis=-1, keepdims=True)
        weights = jnp.exp(scores - top)
        total = jnp.sum(weights, axis=-1, keepdims=True)
        log_ref[g] = top + jnp.log(total)
        outs.append(dot((weights * (1.0 / total)).astype(bf16), values))
    for j in range(GROUP):
        rows = slice(j * BLOCK, (j + 1) * BLOCK)
        out_ref[:, j * 128 : (j + 1) * 128] = jnp.where(
            low_lanes, outs[0][rows], outs[1][rows]
        ).astype(bf16)


def attention_backward_kernel(scalars, q_ref, g_ref, log_ref, older, newer, own, *rest):
    dq_ref, older_ref, newer_ref, own_ref, window, sums = rest[-6:]
    r = pl.program_id(0)

    @pl.when(r == 0)
    def _():
        fill_window(window, older, newer, own)
        sums[...] = jnp.zeros_like(sums)

    span = pl.ds(pl.multiple_of(r * BLOCK, BLOCK), SPAN)
    keys = window[span, 0:128]
    values = window[span, 128:256]
    allowed = allowed_keys(scalars, r)
    low_lanes = lax.broadcasted_iota(jnp.int32, (BLOCK, 128), 1) < HEAD
    outs = []
    for g in range(2):
        lanes = low_lanes if g == 0 else jnp.logical_not(low_lanes)
        q3 = head_rows(q_ref, lanes)
        g3 = head_rows(g_ref, lanes)
        scores = jnp.where(allowed, dot_nt(q3, keys) * scale_factor, masked_score)
        probs = jnp.exp(scores - log_ref[g])
        grad_probs = dot_nt(g3, values)
        inner = jnp.sum(grad_probs * probs, axis=-1, keepdims=True)
        grad_scores = (probs * (grad_probs - inner)).astype(bf16)
        outs.append(dot(grad_scores, keys))
        sums[span, 0:128] += dot_tn(grad_scores, q3)
        sums[span, 128:256] += dot_tn(probs.astype(bf16), g3)
    for j in range(GROUP):
        rows = slice(j * BLOCK, (j + 1) * BLOCK)
        dq_ref[:, j * 128 : (j + 1) * 128] = (
            jnp.where(low_lanes, outs[0][rows], outs[1][rows]) * scale_factor
        ).astype(bf16)

    @pl.when(r == 3)
    def _():
        for part, ref in enumerate((older_ref, newer_ref, own_ref)):
            rows = slice(part * 512, (part + 1) * 512)
            ref[:, 0:128] = (sums[rows, 0:128] * scale_factor).astype(ref.dtype)
            ref[:, 128:256] = sums[rows, 128:256].astype(ref.dtype)


SMEM = pl.BlockSpec(memory_space=pltpu.SMEM)
UNREAD = pl.BlockSpec(memory_space=pl.ANY)


def whole(*shape):
    return pl.BlockSpec(shape, lambda i: (0,) * len(shape))


def params():
    return pltpu.CompilerParams(vmem_limit_bytes=40 * 1024 * 1024)


def attention_forward(scalars, queries, pieces, held):
    return pl.pallas_call(
        attention_forward_kernel,
        grid=(4,),
        in_specs=[SMEM, pl.BlockSpec((BLOCK, 384), lambda i: (i, 0))]
        + [whole(512, 256)] * 3
        + [UNREAD] * len(held),
        out_specs=(
            pl.BlockSpec((BLOCK, 384), lambda i: (i, 0)),
            pl.BlockSpec((2, GROUP * BLOCK, 1), lambda i: (i, 0, 0)),
        ),
        out_shape=(
            jax.ShapeDtypeStruct((512, 384), bf16),
            jax.ShapeDtypeStruct((8, GROUP * BLOCK, 1), f32),
        ),
        scratch_shapes=[pltpu.VMEM((1536, 256), bf16)],
        compiler_params=params(),
        cost_estimate=pl.CostEstimate(
            flops=2 * 2 * 3072 * SPAN * 128, bytes_accessed=3_000_000, transcendentals=3072 * SPAN
        ),
    )(scalars, queries, *pieces, *held)


def attention_backward(scalars, queries, grads, logs, pieces, held):
    return pl.pallas_call(
        attention_backward_kernel,
        grid=(4,),
        in_specs=[
            SMEM,
            pl.BlockSpec((BLOCK, 384), lambda i: (i, 0)),
            pl.BlockSpec((BLOCK, 384), lambda i: (i, 0)),
            pl.BlockSpec((2, GROUP * BLOCK, 1), lambda i: (i, 0, 0)),
        ]
        + [whole(512, 256)] * 3
        + [UNREAD] * len(held),
        out_specs=(
            pl.BlockSpec((BLOCK, 384), lambda i: (i, 0)),
            whole(512, 256),
            whole(512, 256),
            whole(512, 256),
        ),
        out_shape=(
            jax.ShapeDtypeStruct((512, 384), bf16),
            jax.ShapeDtypeStruct((512, 256), bf16),
            jax.ShapeDtypeStruct((512, 256), bf16),
            jax.ShapeDtypeStruct((512, 256), f32),
        ),
        scratch_shapes=[pltpu.VMEM((1536, 256), bf16), pltpu.VMEM((1536, 256), f32)],
        compiler_params=params(),
        cost_estimate=pl.CostEstimate(
            flops=5 * 2 * 3072 * SPAN * 128, bytes_accessed=5_000_000, transcendentals=3072 * SPAN
        ),
    )(scalars, queries, grads, logs, *pieces, *held)


ROWS_AT = (0, 768, 960, 1152, 1344, 1536)
COLUMNS_AT = (0, 768, 1152, 1536)
TILE = 384


def ffn_forward_kernel(n_ref, *refs):
    gate, up, down = refs[0:5], refs[5:10], refs[10:13]
    g_ref, u_ref, a_ref, out_ref, total = refs[13:]
    step = pl.program_id(0)

    def times(weight):
        result = None
        for k, ref in enumerate(weight):
            part = dot(n_ref[:, ROWS_AT[k] : ROWS_AT[k + 1]], ref[...])
            result = part if result is None else result + part
        return result

    gate_pre, up_pre = times(gate), times(up)
    g_ref[...] = gate_pre
    u_ref[...] = up_pre
    activated = (gate_pre * jax.nn.sigmoid(gate_pre) * up_pre).astype(bf16)
    a_ref[...] = activated

    @pl.when(step == 0)
    def _():
        total[...] = jnp.zeros_like(total)

    for k, ref in enumerate(down):
        total[:, COLUMNS_AT[k] : COLUMNS_AT[k + 1]] += dot(activated, ref[...])

    @pl.when(step == pl.num_programs(0) - 1)
    def _():
        out_ref[...] = total[...].astype(bf16)


def ffn_backward_kernel(b_ref, *refs):
    gate, up, down = refs[0:5], refs[5:10], refs[10:13]
    g_ref, u_ref = refs[13:15]
    gg_ref, gu_ref, out_ref, total = refs[-4:]
    step = pl.program_id(0)
    grad = None
    for k, ref in enumerate(down):
        part = dot_nt(b_ref[:, COLUMNS_AT[k] : COLUMNS_AT[k + 1]], ref[...])
        grad = part if grad is None else grad + part
    grad = grad.astype(bf16).astype(f32)
    gate_pre, up_pre = g_ref[...], u_ref[...]
    sigmoid = jax.nn.sigmoid(gate_pre)
    grad_gate = (grad * up_pre * sigmoid * (1.0 + gate_pre * (1.0 - sigmoid))).astype(bf16)
    grad_up = (grad * gate_pre * sigmoid).astype(bf16)
    gg_ref[...] = grad_gate
    gu_ref[...] = grad_up

    @pl.when(step == 0)
    def _():
        total[...] = jnp.zeros_like(total)

    for k in range(5):
        total[:, ROWS_AT[k] : ROWS_AT[k + 1]] += dot_nt(grad_gate, gate[k][...]) + dot_nt(
            grad_up, up[k][...]
        )

    @pl.when(step == pl.num_programs(0) - 1)
    def _():
        out_ref[...] = total[...].astype(bf16)


def ffn_weight_specs():
    by_columns = [
        pl.BlockSpec((ROWS_AT[k + 1] - ROWS_AT[k], TILE), lambda i: (0, i)) for k in range(5)
    ]
    by_rows = [
        pl.BlockSpec((TILE, COLUMNS_AT[k + 1] - COLUMNS_AT[k]), lambda i: (i, 0)) for k in range(3)
    ]
    return by_columns + by_columns + by_rows


def hidden_tile(rows):
    return pl.BlockSpec((rows, TILE), lambda i: (0, i))


def ffn_forward(normed, gate, up, down):
    rows, width = normed.shape
    hidden = down[0].shape[0]
    return pl.pallas_call(
        ffn_forward_kernel,
        grid=(hidden // TILE,),
        in_specs=[whole(rows, width)] + ffn_weight_specs(),
        out_specs=(hidden_tile(rows), hidden_tile(rows), hidden_tile(rows), whole(rows, width)),
        out_shape=(
            jax.ShapeDtypeStruct((rows, hidden), f32),
            jax.ShapeDtypeStruct((rows, hidden), f32),
            jax.ShapeDtypeStruct((rows, hidden), bf16),
            jax.ShapeDtypeStruct((rows, width), bf16),
        ),
        scratch_shapes=[pltpu.VMEM((rows, width), f32)],
        compiler_params=params(),
        cost_estimate=pl.CostEstimate(
            flops=6 * rows * width * hidden,
            bytes_accessed=6 * width * hidden + 10 * rows * hidden,
            transcendentals=rows * hidden,
        ),
    )(normed, *gate, *up, *down)


def ffn_backward(branch, gate, up, down, gate_pre, up_pre):
    rows, width = branch.shape
    hidden = down[0].shape[0]
    return pl.pallas_call(
        ffn_backward_kernel,
        grid=(hidden // TILE,),
        in_specs=[whole(rows, width)] + ffn_weight_specs() + [hidden_tile(rows)] * 2,
        out_specs=(hidden_tile(rows), hidden_tile(rows), whole(rows, width)),
        out_shape=(
            jax.ShapeDtypeStruct((rows, hidden), bf16),
            jax.ShapeDtypeStruct((rows, hidden), bf16),
            jax.ShapeDtypeStruct((rows, width), bf16),
        ),
        scratch_shapes=[pltpu.VMEM((rows, width), f32)],
        compiler_params=params(),
        cost_estimate=pl.CostEstimate(
            flops=6 * rows * width * hidden,
            bytes_accessed=6 * width * hidden + 12 * rows * hidden,
            transcendentals=rows * hidden,
        ),
    )(branch, *gate, *up, *down, gate_pre, up_pre)


def local(
    tokens,
    w_query,
    key_projection_weight,
    value_projection_weight,
    w_out,
    w_gate,
    w_up,
    w_down,
    norm_attn,
    norm_ffn,
    doc_lengths,
    valid_mask,
    teacher,
):
    seq_count, row_count, width = tokens.shape
    rows = seq_count * row_count
    half = width // 2
    quarter = width // 4
    dp = lax.axis_index("dp")
    x_odd = lax.axis_index("x") % 2
    y_index = lax.axis_index("y")
    group_index = lax.axis_index("x") * 2 + lax.axis_index("z_hi")

    def to_local(value):
        own = jnp.where(dp == 0, value[..., :half], value[..., half:])
        other = jnp.where(dp == 0, value[..., half:], value[..., :half])
        first = jnp.where(x_odd == 0, other[..., :quarter], other[..., quarter:])
        second = jnp.where(x_odd == 0, other[..., quarter:], other[..., :quarter])
        return jnp.concatenate([own, first, second], axis=-1)

    def other_half(value):
        first, second = value[..., half : half + quarter], value[..., half + quarter :]
        return jnp.concatenate(
            [jnp.where(x_odd == 0, first, second), jnp.where(x_odd == 0, second, first)], axis=-1
        )

    def from_local(value):
        own, other = value[..., :half], other_half(value)
        return jnp.concatenate(
            [jnp.where(dp == 0, own, other), jnp.where(dp == 0, other, own)], axis=-1
        )

    def two_ways(first, second):
        return z_move(first, 1), z_move(second, -1)

    def fetch(piece):
        length = piece.shape[0] // 2
        one, two = two_ways(piece[:length], piece[length:])
        return one, two, ring_move(one, "x", 1), ring_move(two, "x", -1)

    def to_neighbours(value):
        one, two = two_ways(value[:row_count], value[row_count:])
        return jnp.concatenate([one, two], axis=0)

    w_attn = jnp.concatenate(
        [
            part
            for p in range(2)
            for part in (
                *paired_heads(column_heads(w_query, p * 384)),
                key_projection_weight[:, p * 128 : (p + 1) * 128],
                value_projection_weight[:, p * 128 : (p + 1) * 128],
            )
        ],
        axis=1,
    )
    w_attn_send = jnp.where(
        x_odd == 0, w_attn, jnp.concatenate([w_attn[quarter:], w_attn[:quarter]], axis=0)
    )
    attn_one, attn_two = two_ways(w_attn_send[:quarter], w_attn_send[quarter:])
    w_out_rows = jnp.concatenate(
        [part for p in range(2) for part in paired_heads(row_heads(w_out, p * 384))], axis=0
    )
    gains = jnp.stack([norm_attn, norm_ffn])
    gains_other = swap(gains, "dp")
    gains_first = jnp.where(x_odd == 0, gains_other[:, :quarter], gains_other[:, quarter:])
    gains_second = jnp.where(x_odd == 0, gains_other[:, quarter:], gains_other[:, :quarter])
    gains_full = jnp.concatenate([gains, gains_first, gains_second], axis=1).astype(f32)
    gain_one, gain_two = gains_full[0], gains_full[1]

    mask_values = valid_mask.reshape(rows).astype(f32)

    def column_piece(weight, hold):
        return lax.dynamic_slice_in_dim(weight, x_odd * quarter + hold, quarter, 1)

    def row_piece(weight, hold):
        return lax.dynamic_slice_in_dim(weight, x_odd * quarter + hold, quarter, 0)

    have_attn = nothing(attn_one) + nothing(attn_two)
    out_got = fetch(column_piece(w_out_rows, have_attn))
    gate_got = fetch(row_piece(w_gate, have_attn))
    up_got = fetch(row_piece(w_up, have_attn))
    down_got = fetch(column_piece(w_down, nothing(out_got[0])))
    out_pieces = (
        w_out_rows,
        jnp.concatenate(out_got[:2], axis=0),
        jnp.concatenate(out_got[2:], axis=0),
    )
    gate_pieces = (w_gate, *gate_got)
    up_pieces = (w_up, *up_got)

    residual_in = to_local(tokens.reshape(rows, width)).astype(f32)
    inverse_one = inverse_rms(residual_in)
    normed_one = (residual_in * inverse_one * gain_one).astype(bf16)
    projected = (
        dot(normed_one[:, :half], w_attn)
        + dot(normed_one[:, half : half + quarter], attn_one)
        + dot(normed_one[:, half + quarter :], attn_two)
    ).astype(bf16)
    projected = jnp.concatenate([projected[:, :640], projected[:, 640:]], axis=0)
    mine = lax.all_to_all(projected, "y", 0, 0, tiled=True)
    queries, key_values = mine[:, :384], mine[:, 384:]
    pieces = (group_move(key_values, 2), group_move(key_values, 1), key_values)
    bounds = jnp.cumsum(lax.dynamic_index_in_dim(doc_lengths, y_index % 2, 0, keepdims=False))
    scalars = jnp.concatenate([(group_index * 512)[None], bounds]).astype(jnp.int32)
    attended_mine, logs = attention_forward(
        scalars, queries, pieces, (*out_got, *gate_got, *up_got[:2])
    )
    returned = lax.all_to_all(attended_mine, "y", 0, 0, tiled=True)
    attended = jnp.concatenate([returned[:rows], returned[rows:]], axis=1)

    attn_total = core_sum(
        jnp.concatenate([dot(attended, piece).astype(bf16) for piece in out_pieces], axis=1)
    )
    hidden_state = residual_in + branch_scale * attn_total
    inverse_two = inverse_rms(hidden_state)
    normed_two = (hidden_state * inverse_two * gain_two).astype(bf16)
    down_pieces = (
        w_down,
        jnp.concatenate(down_got[:2], axis=0),
        jnp.concatenate(down_got[2:], axis=0),
    )
    gate_pre, up_pre, activated, ffn_part = ffn_forward(
        normed_two, gate_pieces, up_pieces, down_pieces
    )
    ffn_total = core_sum(ffn_part)
    final_state = hidden_state + branch_scale * ffn_total
    deviation = final_state - to_local(teacher.reshape(rows, width)).astype(f32)
    row_squares = mask_values * jnp.mean(deviation * deviation, axis=-1)
    early = to_neighbours(
        jnp.concatenate([other_half(normed_one), attended, other_half(normed_two), activated], 1)
    )

    grad_final = deviation * mask_values[:, None]
    branch_two = (branch_scale * grad_final).astype(bf16)
    grad_gate_pre, grad_up_pre, part = ffn_backward(
        branch_two, gate_pieces, up_pieces, down_pieces, gate_pre, up_pre
    )
    late = to_neighbours(
        jnp.concatenate([other_half(branch_two), grad_gate_pre, grad_up_pre], axis=1)
    )
    grad_normed_two = core_sum(part)

    def both(own, received):
        return jnp.concatenate([own, received], axis=0)

    normed_two_all = both(normed_two[:, :half], early[:, 2 * half : 3 * half])
    activated_all = both(activated, early[:, 3 * half :])
    branch_two_all = both(branch_two[:, :half], late[:, :half])
    ff = grad_gate_pre.shape[1]
    ffn_grads = jnp.concatenate(
        [
            dot_tn(normed_two_all, both(grad_gate_pre, late[:, half : half + ff])).astype(bf16),
            dot_tn(normed_two_all, both(grad_up_pre, late[:, half + ff :])).astype(bf16),
            dot_tn(branch_two_all, activated_all).astype(bf16),
        ],
        axis=0,
    )
    ffn_share = lax.psum_scatter(ffn_grads, ("x", "y"), scatter_dimension=0, tiled=True)

    grad_from_norm, gain_terms_two = norm_backward(
        hidden_state, inverse_two, gain_two, grad_normed_two
    )
    grad_hidden = grad_final + grad_from_norm
    branch_one = (branch_scale * grad_hidden).astype(bf16)
    grad_attended = sum(
        dot_nt(branch_one[:, COLUMNS_AT[k] : COLUMNS_AT[k + 1]], out_pieces[k]) for k in range(3)
    ).astype(bf16)
    grad_attended = jnp.concatenate([grad_attended[:, :384], grad_attended[:, 384:]], axis=0)
    grad_mine = lax.all_to_all(grad_attended, "y", 0, 0, tiled=True)
    grad_queries, grad_older, grad_newer, grad_own = attention_backward(
        scalars, queries, grad_mine, logs, pieces, (ffn_grads,)
    )
    older = group_move(grad_older, -2)
    newer = group_move(grad_newer, -1)
    grad_key_values = (grad_own + newer.astype(f32) + older.astype(f32)).astype(bf16)
    grad_projected = lax.all_to_all(
        jnp.concatenate([grad_queries, grad_key_values], axis=1), "y", 0, 0, tiled=True
    )
    grad_projected = jnp.concatenate([grad_projected[:rows], grad_projected[rows:]], axis=1)
    last = to_neighbours(jnp.concatenate([other_half(branch_one), grad_projected], axis=1))
    grad_normed_one = core_sum(
        jnp.concatenate(
            [
                dot_nt(grad_projected, piece).astype(bf16)
                for piece in (w_attn, attn_one, attn_two)
            ],
            axis=1,
        )
    )
    gradient_via_first_norm, gain_terms_one = norm_backward(
        residual_in, inverse_one, gain_one, grad_normed_one
    )
    grad_tokens = from_local(grad_hidden + gradient_via_first_norm)

    normed_one_all = both(normed_one[:, :half], early[:, :half])
    attended_all = both(attended, early[:, half : 2 * half])
    branch_one_all = both(branch_one[:, :half], last[:, :half])
    projected_all = both(grad_projected, last[:, half:])
    attn_grads = dot_tn(normed_one_all, projected_all).astype(bf16)
    out_grads = dot_tn(attended_all, branch_one_all).astype(bf16)
    ones = jnp.ones((rows, 128), f32)

    def column_sums(terms):
        return lax.dot_general(
            terms, ones, (((0,), (0,)), ((), ())), precision=lax.Precision.HIGHEST
        )

    def on_rows(values):
        return jnp.pad(jnp.broadcast_to(values[:, None], (rows, 128)), ((0, half - rows), (0, 0)))

    entries = [
        column_sums(gain_terms_one[:, :half]),
        column_sums(other_half(gain_terms_one)),
        column_sums(gain_terms_two[:, :half]),
        column_sums(other_half(gain_terms_two)),
        on_rows(mask_values),
        on_rows(row_squares),
    ]
    slot = lax.broadcasted_iota(jnp.int32, (half, 128), 1) // 16
    tile = jnp.zeros((half, 128), f32)
    for k, entry in enumerate(entries):
        tile = jnp.where(slot == k, entry, tile)
    attn_out = jnp.concatenate([out_grads, attn_grads, tile.astype(bf16)], axis=1)
    cuts = (0, 640, 1152, 1664, 2176)
    channels = reduce_first([attn_out[:, a:b] for a, b in zip(cuts[:-1], cuts[1:])])
    ffn_share = z_sum(held_by(ffn_share, *channels))
    ffn_total_grads = lax.all_gather(ffn_share, ("x", "y"), axis=0, tiled=True)
    reduced = jnp.concatenate(reduce_rest(channels), axis=1)
    small = jnp.transpose(reduced[:, 2048:])[::16].astype(f32)
    small_other = swap(small, "dp")
    valid_count = jnp.sum(small[4]) + jnp.sum(small_other[4])
    loss_value = (jnp.sum(small[5]) + jnp.sum(small_other[5])) / valid_count
    tokens_total = rows * lax.axis_size(("dp", "x", "z_hi", "y"))
    scale = tokens_total / valid_count

    def scaled(*parts):
        return jnp.concatenate(parts, axis=1).astype(f32) * scale

    layer_out = from_local(final_state.astype(bf16)).reshape(seq_count, row_count, width)
    shard = w_gate.shape[0]
    return (
        layer_out,
        loss_value,
        (grad_tokens * scale).reshape(seq_count, row_count, width),
        scaled(
            *plain_heads(column_heads(reduced, 768)), *plain_heads(column_heads(reduced, 1408))
        ),
        scaled(reduced[:, 1152:1280], reduced[:, 1792:1920]),
        scaled(reduced[:, 1280:1408], reduced[:, 1920:2048]),
        scaled(
            jnp.concatenate(
                [
                    part
                    for p in range(2)
                    for part in plain_heads(row_heads(reduced[:, :768], p * 384))
                ],
                axis=0,
            )
        ),
        scaled(ffn_total_grads[:shard]),
        scaled(ffn_total_grads[shard : 2 * shard]),
        scaled(ffn_total_grads[2 * shard :].T),
        (small[0] + small_other[1]) * scale,
        (small[2] + small_other[3]) * scale,
    )


def solution(mesh):
    fine = Mesh(mesh.devices.reshape(2, 4, 2, 4, 2), ("dp", "x", "z_hi", "y", "tensor"))
    ctx = ("x", "z_hi", "y")
    return jax.shard_map(
        local,
        mesh=fine,
        in_specs=(
            P("dp", ctx, None),
            P("dp", "tensor"),
            P("dp", "tensor"),
            P("dp", "tensor"),
            P("tensor", "dp"),
            P("dp", "tensor"),
            P("dp", "tensor"),
            P("tensor", "dp"),
            P("dp"),
            P("dp"),
            P("dp", None),
            P("dp", ctx),
            P("dp", ctx, None),
        ),
        out_specs=(
            P("dp", ctx, None),
            P(),
            P("dp", ctx, None),
            P("dp", "tensor"),
            P("dp", "tensor"),
            P("dp", "tensor"),
            P("tensor", "dp"),
            P("dp", "tensor"),
            P("dp", "tensor"),
            P("tensor", "dp"),
            P("dp"),
            P("dp"),
        ),
        check_vma=False,
    )
```

```python
import math

import jax
import jax.numpy as jnp
from jax import lax
from jax.experimental import pallas as pl
from jax.experimental.pallas import tpu as pltpu
from jax.sharding import Mesh
from jax.sharding import PartitionSpec as P

HEAD = 64
WINDOW = 1024
BLOCK = 128
GROUP = 3
SPAN = WINDOW + BLOCK

branch_scale = 1.4 / math.sqrt(52.0)
norm_epsilon = 1e-05
masked_score = -1e30
scale_factor = 1.0 / math.sqrt(HEAD)
bf16 = jnp.bfloat16
f32 = jnp.float32


def dot(left, right):
    return jnp.dot(left, right, preferred_element_type=f32)


def dot_nt(left, right):
    return lax.dot_general(left, right, (((1,), (1,)), ((), ())), preferred_element_type=f32)


def dot_tn(left, right):
    return lax.dot_general(left, right, (((0,), (0,)), ((), ())), preferred_element_type=f32)


def z_move(value, distance):
    route = []
    for dp in range(2):
        for hi in range(2):
            z = (hi * 2 + dp + distance) % 4
            route.append((dp * 2 + hi, (z % 2) * 2 + z // 2))
    return lax.ppermute(value, ("dp", "z_hi"), route)


def ring_move(value, axis, distance):
    size = lax.axis_size(axis)
    return lax.ppermute(value, axis, [(i, (i + distance) % size) for i in range(size)])


def group_move(value, distance):
    return lax.ppermute(
        value, ("x", "z_hi"), [(i, i + distance) for i in range(8) if 0 <= i + distance < 8]
    )


def swap(value, axis):
    return lax.ppermute(value, axis, [(0, 1), (1, 0)])


PAIRS = {"even": ((0, 1), (1, 0), (2, 3), (3, 2)), "odd": ((0, 3), (3, 0), (1, 2), (2, 1))}


def pair_move(value, step):
    return lax.ppermute(value, step[0], PAIRS[step[1]])


def pair_bit(step):
    index = lax.axis_index(step[0])
    return (index // 2 + index) % 2 if step[1] == "even" else index // 2


def core_sum(part):
    return part.astype(f32) + swap(part, "tensor").astype(f32)


def nothing(value):
    return (value[0, 0] != value[0, 0]).astype(jnp.int32)


def held_by(value, *others):
    return jnp.where(sum(nothing(other) for other in others) == 0, value, 0)


def z_sum(value):
    return (value.astype(f32) + swap(value, "z_hi").astype(f32)).astype(bf16)


def halves(value, step):
    bit = pair_bit(step)
    half = value.shape[0] // 2
    return (
        lax.dynamic_slice_in_dim(value, bit * half, half, 0),
        lax.dynamic_slice_in_dim(value, (1 - bit) * half, half, 0),
    )


def add_moved(keep, send, step):
    return (keep.astype(f32) + pair_move(send, step).astype(f32)).astype(bf16)


def halve(value, step):
    return add_moved(*halves(value, step), step)


def double(value, step):
    other = pair_move(value, step)
    return jnp.where(
        pair_bit(step) == 0,
        jnp.concatenate([value, other], axis=0),
        jnp.concatenate([other, value], axis=0),
    )


FIRST = (
    (("x", "even"), ("x", "odd")),
    (("x", "odd"), ("x", "even")),
    (("y", "even"), ("y", "odd")),
    (("y", "odd"), ("y", "even")),
)
SECOND = ((("y", "even"), ("y", "odd")), (("x", "even"), ("x", "odd")))


def reduce_rest(channels):
    channels = [halve(c, FIRST[i][1]) for i, c in enumerate(channels)]
    widths = [c.shape[1] for c in channels]
    pairs = [jnp.concatenate(channels[k : k + 2], axis=1) for k in (0, 2)]
    for level in (0, 1):
        pairs = [halve(c, SECOND[i][level]) for i, c in enumerate(pairs)]
    at = widths[0] + widths[1]
    total = z_sum(jnp.concatenate(pairs, axis=1))
    pairs = [total[:, :at], total[:, at:]]
    for level in (1, 0):
        pairs = [double(c, SECOND[i][level]) for i, c in enumerate(pairs)]
    channels = [
        pairs[0][:, : widths[0]],
        pairs[0][:, widths[0] :],
        pairs[1][:, : widths[2]],
        pairs[1][:, widths[2] :],
    ]
    for level in (1, 0):
        channels = [double(c, FIRST[i][level]) for i, c in enumerate(channels)]
    return channels


def inverse_rms(source):
    return lax.rsqrt(jnp.mean(source * source, axis=-1, keepdims=True) + norm_epsilon)


def norm_backward(source, inverse, gain_vec, grad_normed):
    weighted = grad_normed * gain_vec
    grad_source = inverse * weighted - source * (inverse * inverse * inverse) * jnp.mean(
        source * weighted, axis=-1, keepdims=True
    )
    return (grad_source, grad_normed * source * inverse)


def allowed_keys(scalars, r):
    shape = (BLOCK, SPAN)
    query_pos = scalars[0] + r * BLOCK + lax.broadcasted_iota(jnp.int32, shape, 0)
    key_pos = scalars[0] + r * BLOCK - WINDOW + lax.broadcasted_iota(jnp.int32, shape, 1)
    lowest = jnp.maximum(query_pos - (WINDOW - 1), 0)
    for d in range(1, 5):
        lowest = jnp.maximum(lowest, jnp.where(query_pos >= scalars[d], scalars[d], 0))
    allowed = (key_pos >= lowest) & (key_pos <= query_pos)
    return jnp.concatenate([allowed] * GROUP, axis=0)


def low_half():
    return lax.broadcasted_iota(jnp.int32, (BLOCK, 128), 1) < HEAD


def head_rows(ref, g):
    lanes = low_half() if g == 0 else jnp.logical_not(low_half())
    parts = []
    for h in range(g * GROUP, (g + 1) * GROUP):
        columns = ref[:, h // 2 * 128 : h // 2 * 128 + 128].astype(f32)
        if h % 2 != g:
            columns = pltpu.roll(columns, HEAD, 1)
        parts.append(jnp.where(lanes, columns, 0.0).astype(bf16))
    return jnp.concatenate(parts, axis=0)


def put_heads(ref, results):
    sides = {}
    for g in range(2):
        for j in range(GROUP):
            h = g * GROUP + j
            columns = results[g][j * BLOCK : (j + 1) * BLOCK]
            sides[h] = pltpu.roll(columns, HEAD, 1) if h % 2 != g else columns
    for t in range(GROUP):
        ref[:, t * 128 : (t + 1) * 128] = jnp.where(
            low_half(), sides[2 * t], sides[2 * t + 1]
        ).astype(ref.dtype)


def fill_window(window, older, newer, own):
    window[0:512] = older[...]
    window[512:1024] = newer[...]
    window[1024:1536] = own[...]


def attention_forward_kernel(scalars, q_ref, older, newer, own, *rest):
    out_ref, log_ref, window = rest[-3:]
    r = pl.program_id(0)

    @pl.when(r == 0)
    def _():
        fill_window(window, older, newer, own)

    span = pl.ds(pl.multiple_of(r * BLOCK, BLOCK), SPAN)
    keys = window[span, 0:128]
    values = window[span, 128:256]
    allowed = allowed_keys(scalars, r)
    outs = []
    for g in range(2):
        q3 = head_rows(q_ref, g)
        scores = jnp.where(allowed, dot_nt(q3, keys) * scale_factor, masked_score)
        top = jnp.max(scores, axis=-1, keepdims=True)
        weights = jnp.exp(scores - top)
        total = jnp.sum(weights, axis=-1, keepdims=True)
        log_ref[g] = top + jnp.log(total)
        outs.append(dot((weights * (1.0 / total)).astype(bf16), values))
    put_heads(out_ref, outs)


def attention_backward_kernel(scalars, q_ref, g_ref, log_ref, older, newer, own, *rest):
    dq_ref, older_ref, newer_ref, own_ref, window, sums = rest[-6:]
    r = pl.program_id(0)

    @pl.when(r == 0)
    def _():
        fill_window(window, older, newer, own)
        sums[...] = jnp.zeros_like(sums)

    span = pl.ds(pl.multiple_of(r * BLOCK, BLOCK), SPAN)
    keys = window[span, 0:128]
    values = window[span, 128:256]
    allowed = allowed_keys(scalars, r)
    outs = []
    for g in range(2):
        q3 = head_rows(q_ref, g)
        g3 = head_rows(g_ref, g)
        scores = jnp.where(allowed, dot_nt(q3, keys) * scale_factor, masked_score)
        probs = jnp.exp(scores - log_ref[g])
        grad_probs = dot_nt(g3, values)
        inner = jnp.sum(grad_probs * probs, axis=-1, keepdims=True)
        grad_scores = (probs * (grad_probs - inner)).astype(bf16)
        outs.append(dot(grad_scores, keys) * scale_factor)
        sums[span, 0:128] += dot_tn(grad_scores, q3)
        sums[span, 128:256] += dot_tn(probs.astype(bf16), g3)
    put_heads(dq_ref, outs)

    @pl.when(r == 3)
    def _():
        for part, ref in enumerate((older_ref, newer_ref, own_ref)):
            rows = slice(part * 512, (part + 1) * 512)
            ref[:, 0:128] = (sums[rows, 0:128] * scale_factor).astype(ref.dtype)
            ref[:, 128:256] = sums[rows, 128:256].astype(ref.dtype)


SMEM = pl.BlockSpec(memory_space=pltpu.SMEM)
UNREAD = pl.BlockSpec(memory_space=pl.ANY)
SHORT = pl.CostEstimate(flops=1000, bytes_accessed=1000, transcendentals=0)


def whole(*shape):
    return pl.BlockSpec(shape, lambda i: (0,) * len(shape))


def params():
    return pltpu.CompilerParams(vmem_limit_bytes=40 * 1024 * 1024)


def copy_blocks(index, outputs, shapes, held):
    blocks = [block for output in outputs for block in output]

    def kernel(index_ref, *refs):
        outs = refs[len(blocks) + len(held) :]
        at = 0
        for output, out in zip(outputs, outs):
            for _, shape, _, row, column in output:
                out[row : row + shape[0], column : column + shape[1]] = refs[at][...]
                at += 1

    return pl.pallas_call(
        kernel,
        grid_spec=pltpu.PrefetchScalarGridSpec(
            num_scalar_prefetch=1,
            grid=(1,),
            in_specs=[
                pl.BlockSpec(block[1], lambda i, ref, place=block[2]: place(ref[0]))
                for block in blocks
            ]
            + [UNREAD] * len(held),
            out_specs=[pl.BlockSpec(shape, lambda i, ref: (0, 0)) for shape in shapes],
        ),
        out_shape=[jax.ShapeDtypeStruct(shape, bf16) for shape in shapes],
        compiler_params=params(),
        cost_estimate=SHORT,
    )(index.reshape(1), *[block[0] for block in blocks], *held)


def hold(values, *held):
    return copy_blocks(
        jnp.zeros((), jnp.int32),
        [[(v, v.shape, lambda c: (0, 0), 0, 0)] for v in values],
        [v.shape for v in values],
        held,
    )


def attention_forward(scalars, queries, pieces, held):
    return pl.pallas_call(
        attention_forward_kernel,
        grid=(4,),
        in_specs=[SMEM, pl.BlockSpec((BLOCK, 384), lambda i: (i, 0))]
        + [whole(512, 256)] * 3
        + [UNREAD] * len(held),
        out_specs=(
            pl.BlockSpec((BLOCK, 384), lambda i: (i, 0)),
            pl.BlockSpec((2, GROUP * BLOCK, 1), lambda i: (i, 0, 0)),
        ),
        out_shape=(
            jax.ShapeDtypeStruct((512, 384), bf16),
            jax.ShapeDtypeStruct((8, GROUP * BLOCK, 1), f32),
        ),
        scratch_shapes=[pltpu.VMEM((1536, 256), bf16)],
        compiler_params=params(),
        cost_estimate=SHORT,
    )(scalars, queries, *pieces, *held)


def attention_backward(scalars, queries, grads, logs, pieces, held):
    return pl.pallas_call(
        attention_backward_kernel,
        grid=(4,),
        in_specs=[
            SMEM,
            pl.BlockSpec((BLOCK, 384), lambda i: (i, 0)),
            pl.BlockSpec((BLOCK, 384), lambda i: (i, 0)),
            pl.BlockSpec((2, GROUP * BLOCK, 1), lambda i: (i, 0, 0)),
        ]
        + [whole(512, 256)] * 3
        + [UNREAD] * len(held),
        out_specs=(
            pl.BlockSpec((BLOCK, 384), lambda i: (i, 0)),
            whole(512, 256),
            whole(512, 256),
            whole(512, 256),
        ),
        out_shape=(
            jax.ShapeDtypeStruct((512, 384), bf16),
            jax.ShapeDtypeStruct((512, 256), bf16),
            jax.ShapeDtypeStruct((512, 256), bf16),
            jax.ShapeDtypeStruct((512, 256), f32),
        ),
        scratch_shapes=[pltpu.VMEM((1536, 256), bf16), pltpu.VMEM((1536, 256), f32)],
        compiler_params=params(),
        cost_estimate=SHORT,
    )(scalars, queries, grads, logs, *pieces, *held)


ROWS_AT = (0, 768, 960, 1152, 1344, 1536)
COLUMNS_AT = (0, 768, 1152, 1536)
TILE = 384


def ffn_weights(refs, step):
    one, two = refs[11:13]
    three, four, five, six = refs[13:17]
    tail = jnp.where(step < 3, four[...], jnp.where(step < 4, five[...], six[...]))
    down = (
        refs[10][...],
        jnp.where(step < 3, one[...], two[...]),
        jnp.where(step < 2, three[...], tail),
    )
    return refs[0:5], refs[5:10], down


def ffn_forward_kernel(n_ref, *refs):
    g_ref, u_ref, a_ref, out_ref, total = refs[-5:]
    step = pl.program_id(0)
    gate, up, down = ffn_weights(refs, step)

    def times(weight):
        result = None
        for k, ref in enumerate(weight):
            part = dot(n_ref[:, ROWS_AT[k] : ROWS_AT[k + 1]], ref[...])
            result = part if result is None else result + part
        return result

    gate_pre, up_pre = times(gate), times(up)
    g_ref[...] = gate_pre
    u_ref[...] = up_pre
    activated = (gate_pre * jax.nn.sigmoid(gate_pre) * up_pre).astype(bf16)
    a_ref[...] = activated

    @pl.when(step == 0)
    def _():
        total[...] = jnp.zeros_like(total)

    for k, weight in enumerate(down):
        total[:, COLUMNS_AT[k] : COLUMNS_AT[k + 1]] += dot(activated, weight)

    @pl.when(step == pl.num_programs(0) - 1)
    def _():
        out_ref[...] = total[...].astype(bf16)


def ffn_backward_kernel(b_ref, *refs):
    g_ref, u_ref = refs[17:19]
    gg_ref, gu_ref, out_ref, total = refs[-4:]
    step = pl.program_id(0)
    gate, up, down = ffn_weights(refs, step)
    grad = None
    for k, weight in enumerate(down):
        part = dot_nt(b_ref[:, COLUMNS_AT[k] : COLUMNS_AT[k + 1]], weight)
        grad = part if grad is None else grad + part
    grad = grad.astype(bf16).astype(f32)
    gate_pre, up_pre = g_ref[...], u_ref[...]
    sigmoid = jax.nn.sigmoid(gate_pre)
    grad_gate = (grad * up_pre * sigmoid * (1.0 + gate_pre * (1.0 - sigmoid))).astype(bf16)
    grad_up = (grad * gate_pre * sigmoid).astype(bf16)
    gg_ref[...] = grad_gate
    gu_ref[...] = grad_up

    @pl.when(step == 0)
    def _():
        total[...] = jnp.zeros_like(total)

    for k in range(5):
        total[:, ROWS_AT[k] : ROWS_AT[k + 1]] += dot_nt(grad_gate, gate[k][...]) + dot_nt(
            grad_up, up[k][...]
        )

    @pl.when(step == pl.num_programs(0) - 1)
    def _():
        out_ref[...] = total[...].astype(bf16)


def ffn_weight_specs():
    own = pl.BlockSpec((768, TILE), lambda i: (0, i))
    alone = pl.BlockSpec((192, TILE), lambda i: (0, i))
    beside = pl.BlockSpec((192, TILE), lambda i: (0, i + 5))
    early = pl.BlockSpec((TILE, 384), lambda i: (jnp.minimum(i, 2), 0))
    late = pl.BlockSpec((TILE, 384), lambda i: (jnp.maximum(i - 3, 0), 0))
    first = pl.BlockSpec((TILE, 384), lambda i: (jnp.minimum(i, 1), 0))
    single = pl.BlockSpec((TILE, 384), lambda i: (0, 0))
    down = [pl.BlockSpec((TILE, 768), lambda i: (i, 0)), early, late, first] + [single] * 3
    return [own] + [alone] * 4 + [own, beside, beside, alone, alone] + down


def hidden_tile(rows):
    return pl.BlockSpec((rows, TILE), lambda i: (0, i))


def ffn_forward(normed, weights):
    rows, width = normed.shape
    hidden = weights[10].shape[0]
    return pl.pallas_call(
        ffn_forward_kernel,
        grid=(hidden // TILE,),
        in_specs=[whole(rows, width)] + ffn_weight_specs(),
        out_specs=(hidden_tile(rows), hidden_tile(rows), hidden_tile(rows), whole(rows, width)),
        out_shape=(
            jax.ShapeDtypeStruct((rows, hidden), f32),
            jax.ShapeDtypeStruct((rows, hidden), f32),
            jax.ShapeDtypeStruct((rows, hidden), bf16),
            jax.ShapeDtypeStruct((rows, width), bf16),
        ),
        scratch_shapes=[pltpu.VMEM((rows, width), f32)],
        compiler_params=params(),
        cost_estimate=SHORT,
    )(normed, *weights)


def ffn_backward(branch, weights, gate_pre, up_pre, held):
    rows, width = branch.shape
    hidden = weights[10].shape[0]
    return pl.pallas_call(
        ffn_backward_kernel,
        grid=(hidden // TILE,),
        in_specs=[whole(rows, width)] + ffn_weight_specs()
        + [hidden_tile(rows)] * 2
        + [UNREAD] * len(held),
        out_specs=(hidden_tile(rows), hidden_tile(rows), whole(rows, width)),
        out_shape=(
            jax.ShapeDtypeStruct((rows, hidden), bf16),
            jax.ShapeDtypeStruct((rows, hidden), bf16),
            jax.ShapeDtypeStruct((rows, width), bf16),
        ),
        scratch_shapes=[pltpu.VMEM((rows, width), f32)],
        compiler_params=params(),
        cost_estimate=SHORT,
    )(branch, *weights, gate_pre, up_pre, *held)


def projection_kernel(n_own, n_other, wq, wk, wv, one, two, out_ref):
    own = n_own[...]
    first, second = n_other[:, :384], n_other[:, 384:]
    rows = own.shape[0]
    for p in range(2):
        place = pl.ds(p * rows, rows)
        q_at, kv_at = slice(p * 384, p * 384 + 384), slice(p * 128, p * 128 + 128)
        for weight, own_at, at, out_at in (
            (wq, q_at, p * 384, slice(0, 384)),
            (wk, kv_at, 768 + p * 128, slice(384, 512)),
            (wv, kv_at, 1024 + p * 128, slice(512, 640)),
        ):
            there = slice(at, at + out_at.stop - out_at.start)
            out_ref[place, out_at] = (
                dot(own, weight[:, own_at])
                + dot(first, one[:, there])
                + dot(second, two[:, there])
            ).astype(bf16)


def projection_backward_kernel(colour, g_ref, wq, wk, wv, one, two, held, out_ref):
    grad = jnp.concatenate(
        [
            g_ref[:, a:b]
            for a, b in ((0, 384), (640, 1024), (384, 512), (1024, 1152), (512, 640), (1152, 1280))
        ],
        axis=1,
    )
    out_ref[:, 0:768] = (
        dot_nt(grad[:, 0:768], wq[...])
        + dot_nt(grad[:, 768:1024], wk[...])
        + dot_nt(grad[:, 1024:1280], wv[...])
    ).astype(bf16)
    first = dot_nt(grad, one[...]).astype(bf16)
    second = dot_nt(grad, two[...]).astype(bf16)

    @pl.when(colour[0] == 0)
    def _():
        out_ref[:, 768:1152] = first
        out_ref[:, 1152:1536] = second

    @pl.when(colour[0] != 0)
    def _():
        out_ref[:, 768:1152] = second
        out_ref[:, 1152:1536] = first


def projection_backward(colour, *operands):
    rows = operands[0].shape[0]
    return pl.pallas_call(
        projection_backward_kernel,
        grid=(1,),
        in_specs=[SMEM] + [whole(*operand.shape) for operand in operands[:-1]] + [UNREAD],
        out_specs=whole(rows, 1536),
        out_shape=jax.ShapeDtypeStruct((rows, 1536), bf16),
        compiler_params=params(),
        cost_estimate=SHORT,
    )(colour.reshape(1), *operands)


def out_blocks(pieces):
    z_one, z_two, x_one, x_two, y_one, y_two = pieces
    operands = [z_one, z_one, z_two, z_two, x_one, y_one, x_two, y_two]
    columns = [10, 11, 10, 11, 5, 5, 5, 5]
    return operands, [pl.BlockSpec((192, 384), lambda i, k=k: (0, k)) for k in columns]


def out_columns(refs):
    return jnp.concatenate([ref[...] for ref in refs], axis=0)


def out_projection_kernel(back_ref, w_ref, *refs):
    part_ref, attended_ref = refs[-2:]
    rows = attended_ref.shape[0]
    attended = jnp.concatenate([back_ref[0:rows], back_ref[rows : 2 * rows]], axis=1)
    attended_ref[...] = attended
    part_ref[:, 0:768] = dot(attended, w_ref[...]).astype(bf16)
    part_ref[:, 768:1152] = dot(attended, out_columns(refs[0:4])).astype(bf16)
    part_ref[:, 1152:1536] = dot(attended, out_columns(refs[4:8])).astype(bf16)


def out_projection(back, w_out, pieces, held):
    rows = back.shape[0] // 2
    operands, specs = out_blocks(pieces)
    return pl.pallas_call(
        out_projection_kernel,
        grid=(1,),
        in_specs=[whole(*back.shape), whole(*w_out.shape)] + specs + [UNREAD] * len(held),
        out_specs=(whole(rows, 1536), whole(rows, 768)),
        out_shape=(
            jax.ShapeDtypeStruct((rows, 1536), bf16),
            jax.ShapeDtypeStruct((rows, 768), bf16),
        ),
        compiler_params=params(),
        cost_estimate=SHORT,
    )(back, w_out, *operands, *held)


def out_backward_kernel(b_ref, w_ref, *refs):
    out_ref = refs[-1]
    rows = b_ref.shape[0]
    grad = (
        dot_nt(b_ref[:, 0:768], w_ref[...])
        + dot_nt(b_ref[:, 768:1152], out_columns(refs[0:4]))
        + dot_nt(b_ref[:, 1152:1536], out_columns(refs[4:8]))
    ).astype(bf16)
    out_ref[0:rows] = grad[:, 0:384]
    out_ref[rows : 2 * rows] = grad[:, 384:768]


def out_backward(branch, w_out, pieces, held):
    rows = branch.shape[0]
    operands, specs = out_blocks(pieces)
    return pl.pallas_call(
        out_backward_kernel,
        grid=(1,),
        in_specs=[whole(*branch.shape), whole(*w_out.shape)] + specs + [UNREAD] * len(held),
        out_specs=whole(2 * rows, 384),
        out_shape=jax.ShapeDtypeStruct((2 * rows, 384), bf16),
        compiler_params=params(),
        cost_estimate=SHORT,
    )(branch, w_out, *operands, *held)


def projection(*operands):
    rows = operands[0].shape[0]
    return pl.pallas_call(
        projection_kernel,
        in_specs=[pl.BlockSpec(memory_space=pltpu.VMEM)] * len(operands),
        out_shape=jax.ShapeDtypeStruct((2 * rows, 640), bf16),
        compiler_params=params(),
        cost_estimate=SHORT,
    )(*operands)


def ffn_gradients_kernel(*refs):
    out_ref = refs[-1]

    def rows_of(k):
        return jnp.concatenate([ref[...] for ref in refs[3 * k : 3 * k + 3]], axis=0)

    normed, branch, gate, up, act = (rows_of(k) for k in range(5))
    width = normed.shape[1]
    out_ref[0:width] = dot_tn(normed, gate).astype(bf16)
    out_ref[width : 2 * width] = dot_tn(normed, up).astype(bf16)
    down = dot_tn(act, branch).astype(bf16)
    for a in range(width // 128):
        for b in range(TILE // 128):
            out_ref[2 * width + a * 128 : 2 * width + a * 128 + 128, b * 128 : b * 128 + 128] = down[
                b * 128 : b * 128 + 128, a * 128 : a * 128 + 128
            ]


def ffn_gradients(normed, branch, gate, up, act, held):
    rows, width = normed[0].shape[0], normed[0].shape[1] // 2
    hidden = gate[0].shape[1]
    operands, specs = [], []
    for own, received, at in (normed, branch):
        operands += [own, *received]
        specs.append(pl.BlockSpec((rows, width), lambda i: (0, 0)))
        specs += [pl.BlockSpec((rows // 2, width), lambda i, at=at // width: (0, at))] * 2
    for own, received, at in (gate, up, act):
        operands += [own, *received]
        specs.append(hidden_tile(rows))
        specs += [pl.BlockSpec((rows // 2, TILE), lambda i, at=at // TILE: (0, at + i))] * 2
    return pl.pallas_call(
        ffn_gradients_kernel,
        grid=(hidden // TILE,),
        in_specs=specs + [UNREAD] * len(held),
        out_specs=pl.BlockSpec((3 * width, TILE), lambda i: (0, i)),
        out_shape=jax.ShapeDtypeStruct((3 * width, hidden), bf16),
        compiler_params=params(),
        cost_estimate=SHORT,
    )(*operands, *held)


CHANNELS = (0, 640, 1152, 1664, 2176)


def attention_gradients_kernel(bits, *refs):
    normed, projected, attended, branch = refs[0:4]
    early, last = refs[4:6], refs[6:8]
    outs, total = refs[10:-1], refs[-1]
    total[:, 2048:2176] = refs[8][...]

    def rows_of(own, received, at, width):
        parts = [own[:, :width]] + [ref[:, at : at + width] for ref in received]
        return jnp.concatenate(parts, axis=0)

    total[:, 0:768] = dot_tn(
        rows_of(attended, early, 768, 768), rows_of(branch, last, 1280, 768)
    ).astype(bf16)
    total[:, 768:2048] = dot_tn(
        rows_of(normed, early, 0, 768), rows_of(projected, last, 0, 1280)
    ).astype(bf16)
    for c in range(4):
        columns = slice(CHANNELS[c], CHANNELS[c + 1])
        keep = pl.multiple_of(bits[c] * 384, 384)
        send = pl.multiple_of(384 - bits[c] * 384, 384)
        outs[2 * c][...] = total[pl.ds(keep, 384), columns]
        outs[2 * c + 1][...] = total[pl.ds(send, 384), columns]


def attention_gradients(bits, *operands):
    widths = [b - a for a, b in zip(CHANNELS[:-1], CHANNELS[1:]) for _ in range(2)]
    return list(
        pl.pallas_call(
            attention_gradients_kernel,
            grid=(1,),
            in_specs=[SMEM] + [whole(*operand.shape) for operand in operands[:-1]] + [UNREAD],
            out_specs=[whole(384, w) for w in widths],
            out_shape=[jax.ShapeDtypeStruct((384, w), bf16) for w in widths],
            scratch_shapes=[pltpu.VMEM((768, 2176), bf16)],
            compiler_params=params(),
            cost_estimate=SHORT,
        )(bits, *operands)
    )


def ffn_results_kernel(scale, total_ref, gate_ref, up_ref, down_ref):
    width = gate_ref.shape[0]
    gate_ref[...] = total_ref[0:width].astype(f32) * scale[0]
    up_ref[...] = total_ref[width : 2 * width].astype(f32) * scale[0]
    for a in range(width // 128):
        for b in range(TILE // 128):
            block = total_ref[
                2 * width + a * 128 : 2 * width + a * 128 + 128, b * 128 : b * 128 + 128
            ]
            down_ref[b * 128 : b * 128 + 128, a * 128 : a * 128 + 128] = (
                block.astype(f32) * scale[0]
            )


def ffn_results(scale, total):
    width, hidden = total.shape[0] // 3, total.shape[1]
    return pl.pallas_call(
        ffn_results_kernel,
        grid=(hidden // TILE,),
        in_specs=[SMEM, pl.BlockSpec((3 * width, TILE), lambda i: (0, i))],
        out_specs=(
            hidden_tile(width),
            hidden_tile(width),
            pl.BlockSpec((TILE, width), lambda i: (i, 0)),
        ),
        out_shape=(
            jax.ShapeDtypeStruct((width, hidden), f32),
            jax.ShapeDtypeStruct((width, hidden), f32),
            jax.ShapeDtypeStruct((hidden, width), f32),
        ),
        compiler_params=params(),
        cost_estimate=SHORT,
    )(scale.reshape(1), total)


def local(
    tokens,
    w_query,
    key_projection_weight,
    value_projection_weight,
    w_out,
    w_gate,
    w_up,
    w_down,
    norm_attn,
    norm_ffn,
    doc_lengths,
    valid_mask,
    teacher,
):
    seq_count, row_count, width = tokens.shape
    rows = seq_count * row_count
    half = width // 2
    quarter = width // 4
    dp = lax.axis_index("dp")
    colour = (lax.axis_index("x") + lax.axis_index("y")) % 2
    y_index = lax.axis_index("y")
    group_index = lax.axis_index("x") * 2 + lax.axis_index("z_hi")

    def to_local(value):
        own = jnp.where(dp == 0, value[..., :half], value[..., half:])
        other = jnp.where(dp == 0, value[..., half:], value[..., :half])
        first = jnp.where(colour == 0, other[..., :quarter], other[..., quarter:])
        second = jnp.where(colour == 0, other[..., quarter:], other[..., :quarter])
        return jnp.concatenate([own, first, second], axis=-1)

    def other_half_of(first, second):
        return jnp.concatenate(
            [jnp.where(colour == 0, first, second), jnp.where(colour == 0, second, first)], axis=-1
        )

    def other_half(value):
        return other_half_of(value[..., half : half + quarter], value[..., half + quarter :])

    def from_local(value):
        own, other = value[..., :half], other_half(value)
        return jnp.concatenate(
            [jnp.where(dp == 0, own, other), jnp.where(dp == 0, other, own)], axis=-1
        )

    def two_ways(first, second):
        return z_move(first, 1), z_move(second, -1)

    def over_x(one, two):
        return ring_move(one, "x", 1), ring_move(two, "x", -1)

    def over_y(one, two):
        return ring_move(one, "y", 1), ring_move(two, "y", -1)

    def to_neighbours(value):
        return two_ways(value[:row_count], value[row_count:])

    gains = jnp.stack([norm_attn, norm_ffn])
    gains_other = swap(gains, "dp")
    gains_first = jnp.where(colour == 0, gains_other[:, :quarter], gains_other[:, quarter:])
    gains_second = jnp.where(colour == 0, gains_other[:, quarter:], gains_other[:, :quarter])
    gains_full = jnp.concatenate([gains, gains_first, gains_second], axis=1).astype(f32)
    gain_one, gain_two = gains_full[0], gains_full[1]

    kv = key_projection_weight.shape[1]
    ff = w_gate.shape[1]
    sent = copy_blocks(
        colour,
        [
            [
                (w_query, (quarter, half), lambda c, k=k: (k, 0), 0, 0),
                (key_projection_weight, (quarter, kv), lambda c, k=k: (k, 0), 0, half),
                (value_projection_weight, (quarter, kv), lambda c, k=k: (k, 0), 0, half + kv),
            ]
            for k in range(2)
        ],
        [(quarter, half + 2 * kv)] * 2,
        (gains_other,),
    )
    qkv_one, qkv_two = two_ways(*sent)
    mask_values = valid_mask.reshape(rows).astype(f32)
    blocks = [
        [
            (w_gate, (192, ff), lambda c, k=k: (2 * c + k, 0), 0, 0),
            (w_up, (192, ff), lambda c, k=k: (2 * c + k, 0), 0, ff),
            (w_out, (192, quarter), lambda c, k=k: (2 * k, c), 0, 2 * ff),
            (w_out, (192, quarter), lambda c, k=k: (2 * k + 1, c), 0, 2 * ff + quarter),
        ]
        for k in range(2)
    ]
    wide_z = two_ways(
        *copy_blocks(colour, blocks, [(192, 2 * (ff + quarter))] * 2, (gains_other,))
    )

    count = jnp.full((8, 128), jnp.sum(mask_values), f32)

    residual_in = to_local(tokens.reshape(rows, width)).astype(f32)
    inverse_one = inverse_rms(residual_in)
    normed_one = (residual_in * inverse_one * gain_one).astype(bf16)
    normed_one_other = other_half(normed_one)
    projected = projection(
        normed_one[:, :half],
        normed_one_other,
        w_query,
        key_projection_weight,
        value_projection_weight,
        qkv_one,
        qkv_two,
    )
    mine = lax.all_to_all(projected, "y", 0, 0, tiled=True)
    queries, key_values = copy_blocks(
        colour,
        [
            [(mine, (512, 128), lambda c, k=k: (0, k), 0, 128 * (k - first)) for k in range(first, last)]
            for first, last in ((0, 3), (3, 5))
        ],
        [(512, 384), (512, 256)],
        (),
    )
    pieces = (group_move(key_values, 2), group_move(key_values, 1), key_values)
    blocks = [
        [
            (w_down, (384, quarter), lambda c, k=k: (k, c), 384 * (k - first), 0)
            for k in range(first, last)
        ]
        for first, last in ((0, 3), (3, 5))
    ]
    down_z = two_ways(
        *copy_blocks(colour, blocks, [(1152, quarter), (768, quarter)], pieces[:2])
    )
    bounds = jnp.cumsum(lax.dynamic_index_in_dim(doc_lengths, y_index % 2, 0, keepdims=False))
    scalars = jnp.concatenate([(group_index * 512)[None], bounds]).astype(jnp.int32)
    attended_mine, logs = attention_forward(scalars, queries, pieces, wide_z)
    split = copy_blocks(
        colour,
        [
            [
                (v, (192, ff), lambda c, k=k: (0, k), 0, 0),
                (v, (192, quarter), lambda c, k=k: (0, 10 + k), 0, ff),
            ]
            for k in range(2)
            for v in wide_z
        ],
        [(192, ff + quarter)] * 4,
        pieces[:2],
    )
    returned = lax.all_to_all(attended_mine, "y", 0, 0, tiled=True)
    split_moved = (*over_x(*split[:2]), *over_y(*split[2:]))
    out_pieces = (*wide_z, *split_moved)
    attn_part, attended = out_projection(returned, w_out, out_pieces, ())
    down_parts = copy_blocks(
        colour,
        [
            [(down_z[0], (384, quarter), lambda c, k=k: (k, 0), 384 * k, 0) for k in range(2)],
            [(down_z[0], (384, quarter), lambda c: (2, 0), 0, 0)],
            [(down_z[1], (384, quarter), lambda c: (0, 0), 0, 0)],
            [(down_z[1], (384, quarter), lambda c: (1, 0), 0, 0)],
        ],
        [(768, quarter)] + [(384, quarter)] * 3,
        (),
    )
    down_moved = (
        ring_move(down_parts[0], "x", 1),
        ring_move(down_parts[1], "y", 1),
        ring_move(down_parts[2], "x", -1),
        ring_move(down_parts[3], "y", -1),
    )
    early = to_neighbours(jnp.concatenate([normed_one_other, attended], axis=1))
    weights = (
        w_gate,
        *wide_z,
        *split_moved[:2],
        w_up,
        *wide_z,
        *split_moved[2:],
        w_down,
        *down_z,
        *down_moved,
    )
    attn_total = core_sum(attn_part)
    hidden_state = residual_in + branch_scale * attn_total
    inverse_two = inverse_rms(hidden_state)
    normed_two = (hidden_state * inverse_two * gain_two).astype(bf16)
    gate_pre, up_pre, activated, ffn_part = ffn_forward(normed_two, weights)
    ffn_total = core_sum(ffn_part)
    final_state = hidden_state + branch_scale * ffn_total
    deviation = final_state - to_local(teacher.reshape(rows, width)).astype(f32)
    row_squares = mask_values * jnp.mean(deviation * deviation, axis=-1)
    middle = to_neighbours(jnp.concatenate([other_half(normed_two), activated], axis=1))

    grad_final = deviation * mask_values[:, None]
    branch_two = (branch_scale * grad_final).astype(bf16)
    count = count + pair_move(count, FIRST[0][0])
    grad_gate_pre, grad_up_pre, part = ffn_backward(
        branch_two, weights, gate_pre, up_pre, (*early, count)
    )
    late = to_neighbours(
        jnp.concatenate([other_half(branch_two), grad_gate_pre, grad_up_pre], axis=1)
    )
    grad_normed_two = core_sum(part)

    grad_from_norm, gain_terms_two = norm_backward(
        hidden_state, inverse_two, gain_two, grad_normed_two
    )
    grad_hidden = grad_final + grad_from_norm
    branch_one = (branch_scale * grad_hidden).astype(bf16)
    count = count + pair_move(count, FIRST[0][1])
    grad_attended = out_backward(branch_one, w_out, out_pieces, (count,))
    grad_mine = lax.all_to_all(grad_attended, "y", 0, 0, tiled=True)
    count = count + pair_move(count, FIRST[2][0])
    ffn_grads = ffn_gradients(
        (normed_two, middle, 0),
        (branch_two, late, 0),
        (grad_gate_pre, late, half),
        (grad_up_pre, late, half + ff),
        (activated, middle, half),
        (grad_mine, count),
    )
    ffn_share = lax.psum_scatter(ffn_grads, ("x", "y"), scatter_dimension=0, tiled=True)
    count = count + pair_move(count, FIRST[2][1])
    grad_queries, grad_older, grad_newer, grad_own = attention_backward(
        scalars, queries, grad_mine, logs, pieces, (ffn_grads[:16, :128], count)
    )
    older = group_move(grad_older, -2)
    newer = group_move(grad_newer, -1)
    grad_key_values = (grad_own + newer.astype(f32) + older.astype(f32)).astype(bf16)
    grad_projected = lax.all_to_all(
        jnp.concatenate([grad_queries, grad_key_values], axis=1), "y", 0, 0, tiled=True
    )
    grad_projected = jnp.concatenate([grad_projected[:rows], grad_projected[rows:]], axis=1)
    last = to_neighbours(jnp.concatenate([grad_projected, other_half(branch_one)], axis=1))
    count = count + swap(count, "z_hi")
    grad_normed_one = core_sum(
        projection_backward(
            colour,
            grad_projected,
            w_query,
            key_projection_weight,
            value_projection_weight,
            qkv_one,
            qkv_two,
            count,
        )
    )
    gradient_via_first_norm, gain_terms_one = norm_backward(
        residual_in, inverse_one, gain_one, grad_normed_one
    )
    grad_tokens = from_local(grad_hidden + gradient_via_first_norm)

    ones = jnp.ones((rows, 128), f32)

    def column_sums(terms):
        return lax.dot_general(
            terms, ones, (((0,), (0,)), ((), ())), precision=lax.Precision.HIGHEST
        )

    def on_rows(values):
        return jnp.pad(jnp.broadcast_to(values[:, None], (rows, 128)), ((0, half - rows), (0, 0)))

    entries = [
        column_sums(gain_terms_one[:, :half]),
        column_sums(other_half(gain_terms_one)),
        column_sums(gain_terms_two[:, :half]),
        column_sums(other_half(gain_terms_two)),
        on_rows(row_squares),
    ]
    slot = lax.broadcasted_iota(jnp.int32, (half, 128), 1) // 16
    tile = jnp.zeros((half, 128), f32)
    for k, entry in enumerate(entries):
        tile = jnp.where(slot == k, entry, tile)
    bits = jnp.stack([pair_bit(steps[0]) for steps in FIRST]).astype(jnp.int32)
    count = count + swap(count, "dp")
    cut_rows = attention_gradients(
        bits,
        normed_one,
        grad_projected,
        attended,
        branch_one,
        *early,
        *last,
        tile.astype(bf16),
        count,
    )
    channels = [
        add_moved(cut_rows[2 * k], cut_rows[2 * k + 1], FIRST[k][0]) for k in range(4)
    ]
    (ffn_share,) = hold([z_sum(ffn_share)], *channels)
    ffn_total_grads = lax.all_gather(ffn_share, ("x", "y"), axis=0, tiled=True)
    reduced = jnp.concatenate(reduce_rest(channels), axis=1)
    small = jnp.transpose(reduced[:, 2048:])[::16].astype(f32)
    small_other = swap(small, "dp")
    valid_count = count[0, 0]
    loss_value = (jnp.sum(small[4]) + jnp.sum(small_other[4])) / valid_count
    tokens_total = rows * lax.axis_size(("dp", "x", "z_hi", "y"))
    scale = tokens_total / valid_count

    def scaled(*parts):
        return jnp.concatenate(parts, axis=1).astype(f32) * scale

    layer_out = from_local(final_state.astype(bf16)).reshape(seq_count, row_count, width)
    return (
        layer_out,
        loss_value,
        (grad_tokens * scale).reshape(seq_count, row_count, width),
        scaled(reduced[:, 768:1152], reduced[:, 1408:1792]),
        scaled(reduced[:, 1152:1280], reduced[:, 1792:1920]),
        scaled(reduced[:, 1280:1408], reduced[:, 1920:2048]),
        scaled(reduced[:, :768]),
        *ffn_results(scale, ffn_total_grads),
        (small[0] + small_other[1]) * scale,
        (small[2] + small_other[3]) * scale,
    )


def solution(mesh):
    fine = Mesh(mesh.devices.reshape(2, 4, 2, 4, 2), ("dp", "x", "z_hi", "y", "tensor"))
    ctx = ("x", "z_hi", "y")
    return jax.shard_map(
        local,
        mesh=fine,
        in_specs=(
            P("dp", ctx, None),
            P("dp", "tensor"),
            P("dp", "tensor"),
            P("dp", "tensor"),
            P("tensor", "dp"),
            P("dp", "tensor"),
            P("dp", "tensor"),
            P("tensor", "dp"),
            P("dp"),
            P("dp"),
            P("dp", None),
            P("dp", ctx),
            P("dp", ctx, None),
        ),
        out_specs=(
            P("dp", ctx, None),
            P(),
            P("dp", ctx, None),
            P("dp", "tensor"),
            P("dp", "tensor"),
            P("dp", "tensor"),
            P("tensor", "dp"),
            P("dp", "tensor"),
            P("dp", "tensor"),
            P("tensor", "dp"),
            P("dp"),
            P("dp"),
        ),
        check_vma=False,
    )
```

```python
import math

import jax
import jax.numpy as jnp
from jax import lax
from jax.experimental import pallas as pl
from jax.experimental.pallas import tpu as pltpu
from jax.sharding import Mesh
from jax.sharding import PartitionSpec as P

HEAD = 64
WINDOW = 1024
BLOCK = 128
GROUP = 3
SPAN = WINDOW + BLOCK

branch_scale = 1.4 / math.sqrt(52.0)
norm_epsilon = 1e-05
masked_score = -1e30
scale_factor = 1.0 / math.sqrt(HEAD)
bf16 = jnp.bfloat16
f32 = jnp.float32


def dot(left, right):
    return jnp.dot(left, right, preferred_element_type=f32)


def dot_nt(left, right):
    return lax.dot_general(left, right, (((1,), (1,)), ((), ())), preferred_element_type=f32)


def dot_tn(left, right):
    return lax.dot_general(left, right, (((0,), (0,)), ((), ())), preferred_element_type=f32)


def z_move(value, distance):
    route = []
    for dp in range(2):
        for hi in range(2):
            z = (hi * 2 + dp + distance) % 4
            route.append((dp * 2 + hi, (z % 2) * 2 + z // 2))
    return lax.ppermute(value, ("dp", "z_hi"), route)


def ring_move(value, axis, distance):
    size = lax.axis_size(axis)
    return lax.ppermute(value, axis, [(i, (i + distance) % size) for i in range(size)])


def group_move(value, distance):
    return lax.ppermute(
        value, ("x", "z_hi"), [(i, i + distance) for i in range(8) if 0 <= i + distance < 8]
    )


def swap(value, axis):
    return lax.ppermute(value, axis, [(0, 1), (1, 0)])


PAIRS = {"even": ((0, 1), (1, 0), (2, 3), (3, 2)), "odd": ((0, 3), (3, 0), (1, 2), (2, 1))}


def pair_move(value, step):
    return lax.ppermute(value, step[0], PAIRS[step[1]])


def pair_bit(step):
    index = lax.axis_index(step[0])
    return (index // 2 + index) % 2 if step[1] == "even" else index // 2


def core_sum(part):
    return part.astype(f32) + swap(part, "tensor").astype(f32)


def z_sum(value):
    return (value.astype(f32) + swap(value, "z_hi").astype(f32)).astype(bf16)


def halves(value, step):
    bit = pair_bit(step)
    half = value.shape[0] // 2
    return (
        lax.dynamic_slice_in_dim(value, bit * half, half, 0),
        lax.dynamic_slice_in_dim(value, (1 - bit) * half, half, 0),
    )


def add_moved(keep, send, step):
    return (keep.astype(f32) + pair_move(send, step).astype(f32)).astype(bf16)


def halve(value, step):
    return add_moved(*halves(value, step), step)


def double(value, step):
    other = pair_move(value, step)
    return jnp.where(
        pair_bit(step) == 0,
        jnp.concatenate([value, other], axis=0),
        jnp.concatenate([other, value], axis=0),
    )


FIRST = (
    (("x", "even"), ("x", "odd")),
    (("x", "odd"), ("x", "even")),
    (("y", "even"), ("y", "odd")),
    (("y", "odd"), ("y", "even")),
)
SECOND = ((("y", "even"), ("y", "odd")), (("x", "even"), ("x", "odd")))


def reduce_second(channels):
    return [halve(c, FIRST[i][1]) for i, c in enumerate(channels)]


def reduce_pairs(pairs, level):
    return [halve(c, SECOND[i][level]) for i, c in enumerate(pairs)]


def reduce_rest(pairs, widths):
    at = widths[0] + widths[1]
    total = jnp.concatenate(pairs, axis=1)
    tile = total[:, -128:]
    beside = z_move(tile, 1).astype(f32) + z_move(tile, -1).astype(f32)
    beside = jnp.concatenate([beside[:, 64:], beside[:, :64]], axis=1).astype(bf16)
    total = z_sum(total)
    total = jnp.concatenate([total[:, :-128], total[:, -128:] + beside], axis=1)
    pairs = [total[:, :at], total[:, at:]]
    for level in (1, 0):
        pairs = [double(c, SECOND[i][level]) for i, c in enumerate(pairs)]
    channels = [
        pairs[0][:, : widths[0]],
        pairs[0][:, widths[0] :],
        pairs[1][:, : widths[2]],
        pairs[1][:, widths[2] :],
    ]
    channels = [double(c, FIRST[i][1]) for i, c in enumerate(channels)]
    return [(c, pair_move(c, FIRST[i][0])) for i, c in enumerate(channels)]


def inverse_rms(source):
    return lax.rsqrt(jnp.mean(source * source, axis=-1, keepdims=True) + norm_epsilon)


def norm_backward(source, inverse, gain_vec, grad_normed):
    weighted = grad_normed * gain_vec
    grad_source = inverse * weighted - source * (inverse * inverse * inverse) * jnp.mean(
        source * weighted, axis=-1, keepdims=True
    )
    return (grad_source, grad_normed * source * inverse)


def allowed_keys(scalars, r):
    shape = (BLOCK, SPAN)
    query_pos = scalars[0] + r * BLOCK + lax.broadcasted_iota(jnp.int32, shape, 0)
    key_pos = scalars[0] + r * BLOCK - WINDOW + lax.broadcasted_iota(jnp.int32, shape, 1)
    lowest = jnp.maximum(query_pos - (WINDOW - 1), 0)
    for d in range(1, 5):
        lowest = jnp.maximum(lowest, jnp.where(query_pos >= scalars[d], scalars[d], 0))
    allowed = (key_pos >= lowest) & (key_pos <= query_pos)
    return jnp.concatenate([allowed] * GROUP, axis=0)


def low_half():
    return lax.broadcasted_iota(jnp.int32, (BLOCK, 128), 1) < HEAD


def head_rows(ref, g):
    lanes = low_half() if g == 0 else jnp.logical_not(low_half())
    parts = []
    for h in range(g * GROUP, (g + 1) * GROUP):
        columns = ref[:, h // 2 * 128 : h // 2 * 128 + 128].astype(f32)
        if h % 2 != g:
            columns = pltpu.roll(columns, HEAD, 1)
        parts.append(jnp.where(lanes, columns, 0.0).astype(bf16))
    return jnp.concatenate(parts, axis=0)


def put_heads(ref, results):
    sides = {}
    for g in range(2):
        for j in range(GROUP):
            h = g * GROUP + j
            columns = results[g][j * BLOCK : (j + 1) * BLOCK]
            sides[h] = pltpu.roll(columns, HEAD, 1) if h % 2 != g else columns
    for t in range(GROUP):
        ref[:, t * 128 : (t + 1) * 128] = jnp.where(
            low_half(), sides[2 * t], sides[2 * t + 1]
        ).astype(ref.dtype)


def fill_window(window, older, newer, own):
    window[0:512] = older[...]
    window[512:1024] = newer[...]
    window[1024:1536] = own[...]


def attention_forward_kernel(scalars, q_ref, older, newer, own, *rest):
    out_ref, log_ref, window = rest[-3:]
    r = pl.program_id(0)

    @pl.when(r == 0)
    def _():
        fill_window(window, older, newer, own)

    span = pl.ds(pl.multiple_of(r * BLOCK, BLOCK), SPAN)
    keys = window[span, 0:128]
    values = window[span, 128:256]
    allowed = allowed_keys(scalars, r)
    outs = []
    for g in range(2):
        q3 = head_rows(q_ref, g)
        scores = jnp.where(allowed, dot_nt(q3, keys) * scale_factor, masked_score)
        top = jnp.max(scores, axis=-1, keepdims=True)
        weights = jnp.exp(scores - top)
        total = jnp.sum(weights, axis=-1, keepdims=True)
        log_ref[g] = top + jnp.log(total)
        outs.append(dot((weights * (1.0 / total)).astype(bf16), values))
    put_heads(out_ref, outs)


def attention_backward_kernel(scalars, q_ref, g_ref, log_ref, older, newer, own, *rest):
    dq_ref, older_ref, newer_ref, own_ref, window, sums = rest[-6:]
    r = pl.program_id(0)

    @pl.when(r == 0)
    def _():
        fill_window(window, older, newer, own)
        sums[...] = jnp.zeros_like(sums)

    span = pl.ds(pl.multiple_of(r * BLOCK, BLOCK), SPAN)
    keys = window[span, 0:128]
    values = window[span, 128:256]
    allowed = allowed_keys(scalars, r)
    outs = []
    for g in range(2):
        q3 = head_rows(q_ref, g)
        g3 = head_rows(g_ref, g)
        scores = jnp.where(allowed, dot_nt(q3, keys) * scale_factor, masked_score)
        probs = jnp.exp(scores - log_ref[g])
        grad_probs = dot_nt(g3, values)
        inner = jnp.sum(grad_probs * probs, axis=-1, keepdims=True)
        grad_scores = (probs * (grad_probs - inner)).astype(bf16)
        outs.append(dot(grad_scores, keys) * scale_factor)
        sums[span, 0:128] += dot_tn(grad_scores, q3)
        sums[span, 128:256] += dot_tn(probs.astype(bf16), g3)
    put_heads(dq_ref, outs)

    @pl.when(r == 3)
    def _():
        for part, ref in enumerate((older_ref, newer_ref, own_ref)):
            rows = slice(part * 512, (part + 1) * 512)
            ref[:, 0:128] = (sums[rows, 0:128] * scale_factor).astype(ref.dtype)
            ref[:, 128:256] = sums[rows, 128:256].astype(ref.dtype)


SMEM = pl.BlockSpec(memory_space=pltpu.SMEM)
UNREAD = pl.BlockSpec(memory_space=pl.ANY)
SHORT = pl.CostEstimate(flops=1000, bytes_accessed=1000, transcendentals=0)


def whole(*shape):
    return pl.BlockSpec(shape, lambda i: (0,) * len(shape))


def params(mebibytes=24):
    return pltpu.CompilerParams(vmem_limit_bytes=mebibytes * 1024 * 1024)


def copy_blocks(index, outputs, shapes, held):
    blocks = [block for output in outputs for block in output]

    def kernel(index_ref, *refs):
        outs = refs[len(blocks) + len(held) :]
        at = 0
        for output, out in zip(outputs, outs):
            for _, shape, _, row, column in output:
                out[row : row + shape[0], column : column + shape[1]] = refs[at][...]
                at += 1

    return pl.pallas_call(
        kernel,
        grid_spec=pltpu.PrefetchScalarGridSpec(
            num_scalar_prefetch=1,
            grid=(1,),
            in_specs=[
                pl.BlockSpec(block[1], lambda i, ref, place=block[2]: place(ref[0]))
                for block in blocks
            ]
            + [UNREAD] * len(held),
            out_specs=[pl.BlockSpec(shape, lambda i, ref: (0, 0)) for shape in shapes],
        ),
        out_shape=[
            jax.ShapeDtypeStruct(shape, output[0][0].dtype)
            for shape, output in zip(shapes, outputs)
        ],
        compiler_params=params(20),
        cost_estimate=SHORT,
    )(index.reshape(1), *[block[0] for block in blocks], *held)


def hold(values, *held):
    return copy_blocks(
        jnp.zeros((), jnp.int32),
        [[(v, v.shape, lambda c: (0, 0), 0, 0)] for v in values],
        [v.shape for v in values],
        held,
    )


def attention_forward(scalars, queries, pieces, held):
    return pl.pallas_call(
        attention_forward_kernel,
        grid=(4,),
        in_specs=[SMEM, pl.BlockSpec((BLOCK, 384), lambda i: (i, 0))]
        + [whole(512, 256)] * 3
        + [UNREAD] * len(held),
        out_specs=(
            pl.BlockSpec((BLOCK, 384), lambda i: (i, 0)),
            pl.BlockSpec((2, GROUP * BLOCK, 1), lambda i: (i, 0, 0)),
        ),
        out_shape=(
            jax.ShapeDtypeStruct((512, 384), bf16),
            jax.ShapeDtypeStruct((8, GROUP * BLOCK, 1), f32),
        ),
        scratch_shapes=[pltpu.VMEM((1536, 256), bf16)],
        compiler_params=params(),
        cost_estimate=SHORT,
    )(scalars, queries, *pieces, *held)


def attention_backward(scalars, queries, grads, logs, pieces, held):
    return pl.pallas_call(
        attention_backward_kernel,
        grid=(4,),
        in_specs=[
            SMEM,
            pl.BlockSpec((BLOCK, 384), lambda i: (i, 0)),
            pl.BlockSpec((BLOCK, 384), lambda i: (i, 0)),
            pl.BlockSpec((2, GROUP * BLOCK, 1), lambda i: (i, 0, 0)),
        ]
        + [whole(512, 256)] * 3
        + [UNREAD] * len(held),
        out_specs=(
            pl.BlockSpec((BLOCK, 384), lambda i: (i, 0)),
            whole(512, 256),
            whole(512, 256),
            whole(512, 256),
        ),
        out_shape=(
            jax.ShapeDtypeStruct((512, 384), bf16),
            jax.ShapeDtypeStruct((512, 256), bf16),
            jax.ShapeDtypeStruct((512, 256), bf16),
            jax.ShapeDtypeStruct((512, 256), f32),
        ),
        scratch_shapes=[pltpu.VMEM((1536, 256), bf16), pltpu.VMEM((1536, 256), f32)],
        compiler_params=params(),
        cost_estimate=SHORT,
    )(scalars, queries, grads, logs, *pieces, *held)


ROWS_AT = (0, 768, 960, 1152, 1344, 1536)
COLUMNS_AT = (0, 768, 1152, 1536)
TILE = 384
TOKENS = 16384


def ffn_weights(refs, step):
    gate = [refs[k][...] for k in range(5)]
    up = [refs[k][...] for k in range(5, 10)]
    down = [refs[10][...]]
    for at in (11, 15):
        down.append(
            jnp.concatenate(
                [
                    jnp.where(step < 3, refs[at][...], refs[at + 1][...]),
                    jnp.where(step < 2, refs[at + 2][...], refs[at + 3][...]),
                ],
                axis=0,
            )
        )
    return gate, up, down


def ffn_operands(w_gate, w_up, w_down, one, two):
    def columns(rows, place):
        return pl.BlockSpec((rows, TILE), lambda i: (0, place(i)))

    operands = [w_gate, *one[0], *one[1], w_up, *two[0], *two[1], w_down]
    specs = ([columns(768, lambda i: i)] + [columns(192, lambda i: i)] * 4) * 2
    specs += [pl.BlockSpec((TILE, 768), lambda i: (i, 0))]
    for (first, second), shift in ((two[0], 5), (two[2], 0)):
        for odd in range(2):
            operands += [first, second]
            specs += [
                columns(192, lambda i, o=odd, s=shift: jnp.minimum(2 * i + o, 4) + s),
                columns(192, lambda i, o=odd, s=shift: jnp.maximum(2 * i + o - 5, 0) + s),
            ]
    return operands, specs


def ffn_forward_kernel(n_ref, *refs):
    g_ref, u_ref, a_ref, out_ref, total = refs[-5:]
    step = pl.program_id(0)
    gate, up, down = ffn_weights(refs, step)

    def times(weights):
        result = None
        for k, weight in enumerate(weights):
            part = dot(n_ref[:, ROWS_AT[k] : ROWS_AT[k + 1]], weight)
            result = part if result is None else result + part
        return result

    gate_pre, up_pre = times(gate), times(up)
    g_ref[...] = gate_pre
    u_ref[...] = up_pre
    activated = (gate_pre * jax.nn.sigmoid(gate_pre) * up_pre).astype(bf16)
    a_ref[...] = activated

    @pl.when(step == 0)
    def _():
        total[...] = jnp.zeros_like(total)

    for k, weight in enumerate(down):
        total[:, COLUMNS_AT[k] : COLUMNS_AT[k + 1]] += dot(activated, weight)

    @pl.when(step == pl.num_programs(0) - 1)
    def _():
        out_ref[...] = total[...].astype(bf16)


def ffn_backward_kernel(b_ref, *refs):
    g_ref, u_ref = refs[19:21]
    gg_ref, gu_ref, out_ref, total = refs[-4:]
    step = pl.program_id(0)
    gate, up, down = ffn_weights(refs, step)
    grad = None
    for k, weight in enumerate(down):
        part = dot_nt(b_ref[:, COLUMNS_AT[k] : COLUMNS_AT[k + 1]], weight)
        grad = part if grad is None else grad + part
    grad = grad.astype(bf16).astype(f32)
    gate_pre, up_pre = g_ref[...], u_ref[...]
    sigmoid = jax.nn.sigmoid(gate_pre)
    grad_gate = (grad * up_pre * sigmoid * (1.0 + gate_pre * (1.0 - sigmoid))).astype(bf16)
    grad_up = (grad * gate_pre * sigmoid).astype(bf16)
    gg_ref[...] = grad_gate
    gu_ref[...] = grad_up

    @pl.when(step == 0)
    def _():
        total[...] = jnp.zeros_like(total)

    for k in range(5):
        total[:, ROWS_AT[k] : ROWS_AT[k + 1]] += dot_nt(grad_gate, gate[k]) + dot_nt(
            grad_up, up[k]
        )

    @pl.when(step == pl.num_programs(0) - 1)
    def _():
        out_ref[...] = total[...].astype(bf16)


def hidden_tile(rows):
    return pl.BlockSpec((rows, TILE), lambda i: (0, i))


def ffn_forward(normed, weights):
    rows, width = normed.shape
    operands, specs = ffn_operands(*weights)
    hidden = weights[2].shape[0]
    return pl.pallas_call(
        ffn_forward_kernel,
        grid=(hidden // TILE,),
        in_specs=[whole(rows, width)] + specs,
        out_specs=(hidden_tile(rows), hidden_tile(rows), hidden_tile(rows), whole(rows, width)),
        out_shape=(
            jax.ShapeDtypeStruct((rows, hidden), f32),
            jax.ShapeDtypeStruct((rows, hidden), f32),
            jax.ShapeDtypeStruct((rows, hidden), bf16),
            jax.ShapeDtypeStruct((rows, width), bf16),
        ),
        scratch_shapes=[pltpu.VMEM((rows, width), f32)],
        compiler_params=params(32),
        cost_estimate=SHORT,
    )(normed, *operands)


def ffn_backward(branch, weights, gate_pre, up_pre, held):
    rows, width = branch.shape
    operands, specs = ffn_operands(*weights)
    hidden = weights[2].shape[0]
    return pl.pallas_call(
        ffn_backward_kernel,
        grid=(hidden // TILE,),
        in_specs=[whole(rows, width)]
        + specs
        + [hidden_tile(rows)] * 2
        + [UNREAD] * len(held),
        out_specs=(hidden_tile(rows), hidden_tile(rows), whole(rows, width)),
        out_shape=(
            jax.ShapeDtypeStruct((rows, hidden), bf16),
            jax.ShapeDtypeStruct((rows, hidden), bf16),
            jax.ShapeDtypeStruct((rows, width), bf16),
        ),
        scratch_shapes=[pltpu.VMEM((rows, width), f32)],
        compiler_params=params(32),
        cost_estimate=SHORT,
    )(branch, *operands, gate_pre, up_pre, *held)


def projection_kernel(n_own, n_other, wq, wk, wv, one, two, out_ref):
    own = n_own[...]
    first, second = n_other[:, :384], n_other[:, 384:]
    rows = own.shape[0]
    for p in range(2):
        place = pl.ds(p * rows, rows)
        q_at, kv_at = slice(p * 384, p * 384 + 384), slice(p * 128, p * 128 + 128)
        for weight, own_at, at, out_at in (
            (wq, q_at, p * 384, slice(0, 384)),
            (wk, kv_at, 768 + p * 128, slice(384, 512)),
            (wv, kv_at, 1024 + p * 128, slice(512, 640)),
        ):
            there = slice(at, at + out_at.stop - out_at.start)
            out_ref[place, out_at] = (
                dot(own, weight[:, own_at])
                + dot(first, one[:, there])
                + dot(second, two[:, there])
            ).astype(bf16)


def projection_backward_kernel(colour, g_ref, wq, wk, wv, one, two, out_ref):
    grad = jnp.concatenate(
        [
            g_ref[:, a:b]
            for a, b in ((0, 384), (640, 1024), (384, 512), (1024, 1152), (512, 640), (1152, 1280))
        ],
        axis=1,
    )
    out_ref[:, 0:768] = (
        dot_nt(grad[:, 0:768], wq[...])
        + dot_nt(grad[:, 768:1024], wk[...])
        + dot_nt(grad[:, 1024:1280], wv[...])
    ).astype(bf16)
    first = dot_nt(grad, one[...]).astype(bf16)
    second = dot_nt(grad, two[...]).astype(bf16)

    @pl.when(colour[0] == 0)
    def _():
        out_ref[:, 768:1152] = first
        out_ref[:, 1152:1536] = second

    @pl.when(colour[0] != 0)
    def _():
        out_ref[:, 768:1152] = second
        out_ref[:, 1152:1536] = first


def projection_backward(colour, *operands):
    rows = operands[0].shape[0]
    return pl.pallas_call(
        projection_backward_kernel,
        grid=(1,),
        in_specs=[SMEM] + [whole(*operand.shape) for operand in operands],
        out_specs=whole(rows, 1536),
        out_shape=jax.ShapeDtypeStruct((rows, 1536), bf16),
        compiler_params=params(),
        cost_estimate=SHORT,
    )(colour.reshape(1), *operands)


def out_blocks(pieces):
    operands = [piece for piece in pieces for _ in range(2)]
    specs = [pl.BlockSpec((192, 384), lambda i, k=k: (0, k)) for k in (5, 6)] * 4
    return operands, specs


def out_columns(refs):
    return jnp.concatenate([ref[...] for ref in refs], axis=0)


def out_projection_kernel(back_ref, w_ref, *refs):
    part_ref, attended_ref = refs[-2:]
    rows = attended_ref.shape[0]
    attended = jnp.concatenate([back_ref[0:rows], back_ref[rows : 2 * rows]], axis=1)
    attended_ref[...] = attended
    part_ref[:, 0:768] = dot(attended, w_ref[...]).astype(bf16)
    part_ref[:, 768:1152] = dot(attended, out_columns(refs[0:4])).astype(bf16)
    part_ref[:, 1152:1536] = dot(attended, out_columns(refs[4:8])).astype(bf16)


def out_projection(back, w_out, pieces, held):
    rows = back.shape[0] // 2
    operands, specs = out_blocks(pieces)
    return pl.pallas_call(
        out_projection_kernel,
        grid=(1,),
        in_specs=[whole(*back.shape), whole(*w_out.shape)] + specs + [UNREAD] * len(held),
        out_specs=(whole(rows, 1536), whole(rows, 768)),
        out_shape=(
            jax.ShapeDtypeStruct((rows, 1536), bf16),
            jax.ShapeDtypeStruct((rows, 768), bf16),
        ),
        compiler_params=params(),
        cost_estimate=SHORT,
    )(back, w_out, *operands, *held)


def out_backward_kernel(b_ref, w_ref, *refs):
    out_ref = refs[-1]
    rows = b_ref.shape[0]
    grad = (
        dot_nt(b_ref[:, 0:768], w_ref[...])
        + dot_nt(b_ref[:, 768:1152], out_columns(refs[0:4]))
        + dot_nt(b_ref[:, 1152:1536], out_columns(refs[4:8]))
    ).astype(bf16)
    out_ref[0:rows] = grad[:, 0:384]
    out_ref[rows : 2 * rows] = grad[:, 384:768]


def out_backward(branch, w_out, pieces, held):
    rows = branch.shape[0]
    operands, specs = out_blocks(pieces)
    return pl.pallas_call(
        out_backward_kernel,
        grid=(1,),
        in_specs=[whole(*branch.shape), whole(*w_out.shape)] + specs + [UNREAD] * len(held),
        out_specs=whole(2 * rows, 384),
        out_shape=jax.ShapeDtypeStruct((2 * rows, 384), bf16),
        compiler_params=params(),
        cost_estimate=SHORT,
    )(branch, w_out, *operands, *held)


def projection(*operands):
    rows = operands[0].shape[0]
    return pl.pallas_call(
        projection_kernel,
        in_specs=[pl.BlockSpec(memory_space=pltpu.VMEM)] * len(operands),
        out_shape=jax.ShapeDtypeStruct((2 * rows, 640), bf16),
        compiler_params=params(),
        cost_estimate=SHORT,
    )(*operands)


def merge_kernel(q_ref, own, newer, older, *rest):
    out_ref = rest[-1]
    out_ref[:, 0:384] = q_ref[...]
    out_ref[:, 384:640] = (
        own[...] + newer[...].astype(f32) + older[...].astype(f32)
    ).astype(bf16)


def merge(grad_queries, own, newer, older, held):
    operands = (grad_queries, own, newer, older)
    return pl.pallas_call(
        merge_kernel,
        grid=(1,),
        in_specs=[whole(*operand.shape) for operand in operands] + [UNREAD] * len(held),
        out_specs=whole(512, 640),
        out_shape=jax.ShapeDtypeStruct((512, 640), bf16),
        compiler_params=params(),
        cost_estimate=SHORT,
    )(*operands, *held)


def add_kernel(keep, moved, *rest):
    rest[-1][...] = (keep[...].astype(f32) + moved[...].astype(f32)).astype(bf16)


def add_rows(keep, moved, held):
    return pl.pallas_call(
        add_kernel,
        grid=(1,),
        in_specs=[whole(*keep.shape)] * 2 + [UNREAD] * len(held),
        out_specs=whole(*keep.shape),
        out_shape=jax.ShapeDtypeStruct(keep.shape, bf16),
        compiler_params=params(),
        cost_estimate=SHORT,
    )(keep, moved, *held)


def ffn_gradients_kernel(*refs):
    out_ref = refs[-1]

    def rows_of(k):
        return jnp.concatenate([ref[...] for ref in refs[3 * k : 3 * k + 3]], axis=0)

    normed, branch, gate, up, act = (rows_of(k) for k in range(5))
    width = normed.shape[1]
    out_ref[0:width] = dot_tn(normed, gate).astype(bf16)
    out_ref[width : 2 * width] = dot_tn(normed, up).astype(bf16)
    down = dot_tn(act, branch).astype(bf16)
    for a in range(width // 128):
        for b in range(TILE // 128):
            out_ref[2 * width + a * 128 : 2 * width + a * 128 + 128, b * 128 : b * 128 + 128] = down[
                b * 128 : b * 128 + 128, a * 128 : a * 128 + 128
            ]


def ffn_gradients(normed, branch, gate, up, act, held):
    rows, width = normed[0].shape[0], normed[0].shape[1] // 2
    hidden = gate[0].shape[1]
    operands, specs = [], []
    for own, received, at in (normed, branch):
        operands += [own, *received]
        specs.append(pl.BlockSpec((rows, width), lambda i: (0, 0)))
        specs += [pl.BlockSpec((rows // 2, width), lambda i, at=at // width: (0, at))] * 2
    for own, received, at in (gate, up, act):
        operands += [own, *received]
        specs.append(hidden_tile(rows))
        specs += [pl.BlockSpec((rows // 2, TILE), lambda i, at=at // TILE: (0, at + i))] * 2
    return pl.pallas_call(
        ffn_gradients_kernel,
        grid=(hidden // TILE,),
        in_specs=specs + [UNREAD] * len(held),
        out_specs=pl.BlockSpec((3 * width, TILE), lambda i: (0, i)),
        out_shape=jax.ShapeDtypeStruct((3 * width, hidden), bf16),
        compiler_params=params(32),
        cost_estimate=SHORT,
    )(*operands, *held)


CHANNELS = (0, 640, 1152, 1664, 2176)


def attention_gradients_kernel(bits, *refs):
    normed, projected, attended, branch = refs[0:4]
    early, last = refs[4:6], refs[6:8]
    outs, total = refs[9:-1], refs[-1]
    total[:, 2048:2176] = refs[8][...]

    def rows_of(own, received, at, width):
        parts = [own[:, :width]] + [ref[:, at : at + width] for ref in received]
        return jnp.concatenate(parts, axis=0)

    total[:, 0:768] = dot_tn(
        rows_of(attended, early, 768, 768), rows_of(branch, last, 1280, 768)
    ).astype(bf16)
    total[:, 768:2048] = dot_tn(
        rows_of(normed, early, 0, 768), rows_of(projected, last, 0, 1280)
    ).astype(bf16)
    for c in range(4):
        columns = slice(CHANNELS[c], CHANNELS[c + 1])
        keep = pl.multiple_of(bits[c] * 384, 384)
        send = pl.multiple_of(384 - bits[c] * 384, 384)
        outs[2 * c][...] = total[pl.ds(keep, 384), columns]
        outs[2 * c + 1][...] = total[pl.ds(send, 384), columns]


def attention_gradients(bits, *operands):
    widths = [b - a for a, b in zip(CHANNELS[:-1], CHANNELS[1:]) for _ in range(2)]
    return list(
        pl.pallas_call(
            attention_gradients_kernel,
            grid=(1,),
            in_specs=[SMEM] + [whole(*operand.shape) for operand in operands],
            out_specs=[whole(384, w) for w in widths],
            out_shape=[jax.ShapeDtypeStruct((384, w), bf16) for w in widths],
            scratch_shapes=[pltpu.VMEM((768, 2176), bf16)],
            compiler_params=params(),
            cost_estimate=SHORT,
        )(bits, *operands)
    )


def ffn_results_kernel(one, two, total_ref, gate_ref, up_ref, down_ref):
    scale = TOKENS / count_of(one, two)
    width = gate_ref.shape[0]
    gate_ref[...] = total_ref[0:width].astype(f32) * scale
    up_ref[...] = total_ref[width : 2 * width].astype(f32) * scale
    for a in range(width // 128):
        for b in range(TILE // 128):
            block = total_ref[
                2 * width + a * 128 : 2 * width + a * 128 + 128, b * 128 : b * 128 + 128
            ]
            down_ref[b * 128 : b * 128 + 128, a * 128 : a * 128 + 128] = (
                block.astype(f32) * scale
            )


def ffn_results(pair, total):
    width, hidden = total.shape[0] // 3, total.shape[1]
    return pl.pallas_call(
        ffn_results_kernel,
        grid=(hidden // TILE,),
        in_specs=[whole(*value.shape) for value in pair]
        + [pl.BlockSpec((3 * width, TILE), lambda i: (0, i))],
        out_specs=(
            hidden_tile(width),
            hidden_tile(width),
            pl.BlockSpec((TILE, width), lambda i: (i, 0)),
        ),
        out_shape=(
            jax.ShapeDtypeStruct((width, hidden), f32),
            jax.ShapeDtypeStruct((width, hidden), f32),
            jax.ShapeDtypeStruct((hidden, width), f32),
        ),
        compiler_params=params(20),
        cost_estimate=SHORT,
    )(*pair, total)


PLACES = (
    (0, 0, 640, 3, 0),
    (1, 0, 128, 3, 640),
    (1, 128, 384, 0, 0),
    (2, 0, 128, 1, 0),
    (2, 128, 128, 2, 0),
    (2, 256, 256, 0, 384),
    (3, 0, 128, 0, 640),
    (3, 128, 128, 1, 128),
    (3, 256, 128, 2, 128),
)


def count_of(ref_one, ref_two):
    total = None
    for ref in (ref_one, ref_two):
        for lane in (32, 96):
            part = jnp.sum(ref[:, 384 + lane : 385 + lane].astype(f32), axis=0, keepdims=True)
            total = part if total is None else total + part
    return total


def attention_results_kernel(bits, *refs):
    outs, rows_ref, tile = refs[8:12], refs[12], refs[13]
    count = count_of(refs[6], refs[7])
    scale = TOKENS / count
    for c, at, width, out, there in PLACES:
        for side in range(2):
            first = bits[c] * 384 if side == 0 else 384 - bits[c] * 384
            outs[out][pl.ds(pl.multiple_of(first, 384), 384), there : there + width] = (
                refs[2 * c + side][:, at : at + width].astype(f32) * scale
            )
    for side in range(2):
        first = bits[3] * 384 if side == 0 else 384 - bits[3] * 384
        tile[pl.ds(pl.multiple_of(first, 384), 384), :] = refs[6 + side][:, 384:512].astype(f32)
    lines = jnp.transpose(tile[...])
    rows_ref[0:1] = (lines[0:1] + lines[72:73]) * scale
    rows_ref[1:2] = (lines[16:17] + lines[88:89]) * scale
    squares = jnp.sum(lines[40:41] + lines[104:105], axis=1, keepdims=True)
    rows_ref[2:3] = jnp.broadcast_to(squares / count, (1, 768))
    rows_ref[3:4] = jnp.broadcast_to(scale, (1, 768))


def attention_results(bits, pairs):
    operands = [value for pair in pairs for value in pair]
    widths = (768, 256, 256, 768)
    return pl.pallas_call(
        attention_results_kernel,
        grid=(1,),
        in_specs=[SMEM] + [whole(*operand.shape) for operand in operands],
        out_specs=[whole(768, width) for width in widths] + [whole(8, 768)],
        out_shape=[jax.ShapeDtypeStruct((768, width), f32) for width in widths]
        + [jax.ShapeDtypeStruct((8, 768), f32)],
        scratch_shapes=[pltpu.VMEM((768, 128), f32)],
        compiler_params=params(),
        cost_estimate=SHORT,
    )(bits, *operands)


def local(
    tokens,
    w_query,
    key_projection_weight,
    value_projection_weight,
    w_out,
    w_gate,
    w_up,
    w_down,
    norm_attn,
    norm_ffn,
    doc_lengths,
    valid_mask,
    teacher,
):
    seq_count, row_count, width = tokens.shape
    rows = seq_count * row_count
    half = width // 2
    quarter = width // 4
    dp = lax.axis_index("dp")
    colour = (lax.axis_index("x") + lax.axis_index("y")) % 2
    y_index = lax.axis_index("y")
    group_index = lax.axis_index("x") * 2 + lax.axis_index("z_hi")

    def to_local(value):
        own = jnp.where(dp == 0, value[..., :half], value[..., half:])
        other = jnp.where(dp == 0, value[..., half:], value[..., :half])
        first = jnp.where(colour == 0, other[..., :quarter], other[..., quarter:])
        second = jnp.where(colour == 0, other[..., quarter:], other[..., :quarter])
        return jnp.concatenate([own, first, second], axis=-1)

    def other_half_of(first, second):
        return jnp.concatenate(
            [jnp.where(colour == 0, first, second), jnp.where(colour == 0, second, first)], axis=-1
        )

    def other_half(value):
        return other_half_of(value[..., half : half + quarter], value[..., half + quarter :])

    def from_local(value):
        own, other = value[..., :half], other_half(value)
        return jnp.concatenate(
            [jnp.where(dp == 0, own, other), jnp.where(dp == 0, other, own)], axis=-1
        )

    def two_ways(first, second):
        return z_move(first, 1), z_move(second, -1)

    def over_x(one, two):
        return ring_move(one, "x", 1), ring_move(two, "x", -1)

    def over_y(one, two):
        return ring_move(one, "y", 1), ring_move(two, "y", -1)

    def to_neighbours(value):
        return two_ways(value[:row_count], value[row_count:])

    gains = jnp.stack([norm_attn, norm_ffn])
    gains_other = swap(gains, "dp")
    gains_first = jnp.where(colour == 0, gains_other[:, :quarter], gains_other[:, quarter:])
    gains_second = jnp.where(colour == 0, gains_other[:, quarter:], gains_other[:, :quarter])
    gains_full = jnp.concatenate([gains, gains_first, gains_second], axis=1).astype(f32)
    gain_one, gain_two = gains_full[0], gains_full[1]

    kv = key_projection_weight.shape[1]
    ff = w_gate.shape[1]
    sent = copy_blocks(
        colour,
        [
            [
                (w_query, (quarter, half), lambda c, k=k: (k, 0), 0, 0),
                (key_projection_weight, (quarter, kv), lambda c, k=k: (k, 0), 0, half),
                (value_projection_weight, (quarter, kv), lambda c, k=k: (k, 0), 0, half + kv),
            ]
            for k in range(2)
        ],
        [(quarter, half + 2 * kv)] * 2,
        (gains_other,),
    )
    qkv_one, qkv_two = two_ways(*sent)
    mask_values = valid_mask.reshape(rows).astype(f32)
    blocks = [
        [
            (w_gate, (192, ff), lambda c, k=k: (2 * c + k, 0), 0, 0),
            (w_out, (192, quarter), lambda c, k=k: (2 * k, c), 0, ff),
            (w_out, (192, quarter), lambda c, k=k: (2 * k + 1, c), 0, ff + quarter),
        ]
        for k in range(2)
    ]
    first_z = two_ways(
        *copy_blocks(colour, blocks, [(192, ff + 2 * quarter)] * 2, (gains_other,))
    )

    residual_in = to_local(tokens.reshape(rows, width)).astype(f32)
    inverse_one = inverse_rms(residual_in)
    normed_one = (residual_in * inverse_one * gain_one).astype(bf16)
    normed_one_other = other_half(normed_one)
    projected = projection(
        normed_one[:, :half],
        normed_one_other,
        w_query,
        key_projection_weight,
        value_projection_weight,
        qkv_one,
        qkv_two,
    )
    mine = lax.all_to_all(projected, "y", 0, 0, tiled=True)
    queries, key_values = copy_blocks(
        colour,
        [
            [(mine, (512, 128), lambda c, k=k: (0, k), 0, 128 * (k - first)) for k in range(first, last)]
            for first, last in ((0, 3), (3, 5))
        ],
        [(512, 384), (512, 256)],
        (),
    )
    pieces = (group_move(key_values, 2), group_move(key_values, 1), key_values)
    blocks = [
        [(w_up, (192, ff), lambda c, k=k: (2 * c + k, 0), 0, 0)]
        + [
            (w_down, (192, quarter), lambda c, k=k, b=b: (5 * k + b, c), 0, ff + quarter * b)
            for b in range(5)
        ]
        for k in range(2)
    ]
    second_z = two_ways(*copy_blocks(colour, blocks, [(192, 2 * ff)] * 2, pieces[:2]))
    first = (first_z, over_x(*hold(first_z, pieces[0])))
    bounds = jnp.cumsum(lax.dynamic_index_in_dim(doc_lengths, y_index % 2, 0, keepdims=False))
    scalars = jnp.concatenate([(group_index * 512)[None], bounds]).astype(jnp.int32)
    attended_mine, logs = attention_forward(scalars, queries, pieces, ())
    attended_mine, *split = copy_blocks(
        colour,
        [[(attended_mine, attended_mine.shape, lambda c: (0, 0), 0, 0)]]
        + [[(v, (192, ff), lambda c, k=k: (0, k), 0, 0)] for k in range(2) for v in second_z],
        [attended_mine.shape] + [(192, ff)] * 4,
        (),
    )
    second = (second_z, over_x(*split[:2]), over_y(*split[2:]))
    returned = lax.all_to_all(attended_mine, "y", 0, 0, tiled=True)
    out_pieces = (*first[0], *first[1])
    attn_part, attended = out_projection(
        returned, w_out, out_pieces, (*second[1], *second[2])
    )
    early = to_neighbours(jnp.concatenate([normed_one_other, attended], axis=1))
    weights = (w_gate, w_up, w_down, first, second)
    attn_total = core_sum(attn_part)
    hidden_state = residual_in + branch_scale * attn_total
    inverse_two = inverse_rms(hidden_state)
    normed_two = (hidden_state * inverse_two * gain_two).astype(bf16)
    gate_pre, up_pre, activated, ffn_part = ffn_forward(normed_two, weights)
    ffn_total = core_sum(ffn_part)
    final_state = hidden_state + branch_scale * ffn_total
    deviation = final_state - to_local(teacher.reshape(rows, width)).astype(f32)
    row_squares = mask_values * jnp.mean(deviation * deviation, axis=-1)
    middle = to_neighbours(jnp.concatenate([other_half(normed_two), activated], axis=1))

    grad_final = deviation * mask_values[:, None]
    branch_two = (branch_scale * grad_final).astype(bf16)
    grad_gate_pre, grad_up_pre, part = ffn_backward(
        branch_two, weights, gate_pre, up_pre, early
    )
    late = to_neighbours(
        jnp.concatenate([other_half(branch_two), grad_gate_pre, grad_up_pre], axis=1)
    )
    grad_normed_two = core_sum(part)

    grad_from_norm, gain_terms_two = norm_backward(
        hidden_state, inverse_two, gain_two, grad_normed_two
    )
    grad_hidden = grad_final + grad_from_norm
    branch_one = (branch_scale * grad_hidden).astype(bf16)
    grad_attended = out_backward(branch_one, w_out, out_pieces, ())
    grad_mine = lax.all_to_all(grad_attended, "y", 0, 0, tiled=True)
    grad_queries, grad_older, grad_newer, grad_own = attention_backward(
        scalars, queries, grad_mine, logs, pieces, ()
    )
    ffn_grads = ffn_gradients(
        (normed_two, middle, 0),
        (branch_two, late, 0),
        (grad_gate_pre, late, half),
        (grad_up_pre, late, half + ff),
        (activated, middle, half),
        (grad_older,),
    )
    ffn_share = lax.psum_scatter(ffn_grads, ("x", "y"), scatter_dimension=0, tiled=True)
    older = group_move(grad_older, -2)
    newer = group_move(grad_newer, -1)
    grad_projected = lax.all_to_all(
        merge(grad_queries, grad_own, newer, older, ()), "y", 0, 0, tiled=True
    )
    grad_projected = jnp.concatenate([grad_projected[:rows], grad_projected[rows:]], axis=1)
    last = to_neighbours(jnp.concatenate([grad_projected, other_half(branch_one)], axis=1))
    grad_normed_one = core_sum(
        projection_backward(
            colour,
            grad_projected,
            w_query,
            key_projection_weight,
            value_projection_weight,
            qkv_one,
            qkv_two,
        )
    )
    gradient_via_first_norm, gain_terms_one = norm_backward(
        residual_in, inverse_one, gain_one, grad_normed_one
    )
    grad_tokens = from_local(grad_hidden + gradient_via_first_norm)

    ones = jnp.ones((rows, 128), f32)

    def column_sums(terms):
        return lax.dot_general(
            terms, ones, (((0,), (0,)), ((), ())), precision=lax.Precision.HIGHEST
        )

    def on_rows(values):
        return jnp.pad(jnp.broadcast_to(values[:, None], (rows, 128)), ((0, half - rows), (0, 0)))

    entries = [
        column_sums(gain_terms_one[:, :half]),
        column_sums(other_half(gain_terms_one)),
        column_sums(gain_terms_two[:, :half]),
        column_sums(other_half(gain_terms_two)),
        on_rows(mask_values),
        on_rows(row_squares),
    ]
    slot = lax.broadcasted_iota(jnp.int32, (half, 128), 1) // 8
    tile = jnp.zeros((half, 128), f32)
    for k, entry in enumerate(entries):
        tile = jnp.where(slot == k, entry, tile)
    bits = jnp.stack([pair_bit(steps[0]) for steps in FIRST]).astype(jnp.int32)
    cut_rows = attention_gradients(
        bits,
        normed_one,
        grad_projected,
        attended,
        branch_one,
        *early,
        *last,
        tile.astype(bf16),
    )
    channels = [
        add_rows(cut_rows[2 * k], pair_move(cut_rows[2 * k + 1], FIRST[k][0]), ())
        for k in range(4)
    ]
    (ffn_share,) = hold([ffn_share], *channels)
    ffn_share = z_sum(ffn_share)
    channels = reduce_second(channels)
    pairs = [jnp.concatenate(channels[k : k + 2], axis=1) for k in (0, 2)]
    pairs = reduce_pairs(pairs, 0)
    (ffn_share,) = hold([ffn_share], *pairs)
    ffn_total_grads = lax.all_gather(ffn_share, ("x", "y"), axis=0, tiled=True)
    pairs = reduce_pairs(pairs, 1)
    pairs = reduce_rest(pairs, [c.shape[1] for c in channels])
    *attn_results, small = attention_results(bits, pairs)
    scale = small[3, 0]

    layer_out = from_local(final_state.astype(bf16)).reshape(seq_count, row_count, width)
    return (
        layer_out,
        small[2, 0],
        (grad_tokens * scale).reshape(seq_count, row_count, width),
        *attn_results,
        *ffn_results(pairs[3], ffn_total_grads),
        small[0],
        small[1],
    )


def solution(mesh):
    fine = Mesh(mesh.devices.reshape(2, 4, 2, 4, 2), ("dp", "x", "z_hi", "y", "tensor"))
    ctx = ("x", "z_hi", "y")
    return jax.shard_map(
        local,
        mesh=fine,
        in_specs=(
            P("dp", ctx, None),
            P("dp", "tensor"),
            P("dp", "tensor"),
            P("dp", "tensor"),
            P("tensor", "dp"),
            P("dp", "tensor"),
            P("dp", "tensor"),
            P("tensor", "dp"),
            P("dp"),
            P("dp"),
            P("dp", None),
            P("dp", ctx),
            P("dp", ctx, None),
        ),
        out_specs=(
            P("dp", ctx, None),
            P(),
            P("dp", ctx, None),
            P("dp", "tensor"),
            P("dp", "tensor"),
            P("dp", "tensor"),
            P("tensor", "dp"),
            P("dp", "tensor"),
            P("dp", "tensor"),
            P("tensor", "dp"),
            P("dp"),
            P("dp"),
        ),
        check_vma=False,
    )
```

```python
import math

import jax
import jax.numpy as jnp
from jax import lax
from jax.experimental import pallas as pl
from jax.experimental.pallas import tpu as pltpu
from jax.sharding import Mesh
from jax.sharding import PartitionSpec as P

HEAD = 64
WINDOW = 1024
BLOCK = 128
GROUP = 3
SPAN = WINDOW + BLOCK

branch_scale = 1.4 / math.sqrt(52.0)
norm_epsilon = 1e-05
masked_score = -1e30
scale_factor = 1.0 / math.sqrt(HEAD)
bf16 = jnp.bfloat16
f32 = jnp.float32


def dot(left, right):
    return jnp.dot(left, right, preferred_element_type=f32)


def dot_nt(left, right):
    return lax.dot_general(left, right, (((1,), (1,)), ((), ())), preferred_element_type=f32)


def dot_tn(left, right):
    return lax.dot_general(left, right, (((0,), (0,)), ((), ())), preferred_element_type=f32)


def z_move(value, distance):
    route = []
    for dp in range(2):
        for hi in range(2):
            z = (hi * 2 + dp + distance) % 4
            route.append((dp * 2 + hi, (z % 2) * 2 + z // 2))
    return lax.ppermute(value, ("dp", "z_hi"), route)


def ring_move(value, axis, distance):
    size = lax.axis_size(axis)
    return lax.ppermute(value, axis, [(i, (i + distance) % size) for i in range(size)])


def group_move(value, distance):
    return lax.ppermute(
        value, ("x", "z_hi"), [(i, i + distance) for i in range(8) if 0 <= i + distance < 8]
    )


def swap(value, axis):
    return lax.ppermute(value, axis, [(0, 1), (1, 0)])


PAIRS = {"even": ((0, 1), (1, 0), (2, 3), (3, 2)), "odd": ((0, 3), (3, 0), (1, 2), (2, 1))}


def pair_move(value, step):
    return lax.ppermute(value, step[0], PAIRS[step[1]])


def pair_bit(step):
    index = lax.axis_index(step[0])
    return (index // 2 + index) % 2 if step[1] == "even" else index // 2


def core_sum(part):
    return part.astype(f32) + swap(part, "tensor").astype(f32)


def z_sum(value):
    return (value.astype(f32) + swap(value, "z_hi").astype(f32)).astype(bf16)


def halves(value, step):
    bit = pair_bit(step)
    half = value.shape[0] // 2
    return (
        lax.dynamic_slice_in_dim(value, bit * half, half, 0),
        lax.dynamic_slice_in_dim(value, (1 - bit) * half, half, 0),
    )


def add_moved(keep, send, step):
    return (keep.astype(f32) + pair_move(send, step).astype(f32)).astype(bf16)


def halve(value, step):
    return add_moved(*halves(value, step), step)


def double(value, step):
    other = pair_move(value, step)
    return jnp.where(
        pair_bit(step) == 0,
        jnp.concatenate([value, other], axis=0),
        jnp.concatenate([other, value], axis=0),
    )


FIRST = (
    (("x", "even"), ("x", "odd")),
    (("x", "odd"), ("x", "even")),
    (("y", "even"), ("y", "odd")),
    (("y", "odd"), ("y", "even")),
)
SECOND = ((("y", "even"), ("y", "odd")), (("x", "even"), ("x", "odd")))


def reduce_second(channels):
    return [halve(c, FIRST[i][1]) for i, c in enumerate(channels)]


def reduce_pairs(pairs, level):
    return [halve(c, SECOND[i][level]) for i, c in enumerate(pairs)]


def reduce_rest(pairs, widths):
    at = widths[0] + widths[1]
    rows = pairs[0].shape[0]
    (total,) = copy_blocks(
        jnp.zeros((), jnp.int32),
        [
            [
                (pair, pair.shape, lambda c: (0, 0), 0, first)
                for pair, first in zip(pairs, (0, at))
            ]
        ],
        [(rows, sum(widths))],
        (),
    )
    tile = total[:, -128:]
    beside = z_move(tile, 1).astype(f32) + z_move(tile, -1).astype(f32)
    beside = jnp.concatenate([beside[:, 64:], beside[:, :64]], axis=1).astype(bf16)
    total = z_sum(total)
    total = jnp.concatenate([total[:, :-128], total[:, -128:] + beside], axis=1)
    pairs = [total[:, :at], total[:, at:]]
    for level in (1, 0):
        pairs = [double(c, SECOND[i][level]) for i, c in enumerate(pairs)]
    channels = [
        pairs[0][:, : widths[0]],
        pairs[0][:, widths[0] :],
        pairs[1][:, : widths[2]],
        pairs[1][:, widths[2] :],
    ]
    channels = [double(c, FIRST[i][1]) for i, c in enumerate(channels)]
    return [(c, pair_move(c, FIRST[i][0])) for i, c in enumerate(channels)]


def inverse_rms(source):
    return lax.rsqrt(jnp.mean(source * source, axis=-1, keepdims=True) + norm_epsilon)


def norm_backward(source, inverse, gain_vec, grad_normed):
    weighted = grad_normed * gain_vec
    grad_source = inverse * weighted - source * (inverse * inverse * inverse) * jnp.mean(
        source * weighted, axis=-1, keepdims=True
    )
    return (grad_source, grad_normed * source * inverse)


def allowed_keys(scalars, r):
    shape = (BLOCK, SPAN)
    query_pos = scalars[0] + r * BLOCK + lax.broadcasted_iota(jnp.int32, shape, 0)
    key_pos = scalars[0] + r * BLOCK - WINDOW + lax.broadcasted_iota(jnp.int32, shape, 1)
    lowest = jnp.maximum(query_pos - (WINDOW - 1), 0)
    for d in range(1, 5):
        lowest = jnp.maximum(lowest, jnp.where(query_pos >= scalars[d], scalars[d], 0))
    allowed = (key_pos >= lowest) & (key_pos <= query_pos)
    return jnp.concatenate([allowed] * (2 * GROUP), axis=0)


def low_half():
    return lax.broadcasted_iota(jnp.int32, (BLOCK, 128), 1) < HEAD


def head_rows(ref):
    parts = []
    for h in range(2 * GROUP):
        g = h // GROUP
        lanes = low_half() if g == 0 else jnp.logical_not(low_half())
        columns = ref[:, h // 2 * 128 : h // 2 * 128 + 128].astype(f32)
        if h % 2 != g:
            columns = pltpu.roll(columns, HEAD, 1)
        parts.append(jnp.where(lanes, columns, 0.0).astype(bf16))
    return jnp.concatenate(parts, axis=0)


def put_heads(ref, results):
    sides = []
    for h in range(2 * GROUP):
        columns = results[h * BLOCK : (h + 1) * BLOCK]
        sides.append(pltpu.roll(columns, HEAD, 1) if h % 2 != h // GROUP else columns)
    for t in range(GROUP):
        ref[:, t * 128 : (t + 1) * 128] = jnp.where(
            low_half(), sides[2 * t], sides[2 * t + 1]
        ).astype(ref.dtype)


def fill_window(window, older, newer, own):
    window[0:512] = older[...]
    window[512:1024] = newer[...]
    window[1024:1536] = own[...]


def attention_forward_kernel(scalars, q_ref, older, newer, own, *rest):
    out_ref, log_ref, window = rest[-3:]
    r = pl.program_id(0)

    @pl.when(r == 0)
    def _():
        fill_window(window, older, newer, own)

    span = pl.ds(pl.multiple_of(r * BLOCK, BLOCK), SPAN)
    keys = window[span, 0:128]
    values = window[span, 128:256]
    allowed = allowed_keys(scalars, r)
    scores = jnp.where(allowed, dot_nt(head_rows(q_ref), keys) * scale_factor, masked_score)
    top = jnp.max(scores, axis=-1, keepdims=True)
    weights = jnp.exp(scores - top)
    total = jnp.sum(weights, axis=-1, keepdims=True)
    log_ref[0] = top + jnp.log(total)
    put_heads(out_ref, dot((weights * (1.0 / total)).astype(bf16), values))


def attention_backward_kernel(scalars, q_ref, g_ref, log_ref, older, newer, own, *rest):
    dq_ref, older_ref, newer_ref, own_ref, window, sums = rest[-6:]
    r = pl.program_id(0)

    @pl.when(r == 0)
    def _():
        fill_window(window, older, newer, own)
        sums[...] = jnp.zeros_like(sums)

    span = pl.ds(pl.multiple_of(r * BLOCK, BLOCK), SPAN)
    keys = window[span, 0:128]
    values = window[span, 128:256]
    allowed = allowed_keys(scalars, r)
    q6 = head_rows(q_ref)
    g6 = head_rows(g_ref)
    scores = jnp.where(allowed, dot_nt(q6, keys) * scale_factor, masked_score)
    probs = jnp.exp(scores - log_ref[0])
    grad_probs = dot_nt(g6, values)
    inner = jnp.sum(grad_probs * probs, axis=-1, keepdims=True)
    grad_scores = (probs * (grad_probs - inner)).astype(bf16)
    put_heads(dq_ref, dot(grad_scores, keys) * scale_factor)
    sums[span, 0:128] += dot_tn(grad_scores, q6)
    sums[span, 128:256] += dot_tn(probs.astype(bf16), g6)

    @pl.when(r == 3)
    def _():
        for part, ref in enumerate((older_ref, newer_ref, own_ref)):
            rows = slice(part * 512, (part + 1) * 512)
            ref[:, 0:128] = (sums[rows, 0:128] * scale_factor).astype(ref.dtype)
            ref[:, 128:256] = sums[rows, 128:256].astype(ref.dtype)


SMEM = pl.BlockSpec(memory_space=pltpu.SMEM)
UNREAD = pl.BlockSpec(memory_space=pl.ANY)
SHORT = pl.CostEstimate(flops=1000, bytes_accessed=1000, transcendentals=0)


def whole(*shape):
    return pl.BlockSpec(shape, lambda i: (0,) * len(shape))


def params(mebibytes=24):
    return pltpu.CompilerParams(vmem_limit_bytes=mebibytes * 1024 * 1024)


def copy_blocks(index, outputs, shapes, held):
    blocks = [block for output in outputs for block in output]

    def kernel(index_ref, *refs):
        outs = refs[len(blocks) + len(held) :]
        at = 0
        for output, out in zip(outputs, outs):
            for _, shape, _, row, column in output:
                out[row : row + shape[0], column : column + shape[1]] = refs[at][...]
                at += 1

    return pl.pallas_call(
        kernel,
        grid_spec=pltpu.PrefetchScalarGridSpec(
            num_scalar_prefetch=1,
            grid=(1,),
            in_specs=[
                pl.BlockSpec(block[1], lambda i, ref, place=block[2]: place(ref[0]))
                for block in blocks
            ]
            + [UNREAD] * len(held),
            out_specs=[pl.BlockSpec(shape, lambda i, ref: (0, 0)) for shape in shapes],
        ),
        out_shape=[
            jax.ShapeDtypeStruct(shape, output[0][0].dtype)
            for shape, output in zip(shapes, outputs)
        ],
        compiler_params=params(20),
        cost_estimate=SHORT,
    )(index.reshape(1), *[block[0] for block in blocks], *held)


def hold(values, *held):
    return copy_blocks(
        jnp.zeros((), jnp.int32),
        [[(v, v.shape, lambda c: (0, 0), 0, 0)] for v in values],
        [v.shape for v in values],
        held,
    )


def attention_forward(scalars, queries, pieces, held):
    return pl.pallas_call(
        attention_forward_kernel,
        grid=(4,),
        in_specs=[SMEM, pl.BlockSpec((BLOCK, 384), lambda i: (i, 0))]
        + [whole(512, 256)] * 3
        + [UNREAD] * len(held),
        out_specs=(
            pl.BlockSpec((BLOCK, 384), lambda i: (i, 0)),
            pl.BlockSpec((1, 2 * GROUP * BLOCK, 1), lambda i: (i, 0, 0)),
        ),
        out_shape=(
            jax.ShapeDtypeStruct((512, 384), bf16),
            jax.ShapeDtypeStruct((4, 2 * GROUP * BLOCK, 1), f32),
        ),
        scratch_shapes=[pltpu.VMEM((1536, 256), bf16)],
        compiler_params=params(32),
        cost_estimate=SHORT,
    )(scalars, queries, *pieces, *held)


def attention_backward(scalars, queries, grads, logs, pieces, held):
    return pl.pallas_call(
        attention_backward_kernel,
        grid=(4,),
        in_specs=[
            SMEM,
            pl.BlockSpec((BLOCK, 384), lambda i: (i, 0)),
            pl.BlockSpec((BLOCK, 384), lambda i: (i, 0)),
            pl.BlockSpec((1, 2 * GROUP * BLOCK, 1), lambda i: (i, 0, 0)),
        ]
        + [whole(512, 256)] * 3
        + [UNREAD] * len(held),
        out_specs=(
            pl.BlockSpec((BLOCK, 384), lambda i: (i, 0)),
            whole(512, 256),
            whole(512, 256),
            whole(512, 256),
        ),
        out_shape=(
            jax.ShapeDtypeStruct((512, 384), bf16),
            jax.ShapeDtypeStruct((512, 256), bf16),
            jax.ShapeDtypeStruct((512, 256), bf16),
            jax.ShapeDtypeStruct((512, 256), f32),
        ),
        scratch_shapes=[pltpu.VMEM((1536, 256), bf16), pltpu.VMEM((1536, 256), f32)],
        compiler_params=params(32),
        cost_estimate=SHORT,
    )(scalars, queries, grads, logs, *pieces, *held)


TILE = 384
TOKENS = 16384
CHUNKS = ((0, 1024), (1024, 1920))


def weight_copies(refs, gate, up, down, sems):
    copies = {"gate": [], "up": [], "down": []}

    def add(group, source, target):
        count = sum(len(entries) for entries in copies.values())
        copies[group].append(pltpu.make_async_copy(source, target, sems.at[count]))

    for group, target, at in (("gate", gate, 0), ("up", up, 5)):
        add(group, refs[at], target.at[pl.ds(0, 768), :])
        for k in range(4):
            add(
                group,
                refs[at + 1 + k].at[:, pl.ds(0, 1920)],
                target.at[pl.ds(768 + 192 * k, 192), :],
            )
    add("down", refs[10], down.at[:, pl.ds(0, 768)])
    for side in range(2):
        for b in range(5):
            rows = pl.ds(960 * side + 192 * b, 192)
            add(
                "down",
                refs[6 + side].at[:, pl.ds(1920 + 384 * b, 384)],
                down.at[rows, pl.ds(768, 384)],
            )
            add(
                "down",
                refs[11 + side].at[:, pl.ds(384 * b, 384)],
                down.at[rows, pl.ds(1152, 384)],
            )
    return copies


def weight_operands(w_gate, w_up, w_down, one, two):
    return [w_gate, *one[0], *one[1], w_up, *two[0], *two[1], w_down, *two[2]]


WEIGHT_SCRATCH = [
    pltpu.VMEM((1536, 1920), bf16),
    pltpu.VMEM((1536, 1920), bf16),
    pltpu.VMEM((1920, 1536), bf16),
    pltpu.SemaphoreType.DMA((31,)),
]


def start_all(copies, order):
    for group in order:
        for copy in copies[group]:
            copy.start()


def wait_all(copies):
    for copy in copies:
        copy.wait()


def ffn_forward_kernel(x_ref, own, moved, gain, *refs):
    weights = refs[:13]
    h_ref, n_ref, r_ref, g_ref, u_ref, a_ref, out_ref, gate, up, down, sems = refs[13:]
    copies = weight_copies(weights, gate, up, down, sems)
    start_all(copies, ("gate", "up", "down"))
    hidden = x_ref[...] + branch_scale * (own[...].astype(f32) + moved[...].astype(f32))
    inverse = inverse_rms(hidden)
    h_ref[...] = hidden
    r_ref[...] = inverse
    n_ref[...] = (hidden * inverse * gain[...]).astype(bf16)
    wait_all(copies["gate"])
    for a, b in CHUNKS:
        g_ref[:, a:b] = dot(n_ref[...], gate[:, a:b])
    wait_all(copies["up"])
    for a, b in CHUNKS:
        up_pre = dot(n_ref[...], up[:, a:b])
        u_ref[:, a:b] = up_pre
        gate_pre = g_ref[:, a:b]
        a_ref[:, a:b] = (gate_pre * jax.nn.sigmoid(gate_pre) * up_pre).astype(bf16)
    wait_all(copies["down"])
    out_ref[...] = dot(a_ref[...], down[...]).astype(bf16)


def ffn_backward_kernel(b_ref, g_ref, u_ref, *refs):
    weights = refs[:13]
    gg_ref, gu_ref, out_ref, gate, up, down, sems = refs[-7:]
    copies = weight_copies(weights, gate, up, down, sems)
    start_all(copies, ("down", "gate", "up"))
    wait_all(copies["down"])
    for a, b in CHUNKS:
        grad = dot_nt(b_ref[...], down[a:b, :]).astype(bf16).astype(f32)
        gate_pre, up_pre = g_ref[:, a:b], u_ref[:, a:b]
        sigmoid = jax.nn.sigmoid(gate_pre)
        gg_ref[:, a:b] = (
            grad * up_pre * sigmoid * (1.0 + gate_pre * (1.0 - sigmoid))
        ).astype(bf16)
        gu_ref[:, a:b] = (grad * gate_pre * sigmoid).astype(bf16)
    wait_all(copies["gate"])
    part = dot_nt(gg_ref[...], gate[...])
    wait_all(copies["up"])
    out_ref[...] = (part + dot_nt(gu_ref[...], up[...])).astype(bf16)


def ffn_forward(residual, own, moved, gain, weights):
    rows, width = residual.shape
    operands = weight_operands(*weights)
    hidden = weights[2].shape[0]
    shapes = [
        ((rows, width), f32),
        ((rows, width), bf16),
        ((rows, 1), f32),
        ((rows, hidden), f32),
        ((rows, hidden), f32),
        ((rows, hidden), bf16),
        ((rows, width), bf16),
    ]
    return pl.pallas_call(
        ffn_forward_kernel,
        grid=(1,),
        in_specs=[whole(rows, width)] * 3 + [whole(1, width)] + [UNREAD] * len(operands),
        out_specs=[whole(*shape) for shape, _ in shapes],
        out_shape=[jax.ShapeDtypeStruct(*entry) for entry in shapes],
        scratch_shapes=WEIGHT_SCRATCH,
        compiler_params=params(48),
        cost_estimate=SHORT,
    )(residual, own, moved, gain.reshape(1, width), *operands)


def ffn_backward(branch, gate_pre, up_pre, weights, held):
    rows, width = branch.shape
    operands = weight_operands(*weights)
    hidden = weights[2].shape[0]
    shapes = [((rows, hidden), bf16), ((rows, hidden), bf16), ((rows, width), bf16)]
    return pl.pallas_call(
        ffn_backward_kernel,
        grid=(1,),
        in_specs=[whole(rows, width)]
        + [whole(rows, hidden)] * 2
        + [UNREAD] * (len(operands) + len(held)),
        out_specs=[whole(*shape) for shape, _ in shapes],
        out_shape=[jax.ShapeDtypeStruct(*entry) for entry in shapes],
        scratch_shapes=WEIGHT_SCRATCH,
        compiler_params=params(44),
        cost_estimate=SHORT,
    )(branch, gate_pre, up_pre, *operands, *held)


def hidden_tile(rows):
    return pl.BlockSpec((rows, TILE), lambda i: (0, i))


def projection_kernel(n_own, n_other, wq, wk, wv, one, two, out_ref):
    own = n_own[...]
    first, second = n_other[:, :384], n_other[:, 384:]
    rows = own.shape[0]
    for p in range(2):
        place = pl.ds(p * rows, rows)
        q_at, kv_at = slice(p * 384, p * 384 + 384), slice(p * 128, p * 128 + 128)
        for weight, own_at, at, out_at in (
            (wq, q_at, p * 384, slice(0, 384)),
            (wk, kv_at, 768 + p * 128, slice(384, 512)),
            (wv, kv_at, 1024 + p * 128, slice(512, 640)),
        ):
            there = slice(at, at + out_at.stop - out_at.start)
            out_ref[place, out_at] = (
                dot(own, weight[:, own_at])
                + dot(first, one[:, there])
                + dot(second, two[:, there])
            ).astype(bf16)


def projection_backward_kernel(colour, g_ref, wq, wk, wv, one, two, out_ref):
    grad = jnp.concatenate(
        [
            g_ref[:, a:b]
            for a, b in ((0, 384), (640, 1024), (384, 512), (1024, 1152), (512, 640), (1152, 1280))
        ],
        axis=1,
    )
    out_ref[:, 0:768] = (
        dot_nt(grad[:, 0:768], wq[...])
        + dot_nt(grad[:, 768:1024], wk[...])
        + dot_nt(grad[:, 1024:1280], wv[...])
    ).astype(bf16)
    first = dot_nt(grad, one[...]).astype(bf16)
    second = dot_nt(grad, two[...]).astype(bf16)

    @pl.when(colour[0] == 0)
    def _():
        out_ref[:, 768:1152] = first
        out_ref[:, 1152:1536] = second

    @pl.when(colour[0] != 0)
    def _():
        out_ref[:, 768:1152] = second
        out_ref[:, 1152:1536] = first


def projection_backward(colour, *operands):
    rows = operands[0].shape[0]
    return pl.pallas_call(
        projection_backward_kernel,
        grid=(1,),
        in_specs=[SMEM] + [whole(*operand.shape) for operand in operands],
        out_specs=whole(rows, 1536),
        out_shape=jax.ShapeDtypeStruct((rows, 1536), bf16),
        compiler_params=params(),
        cost_estimate=SHORT,
    )(colour.reshape(1), *operands)


def out_blocks(pieces):
    operands = [piece for piece in pieces for _ in range(2)]
    specs = [pl.BlockSpec((192, 384), lambda i, k=k: (0, k)) for k in (5, 6)] * 4
    return operands, specs


def out_columns(refs):
    return jnp.concatenate([ref[...] for ref in refs], axis=0)


def out_projection_kernel(back_ref, w_ref, *refs):
    part_ref, attended_ref = refs[-2:]
    rows = attended_ref.shape[0]
    attended = jnp.concatenate([back_ref[0:rows], back_ref[rows : 2 * rows]], axis=1)
    attended_ref[...] = attended
    part_ref[:, 0:768] = dot(attended, w_ref[...]).astype(bf16)
    part_ref[:, 768:1152] = dot(attended, out_columns(refs[0:4])).astype(bf16)
    part_ref[:, 1152:1536] = dot(attended, out_columns(refs[4:8])).astype(bf16)


def out_projection(back, w_out, pieces, held):
    rows = back.shape[0] // 2
    operands, specs = out_blocks(pieces)
    return pl.pallas_call(
        out_projection_kernel,
        grid=(1,),
        in_specs=[whole(*back.shape), whole(*w_out.shape)] + specs + [UNREAD] * len(held),
        out_specs=(whole(rows, 1536), whole(rows, 768)),
        out_shape=(
            jax.ShapeDtypeStruct((rows, 1536), bf16),
            jax.ShapeDtypeStruct((rows, 768), bf16),
        ),
        compiler_params=params(),
        cost_estimate=SHORT,
    )(back, w_out, *operands, *held)


def out_backward_kernel(b_ref, w_ref, *refs):
    out_ref = refs[-1]
    rows = b_ref.shape[0]
    grad = (
        dot_nt(b_ref[:, 0:768], w_ref[...])
        + dot_nt(b_ref[:, 768:1152], out_columns(refs[0:4]))
        + dot_nt(b_ref[:, 1152:1536], out_columns(refs[4:8]))
    ).astype(bf16)
    out_ref[0:rows] = grad[:, 0:384]
    out_ref[rows : 2 * rows] = grad[:, 384:768]


def out_backward(branch, w_out, pieces):
    rows = branch.shape[0]
    operands, specs = out_blocks(pieces)
    return pl.pallas_call(
        out_backward_kernel,
        grid=(1,),
        in_specs=[whole(*branch.shape), whole(*w_out.shape)] + specs,
        out_specs=whole(2 * rows, 384),
        out_shape=jax.ShapeDtypeStruct((2 * rows, 384), bf16),
        compiler_params=params(),
        cost_estimate=SHORT,
    )(branch, w_out, *operands)


def projection(*operands):
    rows = operands[0].shape[0]
    return pl.pallas_call(
        projection_kernel,
        in_specs=[pl.BlockSpec(memory_space=pltpu.VMEM)] * len(operands),
        out_shape=jax.ShapeDtypeStruct((2 * rows, 640), bf16),
        compiler_params=params(),
        cost_estimate=SHORT,
    )(*operands)


def merge_kernel(q_ref, own, newer, older, *rest):
    out_ref = rest[-1]
    out_ref[:, 0:384] = q_ref[...]
    out_ref[:, 384:640] = (
        own[...] + newer[...].astype(f32) + older[...].astype(f32)
    ).astype(bf16)


def merge(grad_queries, own, newer, older, held):
    operands = (grad_queries, own, newer, older)
    return pl.pallas_call(
        merge_kernel,
        grid=(1,),
        in_specs=[whole(*operand.shape) for operand in operands] + [UNREAD] * len(held),
        out_specs=whole(512, 640),
        out_shape=jax.ShapeDtypeStruct((512, 640), bf16),
        compiler_params=params(),
        cost_estimate=SHORT,
    )(*operands, *held)


def ffn_gradients_kernel(normed, branch, gate, up, act, m_one, m_two, l_one, l_two, *rest):
    out_ref, n_all, b_all, gate_all, up_all, act_all, total, in_sems, out_sems = rest[-9:]
    rows, width, hidden = 256, 768, 1920
    copies = {}
    for name, own, received, at, target in (
        ("normed", normed, (m_one, m_two), 0, n_all),
        ("gate", gate, (l_one, l_two), width, gate_all),
        ("up", up, (l_one, l_two), width + hidden, up_all),
        ("act", act, (m_one, m_two), width, act_all),
        ("branch", branch, (l_one, l_two), 0, b_all),
    ):
        columns = target.shape[1]
        parts = [(own.at[:, pl.ds(0, columns)], target.at[pl.ds(0, rows), :])]
        for k, part in enumerate(received):
            parts.append(
                (
                    part.at[:, pl.ds(at, columns)],
                    target.at[pl.ds(rows + 128 * k, 128), :],
                )
            )
        base = 3 * len(copies)
        copies[name] = [
            pltpu.make_async_copy(source, place, in_sems.at[base + k])
            for k, (source, place) in enumerate(parts)
        ]
        for copy in copies[name]:
            copy.start()

    def send(k):
        place = pl.ds(k * width, width)
        copy = pltpu.make_async_copy(total.at[place, :], out_ref.at[place, :], out_sems.at[k])
        copy.start()
        return copy

    wait_all(copies["normed"])
    wait_all(copies["gate"])
    for a, b in CHUNKS:
        total[0:width, a:b] = dot_tn(n_all[...], gate_all[:, a:b]).astype(bf16)
    sent = [send(0)]
    wait_all(copies["up"])
    for a, b in CHUNKS:
        total[width : 2 * width, a:b] = dot_tn(n_all[...], up_all[:, a:b]).astype(bf16)
    sent.append(send(1))
    wait_all(copies["act"])
    wait_all(copies["branch"])
    for a, b in CHUNKS:
        down = dot_tn(act_all[:, a:b], b_all[...]).astype(bf16)
        for r in range(width // 128):
            for c in range((b - a) // 128):
                total[
                    2 * width + r * 128 : 2 * width + r * 128 + 128, a + c * 128 : a + c * 128 + 128
                ] = down[c * 128 : c * 128 + 128, r * 128 : r * 128 + 128]
    sent.append(send(2))
    wait_all(sent)


def ffn_gradients(normed, branch, gate, up, act, middle, late, held):
    operands = (normed, branch, gate, up, act, *middle, *late, *held)
    return pl.pallas_call(
        ffn_gradients_kernel,
        grid=(1,),
        in_specs=[UNREAD] * len(operands),
        out_specs=pl.BlockSpec(memory_space=pltpu.HBM),
        out_shape=jax.ShapeDtypeStruct((2304, 1920), bf16),
        scratch_shapes=[pltpu.VMEM((512, 768), bf16)] * 2
        + [pltpu.VMEM((512, 1920), bf16)] * 3
        + [
            pltpu.VMEM((2304, 1920), bf16),
            pltpu.SemaphoreType.DMA((15,)),
            pltpu.SemaphoreType.DMA((3,)),
        ],
        compiler_params=params(40),
        cost_estimate=SHORT,
    )(*operands)


CHANNELS = (0, 640, 1152, 1664, 2176)


def attention_gradients_kernel(bits, *refs):
    normed, projected, attended, branch = refs[0:4]
    early, last, branch_moved = refs[4:6], refs[6:8], refs[8:10]
    outs, total = refs[11:-1], refs[-1]
    total[:, 2048:2176] = refs[10][...]

    def rows_of(own, received, at, width):
        parts = [own[:, :width]] + [ref[:, at : at + width] for ref in received]
        return jnp.concatenate(parts, axis=0)

    total[:, 0:768] = dot_tn(
        rows_of(attended, early, 768, 768), rows_of(branch, branch_moved, 0, 768)
    ).astype(bf16)
    total[:, 768:2048] = dot_tn(
        rows_of(normed, early, 0, 768), rows_of(projected, last, 0, 1280)
    ).astype(bf16)
    for c in range(4):
        columns = slice(CHANNELS[c], CHANNELS[c + 1])
        keep = pl.multiple_of(bits[c] * 384, 384)
        send = pl.multiple_of(384 - bits[c] * 384, 384)
        outs[2 * c][...] = total[pl.ds(keep, 384), columns]
        outs[2 * c + 1][...] = total[pl.ds(send, 384), columns]


def attention_gradients(bits, *operands):
    widths = [b - a for a, b in zip(CHANNELS[:-1], CHANNELS[1:]) for _ in range(2)]
    return list(
        pl.pallas_call(
            attention_gradients_kernel,
            grid=(1,),
            in_specs=[SMEM] + [whole(*operand.shape) for operand in operands],
            out_specs=[whole(384, w) for w in widths],
            out_shape=[jax.ShapeDtypeStruct((384, w), bf16) for w in widths],
            scratch_shapes=[pltpu.VMEM((768, 2176), bf16)],
            compiler_params=params(),
            cost_estimate=SHORT,
        )(bits, *operands)
    )


def ffn_results_kernel(one, two, total_hbm, *refs):
    outs, total, f_gate, f_up, f_down, in_sems, out_sems = refs[0:3], *refs[3:]
    width, hidden = 768, 1920
    targets = (f_gate, f_up, f_down)
    chunks = []
    for m in range(2):
        for r in range(2):
            place = pl.ds(m * width + r * 384, 384)
            chunks.append((m, r, (place, pl.ds(0, hidden)), (pl.ds(r * 384, 384), pl.ds(0, hidden))))
    for r, (a, b) in enumerate(CHUNKS):
        place = (pl.ds(2 * width, width), pl.ds(a, b - a))
        chunks.append((2, r, place, (pl.ds(a, b - a), pl.ds(0, width))))
    arriving, leaving = [], []
    for k, (_, _, place, _) in enumerate(chunks):
        arriving.append(
            pltpu.make_async_copy(total_hbm.at[place], total.at[place], in_sems.at[k])
        )
        arriving[-1].start()
    scale = TOKENS / count_of(one, two)
    for k, (m, r, _, there) in enumerate(chunks):
        arriving[k].wait()
        if m < 2:
            rows = slice(r * 384, r * 384 + 384)
            source = slice(m * width + r * 384, m * width + r * 384 + 384)
            targets[m][rows] = total[source].astype(f32) * scale
        else:
            a, b = CHUNKS[r]
            for p in range(a // 128, b // 128):
                for q in range(width // 128):
                    f_down[p * 128 : p * 128 + 128, q * 128 : q * 128 + 128] = (
                        total[
                            2 * width + q * 128 : 2 * width + q * 128 + 128,
                            p * 128 : p * 128 + 128,
                        ].astype(f32)
                        * scale
                    )
        leaving.append(
            pltpu.make_async_copy(targets[m].at[there], outs[m].at[there], out_sems.at[k])
        )
        leaving[-1].start()
    wait_all(leaving)


def ffn_results(pair, total):
    width, hidden = total.shape[0] // 3, total.shape[1]
    shapes = ((width, hidden), (width, hidden), (hidden, width))
    hbm = pl.BlockSpec(memory_space=pltpu.HBM)
    return pl.pallas_call(
        ffn_results_kernel,
        grid=(1,),
        in_specs=[whole(*value.shape) for value in pair] + [hbm],
        out_specs=[hbm] * 3,
        out_shape=[jax.ShapeDtypeStruct(shape, f32) for shape in shapes],
        scratch_shapes=[pltpu.VMEM(total.shape, bf16)]
        + [pltpu.VMEM(shape, f32) for shape in shapes]
        + [pltpu.SemaphoreType.DMA((6,)), pltpu.SemaphoreType.DMA((6,))],
        compiler_params=params(58),
        cost_estimate=SHORT,
    )(*pair, total)


PLACES = (
    (0, 0, 640, 3, 0),
    (1, 0, 128, 3, 640),
    (1, 128, 384, 0, 0),
    (2, 0, 128, 1, 0),
    (2, 128, 128, 2, 0),
    (2, 256, 256, 0, 384),
    (3, 0, 128, 0, 640),
    (3, 128, 128, 1, 128),
    (3, 256, 128, 2, 128),
)


def count_of(ref_one, ref_two):
    total = None
    for ref in (ref_one, ref_two):
        for lane in (32, 96):
            part = jnp.sum(ref[:, 384 + lane : 385 + lane].astype(f32), axis=0, keepdims=True)
            total = part if total is None else total + part
    return total


def attention_results_kernel(bits, *refs):
    outs, rows_ref, tile = refs[8:12], refs[12], refs[13]
    count = count_of(refs[6], refs[7])
    scale = TOKENS / count
    for c, at, width, out, there in PLACES:
        for side in range(2):
            first = bits[c] * 384 if side == 0 else 384 - bits[c] * 384
            outs[out][pl.ds(pl.multiple_of(first, 384), 384), there : there + width] = (
                refs[2 * c + side][:, at : at + width].astype(f32) * scale
            )
    for side in range(2):
        first = bits[3] * 384 if side == 0 else 384 - bits[3] * 384
        tile[pl.ds(pl.multiple_of(first, 384), 384), :] = refs[6 + side][:, 384:512].astype(f32)
    lines = jnp.transpose(tile[...])
    rows_ref[0:1] = (lines[0:1] + lines[72:73]) * scale
    rows_ref[1:2] = (lines[16:17] + lines[88:89]) * scale
    squares = jnp.sum(lines[40:41] + lines[104:105], axis=1, keepdims=True)
    rows_ref[2:3] = jnp.broadcast_to(squares / count, (1, 768))
    rows_ref[3:4] = jnp.broadcast_to(scale, (1, 768))


def attention_results(bits, pairs):
    operands = [value for pair in pairs for value in pair]
    widths = (768, 256, 256, 768)
    return pl.pallas_call(
        attention_results_kernel,
        grid=(1,),
        in_specs=[SMEM] + [whole(*operand.shape) for operand in operands],
        out_specs=[whole(768, width) for width in widths] + [whole(8, 768)],
        out_shape=[jax.ShapeDtypeStruct((768, width), f32) for width in widths]
        + [jax.ShapeDtypeStruct((8, 768), f32)],
        scratch_shapes=[pltpu.VMEM((768, 128), f32)],
        compiler_params=params(),
        cost_estimate=SHORT,
    )(bits, *operands)


def local(
    tokens,
    w_query,
    key_projection_weight,
    value_projection_weight,
    w_out,
    w_gate,
    w_up,
    w_down,
    norm_attn,
    norm_ffn,
    doc_lengths,
    valid_mask,
    teacher,
):
    seq_count, row_count, width = tokens.shape
    rows = seq_count * row_count
    half = width // 2
    quarter = width // 4
    dp = lax.axis_index("dp")
    colour = (lax.axis_index("x") + lax.axis_index("y")) % 2
    y_index = lax.axis_index("y")
    group_index = lax.axis_index("x") * 2 + lax.axis_index("z_hi")

    def to_local(value):
        own = jnp.where(dp == 0, value[..., :half], value[..., half:])
        other = jnp.where(dp == 0, value[..., half:], value[..., :half])
        first = jnp.where(colour == 0, other[..., :quarter], other[..., quarter:])
        second = jnp.where(colour == 0, other[..., quarter:], other[..., :quarter])
        return jnp.concatenate([own, first, second], axis=-1)

    def other_half_of(first, second):
        return jnp.concatenate(
            [jnp.where(colour == 0, first, second), jnp.where(colour == 0, second, first)], axis=-1
        )

    def other_half(value):
        return other_half_of(value[..., half : half + quarter], value[..., half + quarter :])

    def from_local(value):
        own, other = value[..., :half], other_half(value)
        return jnp.concatenate(
            [jnp.where(dp == 0, own, other), jnp.where(dp == 0, other, own)], axis=-1
        )

    def two_ways(first, second):
        return z_move(first, 1), z_move(second, -1)

    def over_x(one, two):
        return ring_move(one, "x", 1), ring_move(two, "x", -1)

    def over_y(one, two):
        return ring_move(one, "y", 1), ring_move(two, "y", -1)

    def to_neighbours(value):
        return two_ways(value[:row_count], value[row_count:])

    gains = jnp.stack([norm_attn, norm_ffn])
    gains_other = swap(gains, "dp")
    gains_first = jnp.where(colour == 0, gains_other[:, :quarter], gains_other[:, quarter:])
    gains_second = jnp.where(colour == 0, gains_other[:, quarter:], gains_other[:, :quarter])
    gains_full = jnp.concatenate([gains, gains_first, gains_second], axis=1).astype(f32)
    gain_one, gain_two = gains_full[0], gains_full[1]

    kv = key_projection_weight.shape[1]
    ff = w_gate.shape[1]
    sent = copy_blocks(
        colour,
        [
            [
                (w_query, (quarter, half), lambda c, k=k: (k, 0), 0, 0),
                (key_projection_weight, (quarter, kv), lambda c, k=k: (k, 0), 0, half),
                (value_projection_weight, (quarter, kv), lambda c, k=k: (k, 0), 0, half + kv),
            ]
            for k in range(2)
        ],
        [(quarter, half + 2 * kv)] * 2,
        (gains_other,),
    )
    qkv_one, qkv_two = two_ways(*sent)
    mask_values = valid_mask.reshape(rows).astype(f32)
    blocks = [
        [
            (w_gate, (192, ff), lambda c, k=k: (2 * c + k, 0), 0, 0),
            (w_out, (192, quarter), lambda c, k=k: (2 * k, c), 0, ff),
            (w_out, (192, quarter), lambda c, k=k: (2 * k + 1, c), 0, ff + quarter),
        ]
        for k in range(2)
    ]
    first_z = two_ways(
        *copy_blocks(colour, blocks, [(192, ff + 2 * quarter)] * 2, (gains_other,))
    )

    residual_in = to_local(tokens.reshape(rows, width)).astype(f32)
    inverse_one = inverse_rms(residual_in)
    normed_one = (residual_in * inverse_one * gain_one).astype(bf16)
    normed_one_other = other_half(normed_one)
    projected = projection(
        normed_one[:, :half],
        normed_one_other,
        w_query,
        key_projection_weight,
        value_projection_weight,
        qkv_one,
        qkv_two,
    )
    mine = lax.all_to_all(projected, "y", 0, 0, tiled=True)
    queries, key_values = copy_blocks(
        colour,
        [
            [(mine, (512, 128), lambda c, k=k: (0, k), 0, 128 * (k - first)) for k in range(first, last)]
            for first, last in ((0, 3), (3, 5))
        ],
        [(512, 384), (512, 256)],
        (),
    )
    pieces = (group_move(key_values, 2), group_move(key_values, 1), key_values)
    blocks = [
        [(w_up, (192, ff), lambda c, k=k: (2 * c + k, 0), 0, 0)]
        + [
            (w_down, (192, quarter), lambda c, k=k, b=b: (5 * k + b, c), 0, ff + quarter * b)
            for b in range(5)
        ]
        for k in range(2)
    ]
    second_z = two_ways(*copy_blocks(colour, blocks, [(192, 2 * ff)] * 2, pieces[:2]))
    first = (first_z, over_x(*hold(first_z, pieces[0])))
    bounds = jnp.cumsum(lax.dynamic_index_in_dim(doc_lengths, y_index % 2, 0, keepdims=False))
    scalars = jnp.concatenate([(group_index * 512)[None], bounds]).astype(jnp.int32)
    attended_mine, logs = attention_forward(scalars, queries, pieces, ())
    attended_mine, *split = copy_blocks(
        colour,
        [[(attended_mine, attended_mine.shape, lambda c: (0, 0), 0, 0)]]
        + [[(v, (192, ff), lambda c, k=k: (0, k), 0, 0)] for k in range(2) for v in second_z],
        [attended_mine.shape] + [(192, ff)] * 4,
        (),
    )
    second = (second_z, over_x(*split[:2]), over_y(*split[2:]))
    returned = lax.all_to_all(attended_mine, "y", 0, 0, tiled=True)
    out_pieces = (*first[0], *first[1])
    attn_part, attended = out_projection(
        returned, w_out, out_pieces, (*second[1], *second[2])
    )
    early = to_neighbours(jnp.concatenate([normed_one_other, attended], axis=1))
    weights = (w_gate, w_up, w_down, first, second)
    hidden_state, normed_two, inverse_two, gate_pre, up_pre, activated, ffn_part = ffn_forward(
        residual_in, attn_part, swap(attn_part, "tensor"), gain_two, weights
    )
    middle = to_neighbours(jnp.concatenate([other_half(normed_two), activated], axis=1))

    final_state = hidden_state + branch_scale * core_sum(ffn_part)
    deviation = final_state - to_local(teacher.reshape(rows, width)).astype(f32)
    row_squares = mask_values * jnp.mean(deviation * deviation, axis=-1)
    grad_final = deviation * mask_values[:, None]
    branch_two = (branch_scale * grad_final).astype(bf16)
    grad_gate_pre, grad_up_pre, part = ffn_backward(branch_two, gate_pre, up_pre, weights, early)
    late = to_neighbours(
        jnp.concatenate([other_half(branch_two), grad_gate_pre, grad_up_pre], axis=1)
    )
    grad_normed_two = core_sum(part)

    grad_from_norm, gain_terms_two = norm_backward(
        hidden_state, inverse_two, gain_two, grad_normed_two
    )
    grad_hidden = grad_final + grad_from_norm
    branch_one = (branch_scale * grad_hidden).astype(bf16)
    grad_attended = out_backward(branch_one, w_out, out_pieces)
    branch_moved = to_neighbours(other_half(branch_one))
    grad_mine = lax.all_to_all(grad_attended, "y", 0, 0, tiled=True)
    grad_queries, grad_older, grad_newer, grad_own = attention_backward(
        scalars, queries, grad_mine, logs, pieces, ()
    )
    ffn_grads = ffn_gradients(
        normed_two, branch_two, grad_gate_pre, grad_up_pre, activated, middle, late, (grad_older,)
    )
    ffn_share = lax.psum_scatter(ffn_grads, ("x", "y"), scatter_dimension=0, tiled=True)
    older = group_move(grad_older, -2)
    newer = group_move(grad_newer, -1)
    grad_projected = lax.all_to_all(
        merge(grad_queries, grad_own, newer, older, branch_moved), "y", 0, 0, tiled=True
    )
    grad_projected = jnp.concatenate([grad_projected[:rows], grad_projected[rows:]], axis=1)
    last = to_neighbours(grad_projected)
    grad_normed_one = core_sum(
        projection_backward(
            colour,
            grad_projected,
            w_query,
            key_projection_weight,
            value_projection_weight,
            qkv_one,
            qkv_two,
        )
    )
    gradient_via_first_norm, gain_terms_one = norm_backward(
        residual_in, inverse_one, gain_one, grad_normed_one
    )
    grad_tokens = from_local(grad_hidden + gradient_via_first_norm)

    ones = jnp.ones((rows, 128), f32)

    def column_sums(terms):
        return lax.dot_general(
            terms, ones, (((0,), (0,)), ((), ())), precision=lax.Precision.HIGHEST
        )

    def on_rows(values):
        return jnp.pad(jnp.broadcast_to(values[:, None], (rows, 128)), ((0, half - rows), (0, 0)))

    entries = [
        column_sums(gain_terms_one[:, :half]),
        column_sums(other_half(gain_terms_one)),
        column_sums(gain_terms_two[:, :half]),
        column_sums(other_half(gain_terms_two)),
        on_rows(mask_values),
        on_rows(row_squares),
    ]
    slot = lax.broadcasted_iota(jnp.int32, (half, 128), 1) // 8
    tile = jnp.zeros((half, 128), f32)
    for k, entry in enumerate(entries):
        tile = jnp.where(slot == k, entry, tile)
    bits = jnp.stack([pair_bit(steps[0]) for steps in FIRST]).astype(jnp.int32)
    cut_rows = attention_gradients(
        bits,
        normed_one,
        grad_projected,
        attended,
        branch_one,
        *early,
        *last,
        *branch_moved,
        tile.astype(bf16),
    )
    channels = [
        add_moved(cut_rows[2 * k], cut_rows[2 * k + 1], FIRST[k][0]) for k in range(4)
    ]
    (ffn_share,) = hold([ffn_share], *channels)
    ffn_share = z_sum(ffn_share)
    channels = reduce_second(channels)
    pairs = [jnp.concatenate(channels[k : k + 2], axis=1) for k in (0, 2)]
    pairs = reduce_pairs(pairs, 0)
    (ffn_share,) = hold([ffn_share], *pairs)
    ffn_total_grads = lax.all_gather(ffn_share, ("x", "y"), axis=0, tiled=True)
    pairs = reduce_pairs(pairs, 1)
    pairs = reduce_rest(pairs, [c.shape[1] for c in channels])
    *attn_results, small = attention_results(bits, pairs)
    scale = small[3, 0]

    layer_out = from_local(final_state.astype(bf16)).reshape(seq_count, row_count, width)
    return (
        layer_out,
        small[2, 0],
        (grad_tokens * scale).reshape(seq_count, row_count, width),
        *attn_results,
        *ffn_results(pairs[3], ffn_total_grads),
        small[0],
        small[1],
    )


def solution(mesh):
    fine = Mesh(mesh.devices.reshape(2, 4, 2, 4, 2), ("dp", "x", "z_hi", "y", "tensor"))
    ctx = ("x", "z_hi", "y")
    return jax.shard_map(
        local,
        mesh=fine,
        in_specs=(
            P("dp", ctx, None),
            P("dp", "tensor"),
            P("dp", "tensor"),
            P("dp", "tensor"),
            P("tensor", "dp"),
            P("dp", "tensor"),
            P("dp", "tensor"),
            P("tensor", "dp"),
            P("dp"),
            P("dp"),
            P("dp", None),
            P("dp", ctx),
            P("dp", ctx, None),
        ),
        out_specs=(
            P("dp", ctx, None),
            P(),
            P("dp", ctx, None),
            P("dp", "tensor"),
            P("dp", "tensor"),
            P("dp", "tensor"),
            P("tensor", "dp"),
            P("dp", "tensor"),
            P("dp", "tensor"),
            P("tensor", "dp"),
            P("dp"),
            P("dp"),
        ),
        check_vma=False,
    )
```

```python
import math

import jax
import jax.numpy as jnp
from jax import lax
from jax.experimental import pallas as pl
from jax.experimental.pallas import tpu as pltpu
from jax.sharding import Mesh
from jax.sharding import PartitionSpec as P

HEAD = 64
WINDOW = 1024
BLOCK = 128
GROUP = 3
SPAN = WINDOW + BLOCK

branch_scale = 1.4 / math.sqrt(52.0)
norm_epsilon = 1e-05
masked_score = -1e30
scale_factor = 1.0 / math.sqrt(HEAD)
bf16 = jnp.bfloat16
f32 = jnp.float32


def dot(left, right):
    return jnp.dot(left, right, preferred_element_type=f32)


def dot_nt(left, right):
    return lax.dot_general(left, right, (((1,), (1,)), ((), ())), preferred_element_type=f32)


def dot_tn(left, right):
    return lax.dot_general(left, right, (((0,), (0,)), ((), ())), preferred_element_type=f32)


def z_move(value, distance):
    route = []
    for dp in range(2):
        for hi in range(2):
            z = (hi * 2 + dp + distance) % 4
            route.append((dp * 2 + hi, (z % 2) * 2 + z // 2))
    return lax.ppermute(value, ("dp", "z_hi"), route)


def ring_move(value, axis, distance):
    size = lax.axis_size(axis)
    return lax.ppermute(value, axis, [(i, (i + distance) % size) for i in range(size)])


def group_move(value, distance):
    return lax.ppermute(
        value, ("x", "z_hi"), [(i, i + distance) for i in range(8) if 0 <= i + distance < 8]
    )


def swap(value, axis):
    return lax.ppermute(value, axis, [(0, 1), (1, 0)])


PAIRS = {"even": ((0, 1), (1, 0), (2, 3), (3, 2)), "odd": ((0, 3), (3, 0), (1, 2), (2, 1))}


def pair_move(value, step):
    return lax.ppermute(value, step[0], PAIRS[step[1]])


def pair_bit(step):
    index = lax.axis_index(step[0])
    return (index // 2 + index) % 2 if step[1] == "even" else index // 2


def core_sum(part):
    return part.astype(f32) + swap(part, "tensor").astype(f32)


def z_sum(value):
    return (value.astype(f32) + swap(value, "z_hi").astype(f32)).astype(bf16)


def halves(value, step):
    bit = pair_bit(step)
    half = value.shape[0] // 2
    return (
        lax.dynamic_slice_in_dim(value, bit * half, half, 0),
        lax.dynamic_slice_in_dim(value, (1 - bit) * half, half, 0),
    )


def add_moved(keep, send, step):
    return (keep.astype(f32) + pair_move(send, step).astype(f32)).astype(bf16)


def halve(value, step):
    return add_moved(*halves(value, step), step)


def double(value, step):
    other = pair_move(value, step)
    return jnp.where(
        pair_bit(step) == 0,
        jnp.concatenate([value, other], axis=0),
        jnp.concatenate([other, value], axis=0),
    )


FIRST = (
    (("x", "even"), ("x", "odd")),
    (("x", "odd"), ("x", "even")),
    (("y", "even"), ("y", "odd")),
    (("y", "odd"), ("y", "even")),
)
SECOND = ((("y", "even"), ("y", "odd")), (("x", "even"), ("x", "odd")))


def reduce_second(channels):
    return [halve(c, FIRST[i][1]) for i, c in enumerate(channels)]


def reduce_pairs(pairs, level):
    return [halve(c, SECOND[i][level]) for i, c in enumerate(pairs)]


def reduce_rest(pairs, widths):
    at = widths[0] + widths[1]
    rows = pairs[0].shape[0]
    (total,) = copy_blocks(
        jnp.zeros((), jnp.int32),
        [
            [
                (pair, pair.shape, lambda c: (0, 0), 0, first)
                for pair, first in zip(pairs, (0, at))
            ]
        ],
        [(rows, sum(widths))],
        (),
    )
    tile = total[:, -128:]
    beside = z_move(tile, 1).astype(f32) + z_move(tile, -1).astype(f32)
    beside = jnp.concatenate([beside[:, 64:], beside[:, :64]], axis=1).astype(bf16)
    total = z_sum(total)
    total = jnp.concatenate([total[:, :-128], total[:, -128:] + beside], axis=1)
    pairs = [total[:, :at], total[:, at:]]
    for level in (1, 0):
        pairs = [double(c, SECOND[i][level]) for i, c in enumerate(pairs)]
    channels = [
        pairs[0][:, : widths[0]],
        pairs[0][:, widths[0] :],
        pairs[1][:, : widths[2]],
        pairs[1][:, widths[2] :],
    ]
    channels = [double(c, FIRST[i][1]) for i, c in enumerate(channels)]
    return [(c, pair_move(c, FIRST[i][0])) for i, c in enumerate(channels)]


def inverse_rms(source):
    return lax.rsqrt(jnp.mean(source * source, axis=-1, keepdims=True) + norm_epsilon)


def norm_backward(source, inverse, gain_vec, grad_normed):
    weighted = grad_normed * gain_vec
    grad_source = inverse * weighted - source * (inverse * inverse * inverse) * jnp.mean(
        source * weighted, axis=-1, keepdims=True
    )
    return (grad_source, grad_normed * source * inverse)


def allowed_keys(scalars, r):
    shape = (BLOCK, SPAN)
    query_pos = scalars[0] + r * BLOCK + lax.broadcasted_iota(jnp.int32, shape, 0)
    key_pos = scalars[0] + r * BLOCK - WINDOW + lax.broadcasted_iota(jnp.int32, shape, 1)
    lowest = jnp.maximum(query_pos - (WINDOW - 1), 0)
    for d in range(1, 5):
        lowest = jnp.maximum(lowest, jnp.where(query_pos >= scalars[d], scalars[d], 0))
    allowed = (key_pos >= lowest) & (key_pos <= query_pos)
    return jnp.concatenate([allowed] * (2 * GROUP), axis=0)


def low_half():
    return lax.broadcasted_iota(jnp.int32, (BLOCK, 128), 1) < HEAD


def head_rows(ref):
    parts = []
    for h in range(2 * GROUP):
        g = h // GROUP
        lanes = low_half() if g == 0 else jnp.logical_not(low_half())
        columns = ref[:, h // 2 * 128 : h // 2 * 128 + 128].astype(f32)
        if h % 2 != g:
            columns = pltpu.roll(columns, HEAD, 1)
        parts.append(jnp.where(lanes, columns, 0.0).astype(bf16))
    return jnp.concatenate(parts, axis=0)


def put_heads(ref, results):
    sides = []
    for h in range(2 * GROUP):
        columns = results[h * BLOCK : (h + 1) * BLOCK]
        sides.append(pltpu.roll(columns, HEAD, 1) if h % 2 != h // GROUP else columns)
    for t in range(GROUP):
        ref[:, t * 128 : (t + 1) * 128] = jnp.where(
            low_half(), sides[2 * t], sides[2 * t + 1]
        ).astype(ref.dtype)


def fill_window(window, older, newer, own):
    window[0:512] = older[...]
    window[512:1024] = newer[...]
    window[1024:1536] = own[...]


def attention_forward_kernel(scalars, q_ref, older, newer, own, *rest):
    out_ref, log_ref, window = rest[-3:]
    r = pl.program_id(0)

    @pl.when(r == 0)
    def _():
        fill_window(window, older, newer, own)

    span = pl.ds(pl.multiple_of(r * BLOCK, BLOCK), SPAN)
    keys = window[span, 0:128]
    values = window[span, 128:256]
    allowed = allowed_keys(scalars, r)
    scores = jnp.where(allowed, dot_nt(head_rows(q_ref), keys) * scale_factor, masked_score)
    top = jnp.max(scores, axis=-1, keepdims=True)
    weights = jnp.exp(scores - top)
    total = jnp.sum(weights, axis=-1, keepdims=True)
    log_ref[0] = top + jnp.log(total)
    put_heads(out_ref, dot((weights * (1.0 / total)).astype(bf16), values))


def attention_backward_kernel(scalars, q_ref, g_ref, log_ref, older, newer, own, *rest):
    dq_ref, older_ref, newer_ref, own_ref, window, sums = rest[-6:]
    r = pl.program_id(0)

    @pl.when(r == 0)
    def _():
        fill_window(window, older, newer, own)
        sums[...] = jnp.zeros_like(sums)

    span = pl.ds(pl.multiple_of(r * BLOCK, BLOCK), SPAN)
    keys = window[span, 0:128]
    values = window[span, 128:256]
    allowed = allowed_keys(scalars, r)
    q6 = head_rows(q_ref)
    g6 = head_rows(g_ref)
    scores = jnp.where(allowed, dot_nt(q6, keys) * scale_factor, masked_score)
    probs = jnp.exp(scores - log_ref[0])
    grad_probs = dot_nt(g6, values)
    inner = jnp.sum(grad_probs * probs, axis=-1, keepdims=True)
    grad_scores = (probs * (grad_probs - inner)).astype(bf16)
    put_heads(dq_ref, dot(grad_scores, keys) * scale_factor)
    sums[span, 0:128] += dot_tn(grad_scores, q6)
    sums[span, 128:256] += dot_tn(probs.astype(bf16), g6)

    @pl.when(r == 3)
    def _():
        for part, ref in enumerate((older_ref, newer_ref, own_ref)):
            rows = slice(part * 512, (part + 1) * 512)
            ref[:, 0:128] = (sums[rows, 0:128] * scale_factor).astype(ref.dtype)
            ref[:, 128:256] = sums[rows, 128:256].astype(ref.dtype)


SMEM = pl.BlockSpec(memory_space=pltpu.SMEM)
UNREAD = pl.BlockSpec(memory_space=pl.ANY)
SHORT = pl.CostEstimate(flops=1000, bytes_accessed=1000, transcendentals=0)


def whole(*shape):
    return pl.BlockSpec(shape, lambda i: (0,) * len(shape))


def params(mebibytes=24):
    return pltpu.CompilerParams(vmem_limit_bytes=mebibytes * 1024 * 1024)


def copy_blocks(index, outputs, shapes, held):
    blocks = [block for output in outputs for block in output]

    def kernel(index_ref, *refs):
        outs = refs[len(blocks) + len(held) :]
        at = 0
        for output, out in zip(outputs, outs):
            for _, shape, _, row, column in output:
                out[row : row + shape[0], column : column + shape[1]] = refs[at][...]
                at += 1

    return pl.pallas_call(
        kernel,
        grid_spec=pltpu.PrefetchScalarGridSpec(
            num_scalar_prefetch=1,
            grid=(1,),
            in_specs=[
                pl.BlockSpec(block[1], lambda i, ref, place=block[2]: place(ref[0]))
                for block in blocks
            ]
            + [UNREAD] * len(held),
            out_specs=[pl.BlockSpec(shape, lambda i, ref: (0, 0)) for shape in shapes],
        ),
        out_shape=[
            jax.ShapeDtypeStruct(shape, output[0][0].dtype)
            for shape, output in zip(shapes, outputs)
        ],
        compiler_params=params(20),
        cost_estimate=SHORT,
    )(index.reshape(1), *[block[0] for block in blocks], *held)


def hold(values, *held):
    return copy_blocks(
        jnp.zeros((), jnp.int32),
        [[(v, v.shape, lambda c: (0, 0), 0, 0)] for v in values],
        [v.shape for v in values],
        held,
    )


def attention_forward(scalars, queries, pieces, held):
    return pl.pallas_call(
        attention_forward_kernel,
        grid=(4,),
        in_specs=[SMEM, pl.BlockSpec((BLOCK, 384), lambda i: (i, 0))]
        + [whole(512, 256)] * 3
        + [UNREAD] * len(held),
        out_specs=(
            pl.BlockSpec((BLOCK, 384), lambda i: (i, 0)),
            pl.BlockSpec((1, 2 * GROUP * BLOCK, 1), lambda i: (i, 0, 0)),
        ),
        out_shape=(
            jax.ShapeDtypeStruct((512, 384), bf16),
            jax.ShapeDtypeStruct((4, 2 * GROUP * BLOCK, 1), f32),
        ),
        scratch_shapes=[pltpu.VMEM((1536, 256), bf16)],
        compiler_params=params(32),
        cost_estimate=SHORT,
    )(scalars, queries, *pieces, *held)


def attention_backward(scalars, queries, grads, logs, pieces, held):
    return pl.pallas_call(
        attention_backward_kernel,
        grid=(4,),
        in_specs=[
            SMEM,
            pl.BlockSpec((BLOCK, 384), lambda i: (i, 0)),
            pl.BlockSpec((BLOCK, 384), lambda i: (i, 0)),
            pl.BlockSpec((1, 2 * GROUP * BLOCK, 1), lambda i: (i, 0, 0)),
        ]
        + [whole(512, 256)] * 3
        + [UNREAD] * len(held),
        out_specs=(
            pl.BlockSpec((BLOCK, 384), lambda i: (i, 0)),
            whole(512, 256),
            whole(512, 256),
            whole(512, 256),
        ),
        out_shape=(
            jax.ShapeDtypeStruct((512, 384), bf16),
            jax.ShapeDtypeStruct((512, 256), bf16),
            jax.ShapeDtypeStruct((512, 256), bf16),
            jax.ShapeDtypeStruct((512, 256), f32),
        ),
        scratch_shapes=[pltpu.VMEM((1536, 256), bf16), pltpu.VMEM((1536, 256), f32)],
        compiler_params=params(32),
        cost_estimate=SHORT,
    )(scalars, queries, grads, logs, *pieces, *held)


TILE = 384
TOKENS = 16384
CHUNKS = ((0, 1024), (1024, 1920))


def weight_copies(refs, gate, up, down, sems):
    copies = {"gate": [], "up": [], "down": []}

    def add(group, source, target):
        count = sum(len(entries) for entries in copies.values())
        copies[group].append(pltpu.make_async_copy(source, target, sems.at[count]))

    for group, target, at in (("gate", gate, 0), ("up", up, 5)):
        add(group, refs[at], target.at[pl.ds(0, 768), :])
        for k in range(4):
            add(
                group,
                refs[at + 1 + k].at[:, pl.ds(0, 1920)],
                target.at[pl.ds(768 + 192 * k, 192), :],
            )
    add("down", refs[10], down.at[:, pl.ds(0, 768)])
    for side in range(2):
        for b in range(5):
            rows = pl.ds(960 * side + 192 * b, 192)
            add(
                "down",
                refs[6 + side].at[:, pl.ds(1920 + 384 * b, 384)],
                down.at[rows, pl.ds(768, 384)],
            )
            add(
                "down",
                refs[11 + side].at[:, pl.ds(384 * b, 384)],
                down.at[rows, pl.ds(1152, 384)],
            )
    return copies


def weight_operands(w_gate, w_up, w_down, one, two):
    return [w_gate, *one[0], *one[1], w_up, *two[0], *two[1], w_down, *two[2]]


WEIGHT_SCRATCH = [
    pltpu.VMEM((1536, 1920), bf16),
    pltpu.VMEM((1536, 1920), bf16),
    pltpu.VMEM((1920, 1536), bf16),
    pltpu.SemaphoreType.DMA((31,)),
]


def start_all(copies, order):
    for group in order:
        for copy in copies[group]:
            copy.start()


def wait_all(copies):
    for copy in copies:
        copy.wait()


def ffn_forward_kernel(x_ref, own, moved, gain, *refs):
    weights = refs[:13]
    h_ref, n_ref, r_ref, g_ref, u_ref, a_ref, out_ref, gate, up, down, sems = refs[13:]
    copies = weight_copies(weights, gate, up, down, sems)
    start_all(copies, ("gate", "up", "down"))
    hidden = x_ref[...] + branch_scale * (own[...].astype(f32) + moved[...].astype(f32))
    inverse = inverse_rms(hidden)
    h_ref[...] = hidden
    r_ref[...] = inverse
    n_ref[...] = (hidden * inverse * gain[...]).astype(bf16)
    wait_all(copies["gate"])
    for a, b in CHUNKS:
        g_ref[:, a:b] = dot(n_ref[...], gate[:, a:b])
    wait_all(copies["up"])
    for a, b in CHUNKS:
        up_pre = dot(n_ref[...], up[:, a:b])
        u_ref[:, a:b] = up_pre
        gate_pre = g_ref[:, a:b]
        a_ref[:, a:b] = (gate_pre * jax.nn.sigmoid(gate_pre) * up_pre).astype(bf16)
    wait_all(copies["down"])
    out_ref[...] = dot(a_ref[...], down[...]).astype(bf16)


def ffn_backward_kernel(b_ref, g_ref, u_ref, *refs):
    weights = refs[:13]
    gg_ref, gu_ref, out_ref, gate, up, down, sems = refs[-7:]
    copies = weight_copies(weights, gate, up, down, sems)
    start_all(copies, ("down", "gate", "up"))
    wait_all(copies["down"])
    for a, b in CHUNKS:
        grad = dot_nt(b_ref[...], down[a:b, :]).astype(bf16).astype(f32)
        gate_pre, up_pre = g_ref[:, a:b], u_ref[:, a:b]
        sigmoid = jax.nn.sigmoid(gate_pre)
        gg_ref[:, a:b] = (
            grad * up_pre * sigmoid * (1.0 + gate_pre * (1.0 - sigmoid))
        ).astype(bf16)
        gu_ref[:, a:b] = (grad * gate_pre * sigmoid).astype(bf16)
    wait_all(copies["gate"])
    part = dot_nt(gg_ref[...], gate[...])
    wait_all(copies["up"])
    out_ref[...] = (part + dot_nt(gu_ref[...], up[...])).astype(bf16)


def ffn_forward(residual, own, moved, gain, weights):
    rows, width = residual.shape
    operands = weight_operands(*weights)
    hidden = weights[2].shape[0]
    shapes = [
        ((rows, width), f32),
        ((rows, width), bf16),
        ((rows, 1), f32),
        ((rows, hidden), f32),
        ((rows, hidden), f32),
        ((rows, hidden), bf16),
        ((rows, width), bf16),
    ]
    return pl.pallas_call(
        ffn_forward_kernel,
        grid=(1,),
        in_specs=[whole(rows, width)] * 3 + [whole(1, width)] + [UNREAD] * len(operands),
        out_specs=[whole(*shape) for shape, _ in shapes],
        out_shape=[jax.ShapeDtypeStruct(*entry) for entry in shapes],
        scratch_shapes=WEIGHT_SCRATCH,
        compiler_params=params(48),
        cost_estimate=SHORT,
    )(residual, own, moved, gain.reshape(1, width), *operands)


def ffn_backward(branch, gate_pre, up_pre, weights, held):
    rows, width = branch.shape
    operands = weight_operands(*weights)
    hidden = weights[2].shape[0]
    shapes = [((rows, hidden), bf16), ((rows, hidden), bf16), ((rows, width), bf16)]
    return pl.pallas_call(
        ffn_backward_kernel,
        grid=(1,),
        in_specs=[whole(rows, width)]
        + [whole(rows, hidden)] * 2
        + [UNREAD] * (len(operands) + len(held)),
        out_specs=[whole(*shape) for shape, _ in shapes],
        out_shape=[jax.ShapeDtypeStruct(*entry) for entry in shapes],
        scratch_shapes=WEIGHT_SCRATCH,
        compiler_params=params(44),
        cost_estimate=SHORT,
    )(branch, gate_pre, up_pre, *operands, *held)


def hidden_tile(rows):
    return pl.BlockSpec((rows, TILE), lambda i: (0, i))


def projection_kernel(n_own, n_other, wq, wk, wv, one, two, *rest):
    out_ref = rest[-1]
    own = n_own[...]
    first, second = n_other[:, :384], n_other[:, 384:]
    rows = own.shape[0]
    for p in range(2):
        place = pl.ds(p * rows, rows)
        q_at, kv_at = slice(p * 384, p * 384 + 384), slice(p * 128, p * 128 + 128)
        for weight, own_at, at, out_at in (
            (wq, q_at, p * 384, slice(0, 384)),
            (wk, kv_at, 768 + p * 128, slice(384, 512)),
            (wv, kv_at, 1024 + p * 128, slice(512, 640)),
        ):
            there = slice(at, at + out_at.stop - out_at.start)
            out_ref[place, out_at] = (
                dot(own, weight[:, own_at])
                + dot(first, one[:, there])
                + dot(second, two[:, there])
            ).astype(bf16)


def projection_backward_kernel(colour, g_ref, wq, wk, wv, one, two, out_ref):
    grad = jnp.concatenate(
        [
            g_ref[:, a:b]
            for a, b in ((0, 384), (640, 1024), (384, 512), (1024, 1152), (512, 640), (1152, 1280))
        ],
        axis=1,
    )
    out_ref[:, 0:768] = (
        dot_nt(grad[:, 0:768], wq[...])
        + dot_nt(grad[:, 768:1024], wk[...])
        + dot_nt(grad[:, 1024:1280], wv[...])
    ).astype(bf16)
    first = dot_nt(grad, one[...]).astype(bf16)
    second = dot_nt(grad, two[...]).astype(bf16)

    @pl.when(colour[0] == 0)
    def _():
        out_ref[:, 768:1152] = first
        out_ref[:, 1152:1536] = second

    @pl.when(colour[0] != 0)
    def _():
        out_ref[:, 768:1152] = second
        out_ref[:, 1152:1536] = first


def projection_backward(colour, *operands):
    rows = operands[0].shape[0]
    return pl.pallas_call(
        projection_backward_kernel,
        grid=(1,),
        in_specs=[SMEM] + [whole(*operand.shape) for operand in operands],
        out_specs=whole(rows, 1536),
        out_shape=jax.ShapeDtypeStruct((rows, 1536), bf16),
        compiler_params=params(),
        cost_estimate=SHORT,
    )(colour.reshape(1), *operands)


def out_blocks(pieces):
    operands = [piece for piece in pieces for _ in range(2)]
    specs = [pl.BlockSpec((192, 384), lambda i, k=k: (0, k)) for k in (5, 6)] * 4
    return operands, specs


def out_columns(refs):
    return jnp.concatenate([ref[...] for ref in refs], axis=0)


def out_projection_kernel(back_ref, w_ref, *refs):
    part_ref, attended_ref = refs[-2:]
    rows = attended_ref.shape[0]
    attended = jnp.concatenate([back_ref[0:rows], back_ref[rows : 2 * rows]], axis=1)
    attended_ref[...] = attended
    part_ref[:, 0:768] = dot(attended, w_ref[...]).astype(bf16)
    part_ref[:, 768:1152] = dot(attended, out_columns(refs[0:4])).astype(bf16)
    part_ref[:, 1152:1536] = dot(attended, out_columns(refs[4:8])).astype(bf16)


def out_projection(back, w_out, pieces, held):
    rows = back.shape[0] // 2
    operands, specs = out_blocks(pieces)
    return pl.pallas_call(
        out_projection_kernel,
        grid=(1,),
        in_specs=[whole(*back.shape), whole(*w_out.shape)] + specs + [UNREAD] * len(held),
        out_specs=(whole(rows, 1536), whole(rows, 768)),
        out_shape=(
            jax.ShapeDtypeStruct((rows, 1536), bf16),
            jax.ShapeDtypeStruct((rows, 768), bf16),
        ),
        compiler_params=params(),
        cost_estimate=SHORT,
    )(back, w_out, *operands, *held)


def out_backward_kernel(b_ref, w_ref, *refs):
    out_ref = refs[-1]
    rows = b_ref.shape[0]
    grad = (
        dot_nt(b_ref[:, 0:768], w_ref[...])
        + dot_nt(b_ref[:, 768:1152], out_columns(refs[0:4]))
        + dot_nt(b_ref[:, 1152:1536], out_columns(refs[4:8]))
    ).astype(bf16)
    out_ref[0:rows] = grad[:, 0:384]
    out_ref[rows : 2 * rows] = grad[:, 384:768]


def out_backward(branch, w_out, pieces):
    rows = branch.shape[0]
    operands, specs = out_blocks(pieces)
    return pl.pallas_call(
        out_backward_kernel,
        grid=(1,),
        in_specs=[whole(*branch.shape), whole(*w_out.shape)] + specs,
        out_specs=whole(2 * rows, 384),
        out_shape=jax.ShapeDtypeStruct((2 * rows, 384), bf16),
        compiler_params=params(),
        cost_estimate=SHORT,
    )(branch, w_out, *operands)


def projection(*operands):
    rows = operands[0].shape[0]
    return pl.pallas_call(
        projection_kernel,
        in_specs=[pl.BlockSpec(memory_space=pltpu.VMEM)] * 7 + [UNREAD] * (len(operands) - 7),
        out_shape=jax.ShapeDtypeStruct((2 * rows, 640), bf16),
        compiler_params=params(),
        cost_estimate=SHORT,
    )(*operands)


def merge_kernel(q_ref, own, newer, older, *rest):
    out_ref = rest[-1]
    out_ref[:, 0:384] = q_ref[...]
    out_ref[:, 384:640] = (
        own[...] + newer[...].astype(f32) + older[...].astype(f32)
    ).astype(bf16)


def merge(grad_queries, own, newer, older, held):
    operands = (grad_queries, own, newer, older)
    return pl.pallas_call(
        merge_kernel,
        grid=(1,),
        in_specs=[whole(*operand.shape) for operand in operands] + [UNREAD] * len(held),
        out_specs=whole(512, 640),
        out_shape=jax.ShapeDtypeStruct((512, 640), bf16),
        compiler_params=params(),
        cost_estimate=SHORT,
    )(*operands, *held)


def ffn_gradients_kernel(normed, branch, gate, up, act, m_one, m_two, l_one, l_two, *rest):
    out_ref, n_all, b_all, gate_all, up_all, act_all, total, in_sems, out_sems = rest[-9:]
    rows, width, hidden = 256, 768, 1920
    copies = {}
    for name, own, received, at, target in (
        ("normed", normed, (m_one, m_two), 0, n_all),
        ("gate", gate, (l_one, l_two), width, gate_all),
        ("up", up, (l_one, l_two), width + hidden, up_all),
        ("act", act, (m_one, m_two), width, act_all),
        ("branch", branch, (l_one, l_two), 0, b_all),
    ):
        columns = target.shape[1]
        parts = [(own.at[:, pl.ds(0, columns)], target.at[pl.ds(0, rows), :])]
        for k, part in enumerate(received):
            parts.append(
                (
                    part.at[:, pl.ds(at, columns)],
                    target.at[pl.ds(rows + 128 * k, 128), :],
                )
            )
        base = 3 * len(copies)
        copies[name] = [
            pltpu.make_async_copy(source, place, in_sems.at[base + k])
            for k, (source, place) in enumerate(parts)
        ]
        for copy in copies[name]:
            copy.start()

    def send(k):
        place = pl.ds(k * width, width)
        copy = pltpu.make_async_copy(total.at[place, :], out_ref.at[place, :], out_sems.at[k])
        copy.start()
        return copy

    wait_all(copies["normed"])
    wait_all(copies["gate"])
    for a, b in CHUNKS:
        total[0:width, a:b] = dot_tn(n_all[...], gate_all[:, a:b]).astype(bf16)
    sent = [send(0)]
    wait_all(copies["up"])
    for a, b in CHUNKS:
        total[width : 2 * width, a:b] = dot_tn(n_all[...], up_all[:, a:b]).astype(bf16)
    sent.append(send(1))
    wait_all(copies["act"])
    wait_all(copies["branch"])
    for a, b in CHUNKS:
        down = dot_tn(act_all[:, a:b], b_all[...]).astype(bf16)
        for r in range(width // 128):
            for c in range((b - a) // 128):
                total[
                    2 * width + r * 128 : 2 * width + r * 128 + 128, a + c * 128 : a + c * 128 + 128
                ] = down[c * 128 : c * 128 + 128, r * 128 : r * 128 + 128]
    sent.append(send(2))
    wait_all(sent)


def ffn_gradients(normed, branch, gate, up, act, middle, late, held):
    operands = (normed, branch, gate, up, act, *middle, *late, *held)
    return pl.pallas_call(
        ffn_gradients_kernel,
        grid=(1,),
        in_specs=[UNREAD] * len(operands),
        out_specs=pl.BlockSpec(memory_space=pltpu.HBM),
        out_shape=jax.ShapeDtypeStruct((2304, 1920), bf16),
        scratch_shapes=[pltpu.VMEM((512, 768), bf16)] * 2
        + [pltpu.VMEM((512, 1920), bf16)] * 3
        + [
            pltpu.VMEM((2304, 1920), bf16),
            pltpu.SemaphoreType.DMA((15,)),
            pltpu.SemaphoreType.DMA((3,)),
        ],
        compiler_params=params(40),
        cost_estimate=SHORT,
    )(*operands)


CHANNELS = (0, 640, 1152, 1664, 2176)


def attention_gradients_kernel(bits, *refs):
    normed, projected, attended, branch = refs[0:4]
    early, last, branch_moved = refs[4:6], refs[6:8], refs[8:10]
    outs, total = refs[11:-1], refs[-1]
    total[:, 2048:2176] = refs[10][...]

    def rows_of(own, received, at, width):
        parts = [own[:, :width]] + [ref[:, at : at + width] for ref in received]
        return jnp.concatenate(parts, axis=0)

    total[:, 0:768] = dot_tn(
        rows_of(attended, early, 768, 768), rows_of(branch, branch_moved, 0, 768)
    ).astype(bf16)
    total[:, 768:2048] = dot_tn(
        rows_of(normed, early, 0, 768), rows_of(projected, last, 0, 1280)
    ).astype(bf16)
    for c in range(4):
        columns = slice(CHANNELS[c], CHANNELS[c + 1])
        keep = pl.multiple_of(bits[c] * 384, 384)
        send = pl.multiple_of(384 - bits[c] * 384, 384)
        outs[2 * c][...] = total[pl.ds(keep, 384), columns]
        outs[2 * c + 1][...] = total[pl.ds(send, 384), columns]


def attention_gradients(bits, *operands):
    widths = [b - a for a, b in zip(CHANNELS[:-1], CHANNELS[1:]) for _ in range(2)]
    return list(
        pl.pallas_call(
            attention_gradients_kernel,
            grid=(1,),
            in_specs=[SMEM] + [whole(*operand.shape) for operand in operands],
            out_specs=[whole(384, w) for w in widths],
            out_shape=[jax.ShapeDtypeStruct((384, w), bf16) for w in widths],
            scratch_shapes=[pltpu.VMEM((768, 2176), bf16)],
            compiler_params=params(),
            cost_estimate=SHORT,
        )(bits, *operands)
    )


def ffn_results_kernel(one, two, total_hbm, *refs):
    outs, total, f_gate, f_up, f_down, in_sems, out_sems = refs[0:3], *refs[3:]
    width, hidden = 768, 1920
    targets = (f_gate, f_up, f_down)
    chunks = []
    for m in range(2):
        for r in range(2):
            place = pl.ds(m * width + r * 384, 384)
            chunks.append((m, r, (place, pl.ds(0, hidden)), (pl.ds(r * 384, 384), pl.ds(0, hidden))))
    for r, (a, b) in enumerate(CHUNKS):
        place = (pl.ds(2 * width, width), pl.ds(a, b - a))
        chunks.append((2, r, place, (pl.ds(a, b - a), pl.ds(0, width))))
    arriving, leaving = [], []
    for k, (_, _, place, _) in enumerate(chunks):
        arriving.append(
            pltpu.make_async_copy(total_hbm.at[place], total.at[place], in_sems.at[k])
        )
        arriving[-1].start()
    scale = TOKENS / count_of(one, two)
    for k, (m, r, _, there) in enumerate(chunks):
        arriving[k].wait()
        if m < 2:
            rows = slice(r * 384, r * 384 + 384)
            source = slice(m * width + r * 384, m * width + r * 384 + 384)
            targets[m][rows] = total[source].astype(f32) * scale
        else:
            a, b = CHUNKS[r]
            for p in range(a // 128, b // 128):
                for q in range(width // 128):
                    f_down[p * 128 : p * 128 + 128, q * 128 : q * 128 + 128] = (
                        total[
                            2 * width + q * 128 : 2 * width + q * 128 + 128,
                            p * 128 : p * 128 + 128,
                        ].astype(f32)
                        * scale
                    )
        leaving.append(
            pltpu.make_async_copy(targets[m].at[there], outs[m].at[there], out_sems.at[k])
        )
        leaving[-1].start()
    wait_all(leaving)


def ffn_results(pair, total):
    width, hidden = total.shape[0] // 3, total.shape[1]
    shapes = ((width, hidden), (width, hidden), (hidden, width))
    hbm = pl.BlockSpec(memory_space=pltpu.HBM)
    return pl.pallas_call(
        ffn_results_kernel,
        grid=(1,),
        in_specs=[whole(*value.shape) for value in pair] + [hbm],
        out_specs=[hbm] * 3,
        out_shape=[jax.ShapeDtypeStruct(shape, f32) for shape in shapes],
        scratch_shapes=[pltpu.VMEM(total.shape, bf16)]
        + [pltpu.VMEM(shape, f32) for shape in shapes]
        + [pltpu.SemaphoreType.DMA((6,)), pltpu.SemaphoreType.DMA((6,))],
        compiler_params=params(58),
        cost_estimate=SHORT,
    )(*pair, total)


PLACES = (
    (0, 0, 640, 3, 0),
    (1, 0, 128, 3, 640),
    (1, 128, 384, 0, 0),
    (2, 0, 128, 1, 0),
    (2, 128, 128, 2, 0),
    (2, 256, 256, 0, 384),
    (3, 0, 128, 0, 640),
    (3, 128, 128, 1, 128),
    (3, 256, 128, 2, 128),
)


def count_of(ref_one, ref_two):
    total = None
    for ref in (ref_one, ref_two):
        for lane in (32, 96):
            part = jnp.sum(ref[:, 384 + lane : 385 + lane].astype(f32), axis=0, keepdims=True)
            total = part if total is None else total + part
    return total


def attention_results_kernel(bits, *refs):
    outs, rows_ref, tile = refs[8:12], refs[12], refs[13]
    count = count_of(refs[6], refs[7])
    scale = TOKENS / count
    for c, at, width, out, there in PLACES:
        for side in range(2):
            first = bits[c] * 384 if side == 0 else 384 - bits[c] * 384
            outs[out][pl.ds(pl.multiple_of(first, 384), 384), there : there + width] = (
                refs[2 * c + side][:, at : at + width].astype(f32) * scale
            )
    for side in range(2):
        first = bits[3] * 384 if side == 0 else 384 - bits[3] * 384
        tile[pl.ds(pl.multiple_of(first, 384), 384), :] = refs[6 + side][:, 384:512].astype(f32)
    lines = jnp.transpose(tile[...])
    rows_ref[0:1] = (lines[0:1] + lines[72:73]) * scale
    rows_ref[1:2] = (lines[16:17] + lines[88:89]) * scale
    squares = jnp.sum(lines[40:41] + lines[104:105], axis=1, keepdims=True)
    rows_ref[2:3] = jnp.broadcast_to(squares / count, (1, 768))
    rows_ref[3:4] = jnp.broadcast_to(scale, (1, 768))


def attention_results(bits, pairs):
    operands = [value for pair in pairs for value in pair]
    widths = (768, 256, 256, 768)
    return pl.pallas_call(
        attention_results_kernel,
        grid=(1,),
        in_specs=[SMEM] + [whole(*operand.shape) for operand in operands],
        out_specs=[whole(768, width) for width in widths] + [whole(8, 768)],
        out_shape=[jax.ShapeDtypeStruct((768, width), f32) for width in widths]
        + [jax.ShapeDtypeStruct((8, 768), f32)],
        scratch_shapes=[pltpu.VMEM((768, 128), f32)],
        compiler_params=params(),
        cost_estimate=SHORT,
    )(bits, *operands)


def local(
    tokens,
    w_query,
    key_projection_weight,
    value_projection_weight,
    w_out,
    w_gate,
    w_up,
    w_down,
    norm_attn,
    norm_ffn,
    doc_lengths,
    valid_mask,
    teacher,
):
    seq_count, row_count, width = tokens.shape
    rows = seq_count * row_count
    half = width // 2
    quarter = width // 4
    dp = lax.axis_index("dp")
    colour = (lax.axis_index("x") + lax.axis_index("y")) % 2
    y_index = lax.axis_index("y")
    group_index = lax.axis_index("x") * 2 + lax.axis_index("z_hi")

    def to_local(value):
        own = jnp.where(dp == 0, value[..., :half], value[..., half:])
        other = jnp.where(dp == 0, value[..., half:], value[..., :half])
        first = jnp.where(colour == 0, other[..., :quarter], other[..., quarter:])
        second = jnp.where(colour == 0, other[..., quarter:], other[..., :quarter])
        return jnp.concatenate([own, first, second], axis=-1)

    def other_half_of(first, second):
        return jnp.concatenate(
            [jnp.where(colour == 0, first, second), jnp.where(colour == 0, second, first)], axis=-1
        )

    def other_half(value):
        return other_half_of(value[..., half : half + quarter], value[..., half + quarter :])

    def from_local(value):
        own, other = value[..., :half], other_half(value)
        return jnp.concatenate(
            [jnp.where(dp == 0, own, other), jnp.where(dp == 0, other, own)], axis=-1
        )

    def two_ways(first, second):
        return z_move(first, 1), z_move(second, -1)

    def over_x(one, two):
        return ring_move(one, "x", 1), ring_move(two, "x", -1)

    def over_y(one, two):
        return ring_move(one, "y", 1), ring_move(two, "y", -1)

    def to_neighbours(value):
        return two_ways(value[:row_count], value[row_count:])

    gains = jnp.stack([norm_attn, norm_ffn])
    gains_other = swap(gains, "dp")
    gains_first = jnp.where(colour == 0, gains_other[:, :quarter], gains_other[:, quarter:])
    gains_second = jnp.where(colour == 0, gains_other[:, quarter:], gains_other[:, :quarter])
    gains_full = jnp.concatenate([gains, gains_first, gains_second], axis=1).astype(f32)
    gain_one, gain_two = gains_full[0], gains_full[1]

    kv = key_projection_weight.shape[1]
    ff = w_gate.shape[1]
    sent = copy_blocks(
        colour,
        [
            [
                (w_query, (quarter, half), lambda c, k=k: (k, 0), 0, 0),
                (key_projection_weight, (quarter, kv), lambda c, k=k: (k, 0), 0, half),
                (value_projection_weight, (quarter, kv), lambda c, k=k: (k, 0), 0, half + kv),
            ]
            for k in range(2)
        ],
        [(quarter, half + 2 * kv)] * 2,
        (gains_other,),
    )
    qkv_one, qkv_two = two_ways(*sent)
    mask_values = valid_mask.reshape(rows).astype(f32)
    blocks = [
        [
            (w_gate, (192, ff), lambda c, k=k: (2 * c + k, 0), 0, 0),
            (w_out, (192, quarter), lambda c, k=k: (2 * k, c), 0, ff),
            (w_out, (192, quarter), lambda c, k=k: (2 * k + 1, c), 0, ff + quarter),
        ]
        for k in range(2)
    ]
    first_sent = copy_blocks(colour, blocks, [(192, ff + 2 * quarter)] * 2, (gains_other,))
    first_z = two_ways(*first_sent)

    residual_in = to_local(tokens.reshape(rows, width)).astype(f32)
    inverse_one = inverse_rms(residual_in)
    normed_one = (residual_in * inverse_one * gain_one).astype(bf16)
    normed_one_other = other_half(normed_one)
    projected = projection(
        normed_one[:, :half],
        normed_one_other,
        w_query,
        key_projection_weight,
        value_projection_weight,
        qkv_one,
        qkv_two,
        *first_sent,
    )
    mine = lax.all_to_all(projected, "y", 0, 0, tiled=True)
    queries, key_values = copy_blocks(
        colour,
        [
            [(mine, (512, 128), lambda c, k=k: (0, k), 0, 128 * (k - first)) for k in range(first, last)]
            for first, last in ((0, 3), (3, 5))
        ],
        [(512, 384), (512, 256)],
        (),
    )
    pieces = (group_move(key_values, 2), group_move(key_values, 1), key_values)
    blocks = [
        [(w_up, (192, ff), lambda c, k=k: (2 * c + k, 0), 0, 0)]
        + [
            (w_down, (192, quarter), lambda c, k=k, b=b: (5 * k + b, c), 0, ff + quarter * b)
            for b in range(5)
        ]
        for k in range(2)
    ]
    second_z = two_ways(*copy_blocks(colour, blocks, [(192, 2 * ff)] * 2, pieces[:2]))
    first = (first_z, over_x(*hold(first_z, pieces[0])))
    bounds = jnp.cumsum(lax.dynamic_index_in_dim(doc_lengths, y_index % 2, 0, keepdims=False))
    scalars = jnp.concatenate([(group_index * 512)[None], bounds]).astype(jnp.int32)
    attended_mine, logs = attention_forward(scalars, queries, pieces, ())
    returned = lax.all_to_all(attended_mine, "y", 0, 0, tiled=True)
    out_pieces = (*first[0], *first[1])
    attn_part, attended = out_projection(returned, w_out, out_pieces, ())
    split = copy_blocks(
        colour,
        [[(v, (192, ff), lambda c, k=k: (0, k), 0, 0)] for k in range(2) for v in second_z],
        [(192, ff)] * 4,
        (attn_part,),
    )
    second = (second_z, over_x(*split[:2]), over_y(*split[2:]))
    early = to_neighbours(jnp.concatenate([normed_one_other, attended], axis=1))
    weights = (w_gate, w_up, w_down, first, second)
    hidden_state, normed_two, inverse_two, gate_pre, up_pre, activated, ffn_part = ffn_forward(
        residual_in, attn_part, swap(attn_part, "tensor"), gain_two, weights
    )
    middle = to_neighbours(jnp.concatenate([other_half(normed_two), activated], axis=1))

    final_state = hidden_state + branch_scale * core_sum(ffn_part)
    deviation = final_state - to_local(teacher.reshape(rows, width)).astype(f32)
    row_squares = mask_values * jnp.mean(deviation * deviation, axis=-1)
    grad_final = deviation * mask_values[:, None]
    branch_two = (branch_scale * grad_final).astype(bf16)
    grad_gate_pre, grad_up_pre, part = ffn_backward(branch_two, gate_pre, up_pre, weights, early)
    late = to_neighbours(
        jnp.concatenate([other_half(branch_two), grad_gate_pre, grad_up_pre], axis=1)
    )
    grad_normed_two = core_sum(part)

    grad_from_norm, gain_terms_two = norm_backward(
        hidden_state, inverse_two, gain_two, grad_normed_two
    )
    grad_hidden = grad_final + grad_from_norm
    branch_one = (branch_scale * grad_hidden).astype(bf16)
    grad_attended = out_backward(branch_one, w_out, out_pieces)
    branch_moved = to_neighbours(other_half(branch_one))
    grad_mine = lax.all_to_all(grad_attended, "y", 0, 0, tiled=True)
    grad_queries, grad_older, grad_newer, grad_own = attention_backward(
        scalars, queries, grad_mine, logs, pieces, ()
    )
    ffn_grads = ffn_gradients(
        normed_two, branch_two, grad_gate_pre, grad_up_pre, activated, middle, late, (grad_older,)
    )
    ffn_share = lax.psum_scatter(ffn_grads, ("x", "y"), scatter_dimension=0, tiled=True)
    older = group_move(grad_older, -2)
    newer = group_move(grad_newer, -1)
    grad_projected = lax.all_to_all(
        merge(grad_queries, grad_own, newer, older, branch_moved), "y", 0, 0, tiled=True
    )
    grad_projected = jnp.concatenate([grad_projected[:rows], grad_projected[rows:]], axis=1)
    last = to_neighbours(grad_projected)
    grad_normed_one = core_sum(
        projection_backward(
            colour,
            grad_projected,
            w_query,
            key_projection_weight,
            value_projection_weight,
            qkv_one,
            qkv_two,
        )
    )
    gradient_via_first_norm, gain_terms_one = norm_backward(
        residual_in, inverse_one, gain_one, grad_normed_one
    )
    grad_tokens = from_local(grad_hidden + gradient_via_first_norm)

    ones = jnp.ones((rows, 128), f32)

    def column_sums(terms):
        return lax.dot_general(
            terms, ones, (((0,), (0,)), ((), ())), precision=lax.Precision.HIGHEST
        )

    def on_rows(values):
        return jnp.pad(jnp.broadcast_to(values[:, None], (rows, 128)), ((0, half - rows), (0, 0)))

    entries = [
        column_sums(gain_terms_one[:, :half]),
        column_sums(other_half(gain_terms_one)),
        column_sums(gain_terms_two[:, :half]),
        column_sums(other_half(gain_terms_two)),
        on_rows(mask_values),
        on_rows(row_squares),
    ]
    slot = lax.broadcasted_iota(jnp.int32, (half, 128), 1) // 8
    tile = jnp.zeros((half, 128), f32)
    for k, entry in enumerate(entries):
        tile = jnp.where(slot == k, entry, tile)
    bits = jnp.stack([pair_bit(steps[0]) for steps in FIRST]).astype(jnp.int32)
    cut_rows = attention_gradients(
        bits,
        normed_one,
        grad_projected,
        attended,
        branch_one,
        *early,
        *last,
        *branch_moved,
        tile.astype(bf16),
    )
    channels = [
        add_moved(cut_rows[2 * k], cut_rows[2 * k + 1], FIRST[k][0]) for k in range(4)
    ]
    (ffn_share,) = hold([ffn_share], *channels)
    ffn_share = z_sum(ffn_share)
    channels = reduce_second(channels)
    pairs = [jnp.concatenate(channels[k : k + 2], axis=1) for k in (0, 2)]
    pairs = reduce_pairs(pairs, 0)
    (ffn_share,) = hold([ffn_share], *pairs)
    ffn_total_grads = lax.all_gather(ffn_share, ("x", "y"), axis=0, tiled=True)
    pairs = reduce_pairs(pairs, 1)
    pairs = reduce_rest(pairs, [c.shape[1] for c in channels])
    *attn_results, small = attention_results(bits, pairs)
    scale = small[3, 0]

    layer_out = from_local(final_state.astype(bf16)).reshape(seq_count, row_count, width)
    return (
        layer_out,
        small[2, 0],
        (grad_tokens * scale).reshape(seq_count, row_count, width),
        *attn_results,
        *ffn_results(pairs[3], ffn_total_grads),
        small[0],
        small[1],
    )


def solution(mesh):
    fine = Mesh(mesh.devices.reshape(2, 4, 2, 4, 2), ("dp", "x", "z_hi", "y", "tensor"))
    ctx = ("x", "z_hi", "y")
    return jax.shard_map(
        local,
        mesh=fine,
        in_specs=(
            P("dp", ctx, None),
            P("dp", "tensor"),
            P("dp", "tensor"),
            P("dp", "tensor"),
            P("tensor", "dp"),
            P("dp", "tensor"),
            P("dp", "tensor"),
            P("tensor", "dp"),
            P("dp"),
            P("dp"),
            P("dp", None),
            P("dp", ctx),
            P("dp", ctx, None),
        ),
        out_specs=(
            P("dp", ctx, None),
            P(),
            P("dp", ctx, None),
            P("dp", "tensor"),
            P("dp", "tensor"),
            P("dp", "tensor"),
            P("tensor", "dp"),
            P("dp", "tensor"),
            P("dp", "tensor"),
            P("tensor", "dp"),
            P("dp"),
            P("dp"),
        ),
        check_vma=False,
    )
```

```python
import math

import jax
import jax.numpy as jnp
from jax import lax
from jax.experimental import pallas as pl
from jax.experimental.pallas import tpu as pltpu
from jax.sharding import Mesh
from jax.sharding import PartitionSpec as P

HEAD = 64
WINDOW = 1024
BLOCK = 128
GROUP = 3
SPAN = WINDOW + BLOCK

branch_scale = 1.4 / math.sqrt(52.0)
norm_epsilon = 1e-05
masked_score = -1e30
scale_factor = 1.0 / math.sqrt(HEAD)
bf16 = jnp.bfloat16
f32 = jnp.float32


def dot(left, right):
    return jnp.dot(left, right, preferred_element_type=f32)


def dot_nt(left, right):
    return lax.dot_general(left, right, (((1,), (1,)), ((), ())), preferred_element_type=f32)


def dot_tn(left, right):
    return lax.dot_general(left, right, (((0,), (0,)), ((), ())), preferred_element_type=f32)


def z_move(value, distance):
    route = []
    for dp in range(2):
        for hi in range(2):
            z = (hi * 2 + dp + distance) % 4
            route.append((dp * 2 + hi, (z % 2) * 2 + z // 2))
    return lax.ppermute(value, ("dp", "z_hi"), route)


def ring_move(value, axis, distance):
    size = lax.axis_size(axis)
    return lax.ppermute(value, axis, [(i, (i + distance) % size) for i in range(size)])


def group_move(value, distance):
    return lax.ppermute(
        value, ("x", "z_hi"), [(i, i + distance) for i in range(8) if 0 <= i + distance < 8]
    )


def swap(value, axis):
    return lax.ppermute(value, axis, [(0, 1), (1, 0)])


PAIRS = {"even": ((0, 1), (1, 0), (2, 3), (3, 2)), "odd": ((0, 3), (3, 0), (1, 2), (2, 1))}


def pair_move(value, step):
    return lax.ppermute(value, step[0], PAIRS[step[1]])


def pair_bit(step):
    index = lax.axis_index(step[0])
    return (index // 2 + index) % 2 if step[1] == "even" else index // 2


def core_sum(part):
    return part.astype(f32) + swap(part, "tensor").astype(f32)


def z_sum(value):
    return (value.astype(f32) + swap(value, "z_hi").astype(f32)).astype(bf16)


def halves(value, step):
    bit = pair_bit(step)
    half = value.shape[0] // 2
    return (
        lax.dynamic_slice_in_dim(value, bit * half, half, 0),
        lax.dynamic_slice_in_dim(value, (1 - bit) * half, half, 0),
    )


def add_moved(keep, send, step):
    return (keep.astype(f32) + pair_move(send, step).astype(f32)).astype(bf16)


def halve(value, step):
    return add_moved(*halves(value, step), step)


def double(value, step):
    other = pair_move(value, step)
    return jnp.where(
        pair_bit(step) == 0,
        jnp.concatenate([value, other], axis=0),
        jnp.concatenate([other, value], axis=0),
    )


FIRST = (
    (("x", "even"), ("x", "odd")),
    (("x", "odd"), ("x", "even")),
    (("y", "even"), ("y", "odd")),
    (("y", "odd"), ("y", "even")),
)
SECOND = ((("y", "even"), ("y", "odd")), (("x", "even"), ("x", "odd")))


def reduce_second(channels):
    return [halve(c, FIRST[i][1]) for i, c in enumerate(channels)]


def reduce_pairs(pairs, level):
    return [halve(c, SECOND[i][level]) for i, c in enumerate(pairs)]


def reduce_rest(pairs, widths):
    at = widths[0] + widths[1]
    rows = pairs[0].shape[0]
    (total,) = copy_blocks(
        jnp.zeros((), jnp.int32),
        [
            [
                (pair, pair.shape, lambda c: (0, 0), 0, first)
                for pair, first in zip(pairs, (0, at))
            ]
        ],
        [(rows, sum(widths))],
        (),
    )
    tile = total[:, -128:]
    beside = z_move(tile, 1).astype(f32) + z_move(tile, -1).astype(f32)
    beside = jnp.concatenate([beside[:, 64:], beside[:, :64]], axis=1).astype(bf16)
    total = z_sum(total)
    total = jnp.concatenate([total[:, :-128], total[:, -128:] + beside], axis=1)
    pairs = [total[:, :at], total[:, at:]]
    for level in (1, 0):
        pairs = [double(c, SECOND[i][level]) for i, c in enumerate(pairs)]
    channels = [
        pairs[0][:, : widths[0]],
        pairs[0][:, widths[0] :],
        pairs[1][:, : widths[2]],
        pairs[1][:, widths[2] :],
    ]
    channels = [double(c, FIRST[i][1]) for i, c in enumerate(channels)]
    return [(c, pair_move(c, FIRST[i][0])) for i, c in enumerate(channels)]


def inverse_rms(source):
    return lax.rsqrt(jnp.mean(source * source, axis=-1, keepdims=True) + norm_epsilon)


def norm_backward(source, inverse, gain_vec, grad_normed):
    weighted = grad_normed * gain_vec
    grad_source = inverse * weighted - source * (inverse * inverse * inverse) * jnp.mean(
        source * weighted, axis=-1, keepdims=True
    )
    return (grad_source, grad_normed * source * inverse)


def allowed_keys(scalars, r):
    shape = (BLOCK, SPAN)
    query_pos = scalars[0] + r * BLOCK + lax.broadcasted_iota(jnp.int32, shape, 0)
    key_pos = scalars[0] + r * BLOCK - WINDOW + lax.broadcasted_iota(jnp.int32, shape, 1)
    lowest = jnp.maximum(query_pos - (WINDOW - 1), 0)
    for d in range(1, 5):
        lowest = jnp.maximum(lowest, jnp.where(query_pos >= scalars[d], scalars[d], 0))
    allowed = (key_pos >= lowest) & (key_pos <= query_pos)
    return jnp.concatenate([allowed] * (2 * GROUP), axis=0)


def low_half():
    return lax.broadcasted_iota(jnp.int32, (BLOCK, 128), 1) < HEAD


def head_rows(ref, factor):
    parts = []
    for h in range(2 * GROUP):
        g = h // GROUP
        lanes = low_half() if g == 0 else jnp.logical_not(low_half())
        columns = ref[:, h // 2 * 128 : h // 2 * 128 + 128].astype(f32)
        if h % 2 != g:
            columns = pltpu.roll(columns, HEAD, 1)
        parts.append(jnp.where(lanes, columns * factor, 0.0).astype(bf16))
    return jnp.concatenate(parts, axis=0)


def put_heads(ref, results):
    sides = []
    for h in range(2 * GROUP):
        columns = results[h * BLOCK : (h + 1) * BLOCK]
        sides.append(pltpu.roll(columns, HEAD, 1) if h % 2 != h // GROUP else columns)
    for t in range(GROUP):
        ref[:, t * 128 : (t + 1) * 128] = jnp.where(
            low_half(), sides[2 * t], sides[2 * t + 1]
        ).astype(ref.dtype)


def fill_window(window, older, newer, own):
    window[0:512] = older[...]
    window[512:1024] = newer[...]
    window[1024:1536] = own[...]


def attention_forward_kernel(scalars, q_ref, older, newer, own, *rest):
    out_ref, log_ref, window = rest[-3:]
    r = pl.program_id(0)

    @pl.when(r == 0)
    def _():
        fill_window(window, older, newer, own)

    span = pl.ds(pl.multiple_of(r * BLOCK, BLOCK), SPAN)
    keys = window[span, 0:128]
    values = window[span, 128:256]
    allowed = allowed_keys(scalars, r)
    scores = jnp.where(allowed, dot_nt(head_rows(q_ref, scale_factor), keys), masked_score)
    top = jnp.max(scores, axis=-1, keepdims=True)
    weights = jnp.exp(scores - top)
    total = jnp.sum(weights, axis=-1, keepdims=True)
    log_ref[0] = top + jnp.log(total)
    put_heads(out_ref, dot((weights * (1.0 / total)).astype(bf16), values))


def attention_backward_kernel(scalars, q_ref, g_ref, log_ref, older, newer, own, *rest):
    dq_ref, older_ref, newer_ref, own_ref, window, sums = rest[-6:]
    r = pl.program_id(0)

    @pl.when(r == 0)
    def _():
        fill_window(window, older, newer, own)
        sums[...] = jnp.zeros_like(sums)

    span = pl.ds(pl.multiple_of(r * BLOCK, BLOCK), SPAN)
    keys = window[span, 0:128]
    values = window[span, 128:256]
    allowed = allowed_keys(scalars, r)
    q6 = head_rows(q_ref, scale_factor)
    g6 = head_rows(g_ref, 1.0)
    scores = jnp.where(allowed, dot_nt(q6, keys), masked_score)
    probs = jnp.exp(scores - log_ref[0])
    grad_probs = dot_nt(g6, values)
    inner = jnp.sum(grad_probs * probs, axis=-1, keepdims=True)
    grad_scores = (probs * (grad_probs - inner)).astype(bf16)
    put_heads(dq_ref, dot(grad_scores, keys) * scale_factor)
    sums[span, 0:128] += dot_tn(grad_scores, q6)
    sums[span, 128:256] += dot_tn(probs.astype(bf16), g6)

    @pl.when(r == 3)
    def _():
        for part, ref in enumerate((older_ref, newer_ref, own_ref)):
            rows = slice(part * 512, (part + 1) * 512)
            ref[:, 0:128] = sums[rows, 0:128].astype(ref.dtype)
            ref[:, 128:256] = sums[rows, 128:256].astype(ref.dtype)


SMEM = pl.BlockSpec(memory_space=pltpu.SMEM)
UNREAD = pl.BlockSpec(memory_space=pl.ANY)
SHORT = pl.CostEstimate(flops=1000, bytes_accessed=1000, transcendentals=0)


def whole(*shape):
    return pl.BlockSpec(shape, lambda i: (0,) * len(shape))


def params(mebibytes=24):
    return pltpu.CompilerParams(vmem_limit_bytes=mebibytes * 1024 * 1024)


def copy_blocks(index, outputs, shapes, held):
    blocks = [block for output in outputs for block in output]

    def kernel(index_ref, *refs):
        outs = refs[len(blocks) + len(held) :]
        at = 0
        for output, out in zip(outputs, outs):
            for _, shape, _, row, column in output:
                out[row : row + shape[0], column : column + shape[1]] = refs[at][...]
                at += 1

    return pl.pallas_call(
        kernel,
        grid_spec=pltpu.PrefetchScalarGridSpec(
            num_scalar_prefetch=1,
            grid=(1,),
            in_specs=[
                pl.BlockSpec(block[1], lambda i, ref, place=block[2]: place(ref[0]))
                for block in blocks
            ]
            + [UNREAD] * len(held),
            out_specs=[pl.BlockSpec(shape, lambda i, ref: (0, 0)) for shape in shapes],
        ),
        out_shape=[
            jax.ShapeDtypeStruct(shape, output[0][0].dtype)
            for shape, output in zip(shapes, outputs)
        ],
        compiler_params=params(20),
        cost_estimate=SHORT,
    )(index.reshape(1), *[block[0] for block in blocks], *held)


def hold(values, *held):
    return copy_blocks(
        jnp.zeros((), jnp.int32),
        [[(v, v.shape, lambda c: (0, 0), 0, 0)] for v in values],
        [v.shape for v in values],
        held,
    )


def attention_forward(scalars, queries, pieces, held):
    return pl.pallas_call(
        attention_forward_kernel,
        grid=(4,),
        in_specs=[SMEM, pl.BlockSpec((BLOCK, 384), lambda i: (i, 0))]
        + [whole(512, 256)] * 3
        + [UNREAD] * len(held),
        out_specs=(
            pl.BlockSpec((BLOCK, 384), lambda i: (i, 0)),
            pl.BlockSpec((1, 2 * GROUP * BLOCK, 1), lambda i: (i, 0, 0)),
        ),
        out_shape=(
            jax.ShapeDtypeStruct((512, 384), bf16),
            jax.ShapeDtypeStruct((4, 2 * GROUP * BLOCK, 1), f32),
        ),
        scratch_shapes=[pltpu.VMEM((1536, 256), bf16)],
        compiler_params=params(32),
        cost_estimate=SHORT,
    )(scalars, queries, *pieces, *held)


def attention_backward(scalars, queries, grads, logs, pieces, held):
    return pl.pallas_call(
        attention_backward_kernel,
        grid=(4,),
        in_specs=[
            SMEM,
            pl.BlockSpec((BLOCK, 384), lambda i: (i, 0)),
            pl.BlockSpec((BLOCK, 384), lambda i: (i, 0)),
            pl.BlockSpec((1, 2 * GROUP * BLOCK, 1), lambda i: (i, 0, 0)),
        ]
        + [whole(512, 256)] * 3
        + [UNREAD] * len(held),
        out_specs=(
            pl.BlockSpec((BLOCK, 384), lambda i: (i, 0)),
            whole(512, 256),
            whole(512, 256),
            whole(512, 256),
        ),
        out_shape=(
            jax.ShapeDtypeStruct((512, 384), bf16),
            jax.ShapeDtypeStruct((512, 256), bf16),
            jax.ShapeDtypeStruct((512, 256), bf16),
            jax.ShapeDtypeStruct((512, 256), f32),
        ),
        scratch_shapes=[pltpu.VMEM((1536, 256), bf16), pltpu.VMEM((1536, 256), f32)],
        compiler_params=params(32),
        cost_estimate=SHORT,
    )(scalars, queries, grads, logs, *pieces, *held)


TILE = 384
TOKENS = 16384
CHUNKS = ((0, 1024), (1024, 1920))


def weight_copies(refs, gate, up, down, sems):
    copies = {"gate": [], "up": [], "down": []}

    def add(group, source, target):
        count = sum(len(entries) for entries in copies.values())
        copies[group].append(pltpu.make_async_copy(source, target, sems.at[count]))

    for group, target, at in (("gate", gate, 0), ("up", up, 5)):
        if target is None:
            continue
        add(group, refs[at], target.at[pl.ds(0, 768), :])
        for k in range(4):
            add(
                group,
                refs[at + 1 + k].at[:, pl.ds(0, 1920)],
                target.at[pl.ds(768 + 192 * k, 192), :],
            )
    add("down", refs[10], down.at[:, pl.ds(0, 768)])
    for side in range(2):
        for b in range(5):
            rows = pl.ds(960 * side + 192 * b, 192)
            add(
                "down",
                refs[6 + side].at[:, pl.ds(1920 + 384 * b, 384)],
                down.at[rows, pl.ds(768, 384)],
            )
            add(
                "down",
                refs[11 + side].at[:, pl.ds(384 * b, 384)],
                down.at[rows, pl.ds(1152, 384)],
            )
    return copies


def weight_operands(w_gate, w_up, w_down, one, two):
    return [w_gate, *one[0], *one[1], w_up, *two[0], *two[1], w_down, *two[2]]


WEIGHT_SCRATCH = [
    pltpu.VMEM((1536, 1920), bf16),
    pltpu.VMEM((1536, 1920), bf16),
    pltpu.VMEM((1920, 1536), bf16),
    pltpu.SemaphoreType.DMA((31,)),
]


def start_all(copies, order):
    for group in order:
        for copy in copies[group]:
            copy.start()


def wait_all(copies):
    for copy in copies:
        copy.wait()


def gate_kernel(x_ref, own, moved, gain, *refs):
    h_ref, n_ref, r_ref, g_ref, gate, sems = refs[5:]
    copies = [pltpu.make_async_copy(refs[0], gate.at[pl.ds(0, 768), :], sems.at[0])]
    for k in range(4):
        copies.append(
            pltpu.make_async_copy(
                refs[1 + k].at[:, pl.ds(0, 1920)],
                gate.at[pl.ds(768 + 192 * k, 192), :],
                sems.at[1 + k],
            )
        )
    for copy in copies:
        copy.start()
    hidden = x_ref[...] + branch_scale * (own[...].astype(f32) + moved[...].astype(f32))
    inverse = inverse_rms(hidden)
    h_ref[...] = hidden
    r_ref[...] = inverse
    n_ref[...] = (hidden * inverse * gain[...]).astype(bf16)
    wait_all(copies)
    for a, b in CHUNKS:
        g_ref[:, a:b] = dot(n_ref[...], gate[:, a:b])


def ffn_forward_kernel(n_ref, g_ref, *refs):
    u_ref, a_ref, out_ref, up, down, sems = refs[13:]
    copies = weight_copies(refs[:13], None, up, down, sems)
    start_all(copies, ("up", "down"))
    wait_all(copies["up"])
    for a, b in CHUNKS:
        up_pre = dot(n_ref[...], up[:, a:b])
        u_ref[:, a:b] = up_pre
        gate_pre = g_ref[:, a:b]
        a_ref[:, a:b] = (gate_pre * jax.nn.sigmoid(gate_pre) * up_pre).astype(bf16)
    wait_all(copies["down"])
    out_ref[...] = dot(a_ref[...], down[...]).astype(bf16)


def ffn_backward_kernel(b_ref, g_ref, u_ref, *refs):
    weights = refs[:13]
    gg_ref, gu_ref, out_ref, gate, up, down, sems = refs[-7:]
    copies = weight_copies(weights, gate, up, down, sems)
    start_all(copies, ("down", "gate", "up"))
    wait_all(copies["down"])
    for a, b in CHUNKS:
        grad = dot_nt(b_ref[...], down[a:b, :]).astype(bf16).astype(f32)
        gate_pre, up_pre = g_ref[:, a:b], u_ref[:, a:b]
        sigmoid = jax.nn.sigmoid(gate_pre)
        gg_ref[:, a:b] = (
            grad * up_pre * sigmoid * (1.0 + gate_pre * (1.0 - sigmoid))
        ).astype(bf16)
        gu_ref[:, a:b] = (grad * gate_pre * sigmoid).astype(bf16)
    wait_all(copies["gate"])
    part = dot_nt(gg_ref[...], gate[...])
    wait_all(copies["up"])
    out_ref[...] = (part + dot_nt(gu_ref[...], up[...])).astype(bf16)


def gate_forward(residual, own, moved, gain, w_gate, first):
    rows, width = residual.shape
    hidden = w_gate.shape[1]
    operands = [w_gate, *first[0], *first[1]]
    shapes = [((rows, width), f32), ((rows, width), bf16), ((rows, 1), f32), ((rows, hidden), f32)]
    return pl.pallas_call(
        gate_kernel,
        grid=(1,),
        in_specs=[whole(rows, width)] * 3 + [whole(1, width)] + [UNREAD] * len(operands),
        out_specs=[whole(*shape) for shape, _ in shapes],
        out_shape=[jax.ShapeDtypeStruct(*entry) for entry in shapes],
        scratch_shapes=[pltpu.VMEM((1536, 1920), bf16), pltpu.SemaphoreType.DMA((5,))],
        compiler_params=params(24),
        cost_estimate=SHORT,
    )(residual, own, moved, gain.reshape(1, width), *operands)


def ffn_forward(normed, gate_pre, weights):
    rows, width = normed.shape
    operands = weight_operands(*weights)
    hidden = gate_pre.shape[1]
    shapes = [((rows, hidden), f32), ((rows, hidden), bf16), ((rows, width), bf16)]
    return pl.pallas_call(
        ffn_forward_kernel,
        grid=(1,),
        in_specs=[whole(rows, width), whole(rows, hidden)] + [UNREAD] * len(operands),
        out_specs=[whole(*shape) for shape, _ in shapes],
        out_shape=[jax.ShapeDtypeStruct(*entry) for entry in shapes],
        scratch_shapes=WEIGHT_SCRATCH[1:],
        compiler_params=params(38),
        cost_estimate=SHORT,
    )(normed, gate_pre, *operands)


def ffn_backward(branch, gate_pre, up_pre, weights, held):
    rows, width = branch.shape
    operands = weight_operands(*weights)
    hidden = weights[2].shape[0]
    shapes = [((rows, hidden), bf16), ((rows, hidden), bf16), ((rows, width), bf16)]
    return pl.pallas_call(
        ffn_backward_kernel,
        grid=(1,),
        in_specs=[whole(rows, width)]
        + [whole(rows, hidden)] * 2
        + [UNREAD] * (len(operands) + len(held)),
        out_specs=[whole(*shape) for shape, _ in shapes],
        out_shape=[jax.ShapeDtypeStruct(*entry) for entry in shapes],
        scratch_shapes=WEIGHT_SCRATCH,
        compiler_params=params(44),
        cost_estimate=SHORT,
    )(branch, gate_pre, up_pre, *operands, *held)


def hidden_tile(rows):
    return pl.BlockSpec((rows, TILE), lambda i: (0, i))


def projection_kernel(n_own, n_other, wq, wk, wv, one, two, *rest):
    out_ref = rest[-1]
    own = n_own[...]
    first, second = n_other[:, :384], n_other[:, 384:]
    rows = own.shape[0]
    for p in range(2):
        place = pl.ds(p * rows, rows)
        q_at, kv_at = slice(p * 384, p * 384 + 384), slice(p * 128, p * 128 + 128)
        for weight, own_at, at, out_at in (
            (wq, q_at, p * 384, slice(0, 384)),
            (wk, kv_at, 768 + p * 128, slice(384, 512)),
            (wv, kv_at, 1024 + p * 128, slice(512, 640)),
        ):
            there = slice(at, at + out_at.stop - out_at.start)
            out_ref[place, out_at] = (
                dot(own, weight[:, own_at])
                + dot(first, one[:, there])
                + dot(second, two[:, there])
            ).astype(bf16)


def projection_backward_kernel(colour, g_ref, wq, wk, wv, one, two, out_ref):
    grad = jnp.concatenate(
        [
            g_ref[:, a:b]
            for a, b in ((0, 384), (640, 1024), (384, 512), (1024, 1152), (512, 640), (1152, 1280))
        ],
        axis=1,
    )
    out_ref[:, 0:768] = (
        dot_nt(grad[:, 0:768], wq[...])
        + dot_nt(grad[:, 768:1024], wk[...])
        + dot_nt(grad[:, 1024:1280], wv[...])
    ).astype(bf16)
    first = dot_nt(grad, one[...]).astype(bf16)
    second = dot_nt(grad, two[...]).astype(bf16)

    @pl.when(colour[0] == 0)
    def _():
        out_ref[:, 768:1152] = first
        out_ref[:, 1152:1536] = second

    @pl.when(colour[0] != 0)
    def _():
        out_ref[:, 768:1152] = second
        out_ref[:, 1152:1536] = first


def projection_backward(colour, *operands):
    rows = operands[0].shape[0]
    return pl.pallas_call(
        projection_backward_kernel,
        grid=(1,),
        in_specs=[SMEM] + [whole(*operand.shape) for operand in operands],
        out_specs=whole(rows, 1536),
        out_shape=jax.ShapeDtypeStruct((rows, 1536), bf16),
        compiler_params=params(),
        cost_estimate=SHORT,
    )(colour.reshape(1), *operands)


def out_blocks(pieces):
    operands = [piece for piece in pieces for _ in range(2)]
    specs = [pl.BlockSpec((192, 384), lambda i, k=k: (0, k)) for k in (5, 6)] * 4
    return operands, specs


def out_columns(refs):
    return jnp.concatenate([ref[...] for ref in refs], axis=0)


def out_projection_kernel(back_ref, w_ref, *refs):
    part_ref, attended_ref = refs[-2:]
    rows = attended_ref.shape[0]
    attended = jnp.concatenate([back_ref[0:rows], back_ref[rows : 2 * rows]], axis=1)
    attended_ref[...] = attended
    part_ref[:, 0:768] = dot(attended, w_ref[...]).astype(bf16)
    part_ref[:, 768:1152] = dot(attended, out_columns(refs[0:4])).astype(bf16)
    part_ref[:, 1152:1536] = dot(attended, out_columns(refs[4:8])).astype(bf16)


def out_projection(back, w_out, pieces, held):
    rows = back.shape[0] // 2
    operands, specs = out_blocks(pieces)
    return pl.pallas_call(
        out_projection_kernel,
        grid=(1,),
        in_specs=[whole(*back.shape), whole(*w_out.shape)] + specs + [UNREAD] * len(held),
        out_specs=(whole(rows, 1536), whole(rows, 768)),
        out_shape=(
            jax.ShapeDtypeStruct((rows, 1536), bf16),
            jax.ShapeDtypeStruct((rows, 768), bf16),
        ),
        compiler_params=params(),
        cost_estimate=SHORT,
    )(back, w_out, *operands, *held)


def out_backward_kernel(b_ref, w_ref, *refs):
    out_ref = refs[-1]
    rows = b_ref.shape[0]
    grad = (
        dot_nt(b_ref[:, 0:768], w_ref[...])
        + dot_nt(b_ref[:, 768:1152], out_columns(refs[0:4]))
        + dot_nt(b_ref[:, 1152:1536], out_columns(refs[4:8]))
    ).astype(bf16)
    out_ref[0:rows] = grad[:, 0:384]
    out_ref[rows : 2 * rows] = grad[:, 384:768]


def out_backward(branch, w_out, pieces):
    rows = branch.shape[0]
    operands, specs = out_blocks(pieces)
    return pl.pallas_call(
        out_backward_kernel,
        grid=(1,),
        in_specs=[whole(*branch.shape), whole(*w_out.shape)] + specs,
        out_specs=whole(2 * rows, 384),
        out_shape=jax.ShapeDtypeStruct((2 * rows, 384), bf16),
        compiler_params=params(),
        cost_estimate=SHORT,
    )(branch, w_out, *operands)


def projection(*operands):
    rows = operands[0].shape[0]
    return pl.pallas_call(
        projection_kernel,
        in_specs=[pl.BlockSpec(memory_space=pltpu.VMEM)] * 7 + [UNREAD] * (len(operands) - 7),
        out_shape=jax.ShapeDtypeStruct((2 * rows, 640), bf16),
        compiler_params=params(),
        cost_estimate=SHORT,
    )(*operands)


def merge_kernel(q_ref, own, newer, older, *rest):
    out_ref = rest[-1]
    out_ref[:, 0:384] = q_ref[...]
    out_ref[:, 384:640] = (
        own[...] + newer[...].astype(f32) + older[...].astype(f32)
    ).astype(bf16)


def merge(grad_queries, own, newer, older, held):
    operands = (grad_queries, own, newer, older)
    return pl.pallas_call(
        merge_kernel,
        grid=(1,),
        in_specs=[whole(*operand.shape) for operand in operands] + [UNREAD] * len(held),
        out_specs=whole(512, 640),
        out_shape=jax.ShapeDtypeStruct((512, 640), bf16),
        compiler_params=params(),
        cost_estimate=SHORT,
    )(*operands, *held)


def ffn_gradients_kernel(normed, branch, gate, up, act, m_one, m_two, l_one, l_two, *rest):
    out_ref, n_all, b_all, gate_all, up_all, act_all, total, in_sems, out_sems = rest[-9:]
    rows, width, hidden = 256, 768, 1920
    copies = {}
    for name, own, received, at, target in (
        ("normed", normed, (m_one, m_two), 0, n_all),
        ("gate", gate, (l_one, l_two), width, gate_all),
        ("up", up, (l_one, l_two), width + hidden, up_all),
        ("act", act, (m_one, m_two), width, act_all),
        ("branch", branch, (l_one, l_two), 0, b_all),
    ):
        columns = target.shape[1]
        parts = [(own.at[:, pl.ds(0, columns)], target.at[pl.ds(0, rows), :])]
        for k, part in enumerate(received):
            parts.append(
                (
                    part.at[:, pl.ds(at, columns)],
                    target.at[pl.ds(rows + 128 * k, 128), :],
                )
            )
        base = 3 * len(copies)
        copies[name] = [
            pltpu.make_async_copy(source, place, in_sems.at[base + k])
            for k, (source, place) in enumerate(parts)
        ]
        for copy in copies[name]:
            copy.start()

    def send(k):
        place = pl.ds(k * width, width)
        copy = pltpu.make_async_copy(total.at[place, :], out_ref.at[place, :], out_sems.at[k])
        copy.start()
        return copy

    wait_all(copies["normed"])
    wait_all(copies["gate"])
    for a, b in CHUNKS:
        total[0:width, a:b] = dot_tn(n_all[...], gate_all[:, a:b]).astype(bf16)
    sent = [send(0)]
    wait_all(copies["up"])
    for a, b in CHUNKS:
        total[width : 2 * width, a:b] = dot_tn(n_all[...], up_all[:, a:b]).astype(bf16)
    sent.append(send(1))
    wait_all(copies["act"])
    wait_all(copies["branch"])
    for a, b in CHUNKS:
        down = dot_tn(act_all[:, a:b], b_all[...]).astype(bf16)
        for r in range(width // 128):
            for c in range((b - a) // 128):
                total[
                    2 * width + r * 128 : 2 * width + r * 128 + 128, a + c * 128 : a + c * 128 + 128
                ] = down[c * 128 : c * 128 + 128, r * 128 : r * 128 + 128]
    sent.append(send(2))
    wait_all(sent)


def ffn_gradients(normed, branch, gate, up, act, middle, late, held):
    operands = (normed, branch, gate, up, act, *middle, *late, *held)
    return pl.pallas_call(
        ffn_gradients_kernel,
        grid=(1,),
        in_specs=[UNREAD] * len(operands),
        out_specs=pl.BlockSpec(memory_space=pltpu.HBM),
        out_shape=jax.ShapeDtypeStruct((2304, 1920), bf16),
        scratch_shapes=[pltpu.VMEM((512, 768), bf16)] * 2
        + [pltpu.VMEM((512, 1920), bf16)] * 3
        + [
            pltpu.VMEM((2304, 1920), bf16),
            pltpu.SemaphoreType.DMA((15,)),
            pltpu.SemaphoreType.DMA((3,)),
        ],
        compiler_params=params(40),
        cost_estimate=SHORT,
    )(*operands)


CHANNELS = (0, 640, 1152, 1664, 2176)


def attention_gradients_kernel(bits, *refs):
    normed, projected, attended, branch = refs[0:4]
    early, last, branch_moved = refs[4:6], refs[6:8], refs[8:10]
    outs, total = refs[11:-1], refs[-1]
    total[:, 2048:2176] = refs[10][...]

    def rows_of(own, received, at, width):
        parts = [own[:, :width]] + [ref[:, at : at + width] for ref in received]
        return jnp.concatenate(parts, axis=0)

    total[:, 0:768] = dot_tn(
        rows_of(attended, early, 768, 768), rows_of(branch, branch_moved, 0, 768)
    ).astype(bf16)
    total[:, 768:2048] = dot_tn(
        rows_of(normed, early, 0, 768), rows_of(projected, last, 0, 1280)
    ).astype(bf16)
    for c in range(4):
        columns = slice(CHANNELS[c], CHANNELS[c + 1])
        keep = pl.multiple_of(bits[c] * 384, 384)
        send = pl.multiple_of(384 - bits[c] * 384, 384)
        outs[2 * c][...] = total[pl.ds(keep, 384), columns]
        outs[2 * c + 1][...] = total[pl.ds(send, 384), columns]


def attention_gradients(bits, *operands):
    widths = [b - a for a, b in zip(CHANNELS[:-1], CHANNELS[1:]) for _ in range(2)]
    return list(
        pl.pallas_call(
            attention_gradients_kernel,
            grid=(1,),
            in_specs=[SMEM] + [whole(*operand.shape) for operand in operands],
            out_specs=[whole(384, w) for w in widths],
            out_shape=[jax.ShapeDtypeStruct((384, w), bf16) for w in widths],
            scratch_shapes=[pltpu.VMEM((768, 2176), bf16)],
            compiler_params=params(),
            cost_estimate=SHORT,
        )(bits, *operands)
    )


def ffn_results_kernel(one, two, total_hbm, *refs):
    outs, total, f_gate, f_up, f_down, in_sems, out_sems = refs[0:3], *refs[3:]
    width, hidden = 768, 1920
    targets = (f_gate, f_up, f_down)
    chunks = []
    for m in range(2):
        for r in range(2):
            place = pl.ds(m * width + r * 384, 384)
            chunks.append((m, r, (place, pl.ds(0, hidden)), (pl.ds(r * 384, 384), pl.ds(0, hidden))))
    for r, (a, b) in enumerate(CHUNKS):
        place = (pl.ds(2 * width, width), pl.ds(a, b - a))
        chunks.append((2, r, place, (pl.ds(a, b - a), pl.ds(0, width))))
    arriving, leaving = [], []
    for k, (_, _, place, _) in enumerate(chunks):
        arriving.append(
            pltpu.make_async_copy(total_hbm.at[place], total.at[place], in_sems.at[k])
        )
        arriving[-1].start()
    scale = TOKENS / count_of(one, two)
    for k, (m, r, _, there) in enumerate(chunks):
        arriving[k].wait()
        if m < 2:
            rows = slice(r * 384, r * 384 + 384)
            source = slice(m * width + r * 384, m * width + r * 384 + 384)
            targets[m][rows] = total[source].astype(f32) * scale
        else:
            a, b = CHUNKS[r]
            for p in range(a // 128, b // 128):
                for q in range(width // 128):
                    f_down[p * 128 : p * 128 + 128, q * 128 : q * 128 + 128] = (
                        total[
                            2 * width + q * 128 : 2 * width + q * 128 + 128,
                            p * 128 : p * 128 + 128,
                        ].astype(f32)
                        * scale
                    )
        leaving.append(
            pltpu.make_async_copy(targets[m].at[there], outs[m].at[there], out_sems.at[k])
        )
        leaving[-1].start()
    wait_all(leaving)


def ffn_results(pair, total):
    width, hidden = total.shape[0] // 3, total.shape[1]
    shapes = ((width, hidden), (width, hidden), (hidden, width))
    hbm = pl.BlockSpec(memory_space=pltpu.HBM)
    return pl.pallas_call(
        ffn_results_kernel,
        grid=(1,),
        in_specs=[whole(*value.shape) for value in pair] + [hbm],
        out_specs=[hbm] * 3,
        out_shape=[jax.ShapeDtypeStruct(shape, f32) for shape in shapes],
        scratch_shapes=[pltpu.VMEM(total.shape, bf16)]
        + [pltpu.VMEM(shape, f32) for shape in shapes]
        + [pltpu.SemaphoreType.DMA((6,)), pltpu.SemaphoreType.DMA((6,))],
        compiler_params=params(58),
        cost_estimate=SHORT,
    )(*pair, total)


PLACES = (
    (0, 0, 640, 3, 0),
    (1, 0, 128, 3, 640),
    (1, 128, 384, 0, 0),
    (2, 0, 128, 1, 0),
    (2, 128, 128, 2, 0),
    (2, 256, 256, 0, 384),
    (3, 0, 128, 0, 640),
    (3, 128, 128, 1, 128),
    (3, 256, 128, 2, 128),
)


def count_of(ref_one, ref_two):
    total = None
    for ref in (ref_one, ref_two):
        for lane in (32, 96):
            part = jnp.sum(ref[:, 384 + lane : 385 + lane].astype(f32), axis=0, keepdims=True)
            total = part if total is None else total + part
    return total


def attention_results_kernel(bits, *refs):
    outs, rows_ref, tile = refs[8:12], refs[12], refs[13]
    count = count_of(refs[6], refs[7])
    scale = TOKENS / count
    for c, at, width, out, there in PLACES:
        for side in range(2):
            first = bits[c] * 384 if side == 0 else 384 - bits[c] * 384
            outs[out][pl.ds(pl.multiple_of(first, 384), 384), there : there + width] = (
                refs[2 * c + side][:, at : at + width].astype(f32) * scale
            )
    for side in range(2):
        first = bits[3] * 384 if side == 0 else 384 - bits[3] * 384
        tile[pl.ds(pl.multiple_of(first, 384), 384), :] = refs[6 + side][:, 384:512].astype(f32)
    lines = jnp.transpose(tile[...])
    rows_ref[0:1] = (lines[0:1] + lines[72:73]) * scale
    rows_ref[1:2] = (lines[16:17] + lines[88:89]) * scale
    squares = jnp.sum(lines[40:41] + lines[104:105], axis=1, keepdims=True)
    rows_ref[2:3] = jnp.broadcast_to(squares / count, (1, 768))
    rows_ref[3:4] = jnp.broadcast_to(scale, (1, 768))


def attention_results(bits, pairs):
    operands = [value for pair in pairs for value in pair]
    widths = (768, 256, 256, 768)
    return pl.pallas_call(
        attention_results_kernel,
        grid=(1,),
        in_specs=[SMEM] + [whole(*operand.shape) for operand in operands],
        out_specs=[whole(768, width) for width in widths] + [whole(8, 768)],
        out_shape=[jax.ShapeDtypeStruct((768, width), f32) for width in widths]
        + [jax.ShapeDtypeStruct((8, 768), f32)],
        scratch_shapes=[pltpu.VMEM((768, 128), f32)],
        compiler_params=params(),
        cost_estimate=SHORT,
    )(bits, *operands)


def local(
    tokens,
    w_query,
    key_projection_weight,
    value_projection_weight,
    w_out,
    w_gate,
    w_up,
    w_down,
    norm_attn,
    norm_ffn,
    doc_lengths,
    valid_mask,
    teacher,
):
    seq_count, row_count, width = tokens.shape
    rows = seq_count * row_count
    half = width // 2
    quarter = width // 4
    dp = lax.axis_index("dp")
    colour = (lax.axis_index("x") + lax.axis_index("y")) % 2
    y_index = lax.axis_index("y")
    group_index = lax.axis_index("x") * 2 + lax.axis_index("z_hi")

    def to_local(value):
        own = jnp.where(dp == 0, value[..., :half], value[..., half:])
        other = jnp.where(dp == 0, value[..., half:], value[..., :half])
        first = jnp.where(colour == 0, other[..., :quarter], other[..., quarter:])
        second = jnp.where(colour == 0, other[..., quarter:], other[..., :quarter])
        return jnp.concatenate([own, first, second], axis=-1)

    def other_half_of(first, second):
        return jnp.concatenate(
            [jnp.where(colour == 0, first, second), jnp.where(colour == 0, second, first)], axis=-1
        )

    def other_half(value):
        return other_half_of(value[..., half : half + quarter], value[..., half + quarter :])

    def from_local(value):
        own, other = value[..., :half], other_half(value)
        return jnp.concatenate(
            [jnp.where(dp == 0, own, other), jnp.where(dp == 0, other, own)], axis=-1
        )

    def two_ways(first, second):
        return z_move(first, 1), z_move(second, -1)

    def over_x(one, two):
        return ring_move(one, "x", 1), ring_move(two, "x", -1)

    def over_y(one, two):
        return ring_move(one, "y", 1), ring_move(two, "y", -1)

    def to_neighbours(value):
        return two_ways(value[:row_count], value[row_count:])

    gains = jnp.stack([norm_attn, norm_ffn])
    gains_other = swap(gains, "dp")
    gains_first = jnp.where(colour == 0, gains_other[:, :quarter], gains_other[:, quarter:])
    gains_second = jnp.where(colour == 0, gains_other[:, quarter:], gains_other[:, :quarter])
    gains_full = jnp.concatenate([gains, gains_first, gains_second], axis=1).astype(f32)
    gain_one, gain_two = gains_full[0], gains_full[1]

    kv = key_projection_weight.shape[1]
    ff = w_gate.shape[1]
    sent = copy_blocks(
        colour,
        [
            [
                (w_query, (quarter, half), lambda c, k=k: (k, 0), 0, 0),
                (key_projection_weight, (quarter, kv), lambda c, k=k: (k, 0), 0, half),
                (value_projection_weight, (quarter, kv), lambda c, k=k: (k, 0), 0, half + kv),
            ]
            for k in range(2)
        ],
        [(quarter, half + 2 * kv)] * 2,
        (gains_other,),
    )
    qkv_one, qkv_two = two_ways(*sent)
    mask_values = valid_mask.reshape(rows).astype(f32)
    blocks = [
        [
            (w_gate, (192, ff), lambda c, k=k: (2 * c + k, 0), 0, 0),
            (w_out, (192, quarter), lambda c, k=k: (2 * k, c), 0, ff),
            (w_out, (192, quarter), lambda c, k=k: (2 * k + 1, c), 0, ff + quarter),
        ]
        for k in range(2)
    ]
    first_sent = copy_blocks(colour, blocks, [(192, ff + 2 * quarter)] * 2, (gains_other,))
    first_z = two_ways(*first_sent)

    residual_in = to_local(tokens.reshape(rows, width)).astype(f32)
    inverse_one = inverse_rms(residual_in)
    normed_one = (residual_in * inverse_one * gain_one).astype(bf16)
    normed_one_other = other_half(normed_one)
    projected = projection(
        normed_one[:, :half],
        normed_one_other,
        w_query,
        key_projection_weight,
        value_projection_weight,
        qkv_one,
        qkv_two,
        *first_sent,
    )
    mine = lax.all_to_all(projected, "y", 0, 0, tiled=True)
    queries, key_values = copy_blocks(
        colour,
        [
            [(mine, (512, 128), lambda c, k=k: (0, k), 0, 128 * (k - first)) for k in range(first, last)]
            for first, last in ((0, 3), (3, 5))
        ],
        [(512, 384), (512, 256)],
        (),
    )
    pieces = (group_move(key_values, 2), group_move(key_values, 1), key_values)
    blocks = [
        [(w_up, (192, ff), lambda c, k=k: (2 * c + k, 0), 0, 0)]
        + [
            (w_down, (192, quarter), lambda c, k=k, b=b: (5 * k + b, c), 0, ff + quarter * b)
            for b in range(5)
        ]
        for k in range(2)
    ]
    second_z = two_ways(*copy_blocks(colour, blocks, [(192, 2 * ff)] * 2, pieces[:2]))
    first = (first_z, over_x(*hold(first_z, pieces[0])))
    bounds = jnp.cumsum(lax.dynamic_index_in_dim(doc_lengths, y_index % 2, 0, keepdims=False))
    scalars = jnp.concatenate([(group_index * 512)[None], bounds]).astype(jnp.int32)
    attended_mine, logs = attention_forward(scalars, queries, pieces, ())
    returned = lax.all_to_all(attended_mine, "y", 0, 0, tiled=True)
    out_pieces = (*first[0], *first[1])
    attn_part, attended = out_projection(returned, w_out, out_pieces, ())
    split = copy_blocks(
        colour,
        [[(v, (192, ff), lambda c, k=k: (0, k), 0, 0)] for k in range(2) for v in second_z],
        [(192, ff)] * 4,
        (attn_part,),
    )
    second = (second_z, over_x(*split[:2]), over_y(*split[2:]))
    early = to_neighbours(jnp.concatenate([normed_one_other, attended], axis=1))
    weights = (w_gate, w_up, w_down, first, second)
    hidden_state, normed_two, inverse_two, gate_pre = gate_forward(
        residual_in, attn_part, swap(attn_part, "tensor"), gain_two, w_gate, first
    )
    up_pre, activated, ffn_part = ffn_forward(normed_two, gate_pre, weights)
    middle = to_neighbours(jnp.concatenate([other_half(normed_two), activated], axis=1))

    final_state = hidden_state + branch_scale * core_sum(ffn_part)
    deviation = final_state - to_local(teacher.reshape(rows, width)).astype(f32)
    row_squares = mask_values * jnp.mean(deviation * deviation, axis=-1)
    grad_final = deviation * mask_values[:, None]
    branch_two = (branch_scale * grad_final).astype(bf16)
    grad_gate_pre, grad_up_pre, part = ffn_backward(branch_two, gate_pre, up_pre, weights, early)
    late = to_neighbours(
        jnp.concatenate([other_half(branch_two), grad_gate_pre, grad_up_pre], axis=1)
    )
    grad_normed_two = core_sum(part)

    grad_from_norm, gain_terms_two = norm_backward(
        hidden_state, inverse_two, gain_two, grad_normed_two
    )
    grad_hidden = grad_final + grad_from_norm
    branch_one = (branch_scale * grad_hidden).astype(bf16)
    grad_attended = out_backward(branch_one, w_out, out_pieces)
    branch_moved = to_neighbours(other_half(branch_one))
    grad_mine = lax.all_to_all(grad_attended, "y", 0, 0, tiled=True)
    grad_queries, grad_older, grad_newer, grad_own = attention_backward(
        scalars, queries, grad_mine, logs, pieces, ()
    )
    ffn_grads = ffn_gradients(
        normed_two, branch_two, grad_gate_pre, grad_up_pre, activated, middle, late, (grad_older,)
    )
    ffn_share = lax.psum_scatter(ffn_grads, ("x", "y"), scatter_dimension=0, tiled=True)
    older = group_move(grad_older, -2)
    newer = group_move(grad_newer, -1)
    grad_projected = lax.all_to_all(
        merge(grad_queries, grad_own, newer, older, branch_moved), "y", 0, 0, tiled=True
    )
    grad_projected = jnp.concatenate([grad_projected[:rows], grad_projected[rows:]], axis=1)
    last = to_neighbours(grad_projected)
    grad_normed_one = core_sum(
        projection_backward(
            colour,
            grad_projected,
            w_query,
            key_projection_weight,
            value_projection_weight,
            qkv_one,
            qkv_two,
        )
    )
    gradient_via_first_norm, gain_terms_one = norm_backward(
        residual_in, inverse_one, gain_one, grad_normed_one
    )
    grad_tokens = from_local(grad_hidden + gradient_via_first_norm)

    ones = jnp.ones((rows, 128), f32)

    def column_sums(terms):
        return lax.dot_general(
            terms, ones, (((0,), (0,)), ((), ())), precision=lax.Precision.HIGHEST
        )

    def on_rows(values):
        return jnp.pad(jnp.broadcast_to(values[:, None], (rows, 128)), ((0, half - rows), (0, 0)))

    entries = [
        column_sums(gain_terms_one[:, :half]),
        column_sums(other_half(gain_terms_one)),
        column_sums(gain_terms_two[:, :half]),
        column_sums(other_half(gain_terms_two)),
        on_rows(mask_values),
        on_rows(row_squares),
    ]
    slot = lax.broadcasted_iota(jnp.int32, (half, 128), 1) // 8
    tile = jnp.zeros((half, 128), f32)
    for k, entry in enumerate(entries):
        tile = jnp.where(slot == k, entry, tile)
    bits = jnp.stack([pair_bit(steps[0]) for steps in FIRST]).astype(jnp.int32)
    cut_rows = attention_gradients(
        bits,
        normed_one,
        grad_projected,
        attended,
        branch_one,
        *early,
        *last,
        *branch_moved,
        tile.astype(bf16),
    )
    channels = [
        add_moved(cut_rows[2 * k], cut_rows[2 * k + 1], FIRST[k][0]) for k in range(4)
    ]
    (ffn_share,) = hold([ffn_share], *channels)
    channels = reduce_second(channels)
    pairs = [
        copy_blocks(
            colour,
            [
                [
                    (left, left.shape, lambda c: (0, 0), 0, 0),
                    (right, right.shape, lambda c: (0, 0), 0, left.shape[1]),
                ]
            ],
            [(left.shape[0], left.shape[1] + right.shape[1])],
            held,
        )[0]
        for left, right, held in (
            (channels[0], channels[1], (ffn_share,)),
            (channels[2], channels[3], (ffn_share,)),
        )
    ]
    ffn_share = z_sum(ffn_share)
    pairs = reduce_pairs(pairs, 0)
    (ffn_share,) = hold([ffn_share], *pairs)
    ffn_total_grads = lax.all_gather(ffn_share, ("x", "y"), axis=0, tiled=True)
    pairs = reduce_pairs(pairs, 1)
    pairs = reduce_rest(pairs, [c.shape[1] for c in channels])
    *attn_results, small = attention_results(bits, pairs)
    scale = small[3, 0]

    layer_out = from_local(final_state.astype(bf16)).reshape(seq_count, row_count, width)
    return (
        layer_out,
        small[2, 0],
        (grad_tokens * scale).reshape(seq_count, row_count, width),
        *attn_results,
        *ffn_results(pairs[3], ffn_total_grads),
        small[0],
        small[1],
    )


def solution(mesh):
    fine = Mesh(mesh.devices.reshape(2, 4, 2, 4, 2), ("dp", "x", "z_hi", "y", "tensor"))
    ctx = ("x", "z_hi", "y")
    return jax.shard_map(
        local,
        mesh=fine,
        in_specs=(
            P("dp", ctx, None),
            P("dp", "tensor"),
            P("dp", "tensor"),
            P("dp", "tensor"),
            P("tensor", "dp"),
            P("dp", "tensor"),
            P("dp", "tensor"),
            P("tensor", "dp"),
            P("dp"),
            P("dp"),
            P("dp", None),
            P("dp", ctx),
            P("dp", ctx, None),
        ),
        out_specs=(
            P("dp", ctx, None),
            P(),
            P("dp", ctx, None),
            P("dp", "tensor"),
            P("dp", "tensor"),
            P("dp", "tensor"),
            P("tensor", "dp"),
            P("dp", "tensor"),
            P("dp", "tensor"),
            P("tensor", "dp"),
            P("dp"),
            P("dp"),
        ),
        check_vma=False,
    )
```

```python
import math

import jax
import jax.numpy as jnp
from jax import lax
from jax.experimental import pallas as pl
from jax.experimental.pallas import tpu as pltpu
from jax.sharding import Mesh
from jax.sharding import PartitionSpec as P

HEAD = 64
WINDOW = 1024
BLOCK = 128
GROUP = 3
SPAN = WINDOW + BLOCK

branch_scale = 1.4 / math.sqrt(52.0)
norm_epsilon = 1e-05
masked_score = -1e30
scale_factor = 1.0 / math.sqrt(HEAD)
bf16 = jnp.bfloat16
f32 = jnp.float32


def dot(left, right):
    return jnp.dot(left, right, preferred_element_type=f32)


def dot_nt(left, right):
    return lax.dot_general(left, right, (((1,), (1,)), ((), ())), preferred_element_type=f32)


def dot_tn(left, right):
    return lax.dot_general(left, right, (((0,), (0,)), ((), ())), preferred_element_type=f32)


def z_move(value, distance):
    route = []
    for dp in range(2):
        for hi in range(2):
            z = (hi * 2 + dp + distance) % 4
            route.append((dp * 2 + hi, (z % 2) * 2 + z // 2))
    return lax.ppermute(value, ("dp", "z_hi"), route)


def ring_move(value, axis, distance):
    size = lax.axis_size(axis)
    return lax.ppermute(value, axis, [(i, (i + distance) % size) for i in range(size)])


def group_move(value, distance):
    return lax.ppermute(
        value, ("x", "z_hi"), [(i, i + distance) for i in range(8) if 0 <= i + distance < 8]
    )


def swap(value, axis):
    return lax.ppermute(value, axis, [(0, 1), (1, 0)])


PAIRS = {"even": ((0, 1), (1, 0), (2, 3), (3, 2)), "odd": ((0, 3), (3, 0), (1, 2), (2, 1))}


def pair_move(value, step):
    return lax.ppermute(value, step[0], PAIRS[step[1]])


def pair_bit(step):
    index = lax.axis_index(step[0])
    return (index // 2 + index) % 2 if step[1] == "even" else index // 2


def core_sum(part):
    return part.astype(f32) + swap(part, "tensor").astype(f32)


def z_sum(value):
    return (value.astype(f32) + swap(value, "z_hi").astype(f32)).astype(bf16)


def halves(value, step):
    bit = pair_bit(step)
    half = value.shape[0] // 2
    return (
        lax.dynamic_slice_in_dim(value, bit * half, half, 0),
        lax.dynamic_slice_in_dim(value, (1 - bit) * half, half, 0),
    )


def add_moved(keep, send, step):
    return (keep.astype(f32) + pair_move(send, step).astype(f32)).astype(bf16)


def halve(value, step):
    return add_moved(*halves(value, step), step)


def double(value, step):
    other = pair_move(value, step)
    return jnp.where(
        pair_bit(step) == 0,
        jnp.concatenate([value, other], axis=0),
        jnp.concatenate([other, value], axis=0),
    )


FIRST = (
    (("x", "even"), ("x", "odd")),
    (("x", "odd"), ("x", "even")),
    (("y", "even"), ("y", "odd")),
    (("y", "odd"), ("y", "even")),
)
SECOND = ((("y", "even"), ("y", "odd")), (("x", "even"), ("x", "odd")))


def reduce_second(channels):
    return [halve(c, FIRST[i][1]) for i, c in enumerate(channels)]


def reduce_pairs(pairs, level):
    return [halve(c, SECOND[i][level]) for i, c in enumerate(pairs)]


def reduce_rest(pairs, widths):
    at = widths[0] + widths[1]
    rows = pairs[0].shape[0]
    (total,) = copy_blocks(
        jnp.zeros((), jnp.int32),
        [
            [
                (pair, pair.shape, lambda c: (0, 0), 0, first)
                for pair, first in zip(pairs, (0, at))
            ]
        ],
        [(rows, sum(widths))],
        (),
    )
    tile = total[:, -128:]
    beside = z_move(tile, 1).astype(f32) + z_move(tile, -1).astype(f32)
    beside = jnp.concatenate([beside[:, 64:], beside[:, :64]], axis=1).astype(bf16)
    total = z_sum(total)
    total = jnp.concatenate([total[:, :-128], total[:, -128:] + beside], axis=1)
    pairs = [total[:, :at], total[:, at:]]
    for level in (1, 0):
        pairs = [double(c, SECOND[i][level]) for i, c in enumerate(pairs)]
    channels = [
        pairs[0][:, : widths[0]],
        pairs[0][:, widths[0] :],
        pairs[1][:, : widths[2]],
        pairs[1][:, widths[2] :],
    ]
    channels = [double(c, FIRST[i][1]) for i, c in enumerate(channels)]
    return [(c, pair_move(c, FIRST[i][0])) for i, c in enumerate(channels)]


def inverse_rms(source):
    return lax.rsqrt(jnp.mean(source * source, axis=-1, keepdims=True) + norm_epsilon)


def norm_backward(source, inverse, gain_vec, grad_normed):
    weighted = grad_normed * gain_vec
    grad_source = inverse * weighted - source * (inverse * inverse * inverse) * jnp.mean(
        source * weighted, axis=-1, keepdims=True
    )
    return (grad_source, grad_normed * source * inverse)


def allowed_keys(scalars, r):
    shape = (BLOCK, SPAN)
    query_pos = scalars[0] + r * BLOCK + lax.broadcasted_iota(jnp.int32, shape, 0)
    key_pos = scalars[0] + r * BLOCK - WINDOW + lax.broadcasted_iota(jnp.int32, shape, 1)
    lowest = jnp.maximum(query_pos - (WINDOW - 1), 0)
    for d in range(1, 5):
        lowest = jnp.maximum(lowest, jnp.where(query_pos >= scalars[d], scalars[d], 0))
    allowed = (key_pos >= lowest) & (key_pos <= query_pos)
    return jnp.concatenate([allowed] * (2 * GROUP), axis=0)


def low_half():
    return lax.broadcasted_iota(jnp.int32, (BLOCK, 128), 1) < HEAD


def head_rows(ref, factor):
    parts = []
    for h in range(2 * GROUP):
        g = h // GROUP
        lanes = low_half() if g == 0 else jnp.logical_not(low_half())
        columns = ref[:, h // 2 * 128 : h // 2 * 128 + 128].astype(f32)
        if h % 2 != g:
            columns = pltpu.roll(columns, HEAD, 1)
        parts.append(jnp.where(lanes, columns * factor, 0.0).astype(bf16))
    return jnp.concatenate(parts, axis=0)


def put_heads(ref, results):
    sides = []
    for h in range(2 * GROUP):
        columns = results[h * BLOCK : (h + 1) * BLOCK]
        sides.append(pltpu.roll(columns, HEAD, 1) if h % 2 != h // GROUP else columns)
    for t in range(GROUP):
        ref[:, t * 128 : (t + 1) * 128] = jnp.where(
            low_half(), sides[2 * t], sides[2 * t + 1]
        ).astype(ref.dtype)


def fill_window(window, older, newer, own):
    window[0:512] = older[...]
    window[512:1024] = newer[...]
    window[1024:1536] = own[...]


def attention_forward_kernel(scalars, q_ref, older, newer, own, *rest):
    out_ref, log_ref, window = rest[-3:]
    r = pl.program_id(0)

    @pl.when(r == 0)
    def _():
        fill_window(window, older, newer, own)

    span = pl.ds(pl.multiple_of(r * BLOCK, BLOCK), SPAN)
    keys = window[span, 0:128]
    values = window[span, 128:256]
    allowed = allowed_keys(scalars, r)
    scores = jnp.where(allowed, dot_nt(head_rows(q_ref, scale_factor), keys), masked_score)
    top = jnp.max(scores, axis=-1, keepdims=True)
    weights = jnp.exp(scores - top)
    total = jnp.sum(weights, axis=-1, keepdims=True)
    log_ref[0] = top + jnp.log(total)
    put_heads(out_ref, dot((weights * (1.0 / total)).astype(bf16), values))


def attention_backward_kernel(scalars, q_ref, g_ref, log_ref, older, newer, own, *rest):
    dq_ref, older_ref, newer_ref, own_ref, window, sums = rest[-6:]
    r = pl.program_id(0)

    @pl.when(r == 0)
    def _():
        fill_window(window, older, newer, own)
        sums[...] = jnp.zeros_like(sums)

    span = pl.ds(pl.multiple_of(r * BLOCK, BLOCK), SPAN)
    keys = window[span, 0:128]
    values = window[span, 128:256]
    allowed = allowed_keys(scalars, r)
    q6 = head_rows(q_ref, scale_factor)
    g6 = head_rows(g_ref, 1.0)
    scores = jnp.where(allowed, dot_nt(q6, keys), masked_score)
    probs = jnp.exp(scores - log_ref[0])
    grad_probs = dot_nt(g6, values)
    inner = jnp.sum(grad_probs * probs, axis=-1, keepdims=True)
    grad_scores = (probs * (grad_probs - inner)).astype(bf16)
    put_heads(dq_ref, dot(grad_scores, keys) * scale_factor)
    sums[span, 0:128] += dot_tn(grad_scores, q6)
    sums[span, 128:256] += dot_tn(probs.astype(bf16), g6)

    @pl.when(r == 3)
    def _():
        for part, ref in enumerate((older_ref, newer_ref, own_ref)):
            rows = slice(part * 512, (part + 1) * 512)
            ref[:, 0:128] = sums[rows, 0:128].astype(ref.dtype)
            ref[:, 128:256] = sums[rows, 128:256].astype(ref.dtype)


SMEM = pl.BlockSpec(memory_space=pltpu.SMEM)
UNREAD = pl.BlockSpec(memory_space=pl.ANY)
SHORT = pl.CostEstimate(flops=1000, bytes_accessed=1000, transcendentals=0)


def whole(*shape):
    return pl.BlockSpec(shape, lambda i: (0,) * len(shape))


def params(mebibytes=24):
    return pltpu.CompilerParams(vmem_limit_bytes=mebibytes * 1024 * 1024)


def copy_blocks(index, outputs, shapes, held):
    blocks = [block for output in outputs for block in output]

    def kernel(index_ref, *refs):
        outs = refs[len(blocks) + len(held) :]
        at = 0
        for output, out in zip(outputs, outs):
            for _, shape, _, row, column in output:
                out[row : row + shape[0], column : column + shape[1]] = refs[at][...]
                at += 1

    return pl.pallas_call(
        kernel,
        grid_spec=pltpu.PrefetchScalarGridSpec(
            num_scalar_prefetch=1,
            grid=(1,),
            in_specs=[
                pl.BlockSpec(block[1], lambda i, ref, place=block[2]: place(ref[0]))
                for block in blocks
            ]
            + [UNREAD] * len(held),
            out_specs=[pl.BlockSpec(shape, lambda i, ref: (0, 0)) for shape in shapes],
        ),
        out_shape=[
            jax.ShapeDtypeStruct(shape, output[0][0].dtype)
            for shape, output in zip(shapes, outputs)
        ],
        compiler_params=params(20),
        cost_estimate=SHORT,
    )(index.reshape(1), *[block[0] for block in blocks], *held)


def hold(values, *held):
    return copy_blocks(
        jnp.zeros((), jnp.int32),
        [[(v, v.shape, lambda c: (0, 0), 0, 0)] for v in values],
        [v.shape for v in values],
        held,
    )


def attention_forward(scalars, queries, pieces, held):
    return pl.pallas_call(
        attention_forward_kernel,
        grid=(4,),
        in_specs=[SMEM, pl.BlockSpec((BLOCK, 384), lambda i: (i, 0))]
        + [whole(512, 256)] * 3
        + [UNREAD] * len(held),
        out_specs=(
            pl.BlockSpec((BLOCK, 384), lambda i: (i, 0)),
            pl.BlockSpec((1, 2 * GROUP * BLOCK, 1), lambda i: (i, 0, 0)),
        ),
        out_shape=(
            jax.ShapeDtypeStruct((512, 384), bf16),
            jax.ShapeDtypeStruct((4, 2 * GROUP * BLOCK, 1), f32),
        ),
        scratch_shapes=[pltpu.VMEM((1536, 256), bf16)],
        compiler_params=params(32),
        cost_estimate=SHORT,
    )(scalars, queries, *pieces, *held)


def attention_backward(scalars, queries, grads, logs, pieces, held):
    return pl.pallas_call(
        attention_backward_kernel,
        grid=(4,),
        in_specs=[
            SMEM,
            pl.BlockSpec((BLOCK, 384), lambda i: (i, 0)),
            pl.BlockSpec((BLOCK, 384), lambda i: (i, 0)),
            pl.BlockSpec((1, 2 * GROUP * BLOCK, 1), lambda i: (i, 0, 0)),
        ]
        + [whole(512, 256)] * 3
        + [UNREAD] * len(held),
        out_specs=(
            pl.BlockSpec((BLOCK, 384), lambda i: (i, 0)),
            whole(512, 256),
            whole(512, 256),
            whole(512, 256),
        ),
        out_shape=(
            jax.ShapeDtypeStruct((512, 384), bf16),
            jax.ShapeDtypeStruct((512, 256), bf16),
            jax.ShapeDtypeStruct((512, 256), bf16),
            jax.ShapeDtypeStruct((512, 256), f32),
        ),
        scratch_shapes=[pltpu.VMEM((1536, 256), bf16), pltpu.VMEM((1536, 256), f32)],
        compiler_params=params(32),
        cost_estimate=SHORT,
    )(scalars, queries, grads, logs, *pieces, *held)


TILE = 384
TOKENS = 16384
CHUNKS = ((0, 1024), (1024, 1920))


def weight_copies(refs, gate, up, down, sems):
    copies = {"gate": [], "up": [], "down": []}

    def add(group, source, target):
        count = sum(len(entries) for entries in copies.values())
        copies[group].append(pltpu.make_async_copy(source, target, sems.at[count]))

    for group, target, at in (("gate", gate, 0), ("up", up, 5)):
        if target is None:
            continue
        add(group, refs[at], target.at[pl.ds(0, 768), :])
        for k in range(4):
            add(
                group,
                refs[at + 1 + k].at[:, pl.ds(0, 1920)],
                target.at[pl.ds(768 + 192 * k, 192), :],
            )
    add("down", refs[10], down.at[:, pl.ds(0, 768)])
    for side in range(2):
        for b in range(5):
            rows = pl.ds(960 * side + 192 * b, 192)
            add(
                "down",
                refs[6 + side].at[:, pl.ds(1920 + 384 * b, 384)],
                down.at[rows, pl.ds(768, 384)],
            )
            add(
                "down",
                refs[11 + side].at[:, pl.ds(384 * b, 384)],
                down.at[rows, pl.ds(1152, 384)],
            )
    return copies


def weight_operands(w_gate, w_up, w_down, one, two):
    return [w_gate, *one[0], *one[1], w_up, *two[0], *two[1], w_down, *two[2]]


WEIGHT_SCRATCH = [
    pltpu.VMEM((1536, 1920), bf16),
    pltpu.VMEM((1536, 1920), bf16),
    pltpu.VMEM((1920, 1536), bf16),
    pltpu.SemaphoreType.DMA((31,)),
]


def start_all(copies, order):
    for group in order:
        for copy in copies[group]:
            copy.start()


def wait_all(copies):
    for copy in copies:
        copy.wait()


def gate_kernel(x_ref, own, moved, gain, *refs):
    h_ref, n_ref, r_ref, g_ref, gate, sems = refs[5:]
    copies = [pltpu.make_async_copy(refs[0], gate.at[pl.ds(0, 768), :], sems.at[0])]
    for k in range(4):
        copies.append(
            pltpu.make_async_copy(
                refs[1 + k].at[:, pl.ds(0, 1920)],
                gate.at[pl.ds(768 + 192 * k, 192), :],
                sems.at[1 + k],
            )
        )
    for copy in copies:
        copy.start()
    hidden = x_ref[...] + branch_scale * (own[...].astype(f32) + moved[...].astype(f32))
    inverse = inverse_rms(hidden)
    h_ref[...] = hidden
    r_ref[...] = inverse
    n_ref[...] = (hidden * inverse * gain[...]).astype(bf16)
    wait_all(copies)
    for a, b in CHUNKS:
        g_ref[:, a:b] = dot(n_ref[...], gate[:, a:b])


def ffn_forward_kernel(n_ref, g_hbm, *refs):
    u_ref, a_ref, out_ref, up, down, sems, g_ref, more = refs[13:]
    copies = weight_copies(refs[:13], None, up, down, sems)
    copies["pre"] = [pltpu.make_async_copy(g_hbm, g_ref, more.at[0])]
    start_all(copies, ("up", "pre", "down"))
    wait_all(copies["up"])
    wait_all(copies["pre"])
    for a, b in CHUNKS:
        up_pre = dot(n_ref[...], up[:, a:b])
        u_ref[:, a:b] = up_pre
        gate_pre = g_ref[:, a:b]
        a_ref[:, a:b] = (gate_pre * jax.nn.sigmoid(gate_pre) * up_pre).astype(bf16)
    wait_all(copies["down"])
    out_ref[...] = dot(a_ref[...], down[...]).astype(bf16)


def ffn_backward_kernel(b_ref, g_hbm, u_hbm, *refs):
    weights = refs[:13]
    gg_ref, gu_ref, out_ref, gate, up, down, sems, g_ref, u_ref, more = refs[-10:]
    copies = weight_copies(weights, gate, up, down, sems)
    copies["pre"] = [
        pltpu.make_async_copy(g_hbm, g_ref, more.at[0]),
        pltpu.make_async_copy(u_hbm, u_ref, more.at[1]),
    ]
    start_all(copies, ("down", "pre", "gate", "up"))
    wait_all(copies["down"])
    wait_all(copies["pre"])
    for a, b in CHUNKS:
        grad = dot_nt(b_ref[...], down[a:b, :]).astype(bf16).astype(f32)
        gate_pre, up_pre = g_ref[:, a:b], u_ref[:, a:b]
        sigmoid = jax.nn.sigmoid(gate_pre)
        gg_ref[:, a:b] = (
            grad * up_pre * sigmoid * (1.0 + gate_pre * (1.0 - sigmoid))
        ).astype(bf16)
        gu_ref[:, a:b] = (grad * gate_pre * sigmoid).astype(bf16)
    wait_all(copies["gate"])
    part = dot_nt(gg_ref[...], gate[...])
    wait_all(copies["up"])
    out_ref[...] = (part + dot_nt(gu_ref[...], up[...])).astype(bf16)


def gate_forward(residual, own, moved, gain, w_gate, first):
    rows, width = residual.shape
    hidden = w_gate.shape[1]
    operands = [w_gate, *first[0], *first[1]]
    shapes = [((rows, width), f32), ((rows, width), bf16), ((rows, 1), f32), ((rows, hidden), f32)]
    return pl.pallas_call(
        gate_kernel,
        grid=(1,),
        in_specs=[whole(rows, width)] * 3 + [whole(1, width)] + [UNREAD] * len(operands),
        out_specs=[whole(*shape) for shape, _ in shapes],
        out_shape=[jax.ShapeDtypeStruct(*entry) for entry in shapes],
        scratch_shapes=[pltpu.VMEM((1536, 1920), bf16), pltpu.SemaphoreType.DMA((5,))],
        compiler_params=params(24),
        cost_estimate=SHORT,
    )(residual, own, moved, gain.reshape(1, width), *operands)


def ffn_forward(normed, gate_pre, weights):
    rows, width = normed.shape
    operands = weight_operands(*weights)
    hidden = gate_pre.shape[1]
    shapes = [((rows, hidden), f32), ((rows, hidden), bf16), ((rows, width), bf16)]
    return pl.pallas_call(
        ffn_forward_kernel,
        grid=(1,),
        in_specs=[whole(rows, width)] + [UNREAD] * (1 + len(operands)),
        out_specs=[whole(*shape) for shape, _ in shapes],
        out_shape=[jax.ShapeDtypeStruct(*entry) for entry in shapes],
        scratch_shapes=WEIGHT_SCRATCH[1:]
        + [pltpu.VMEM((rows, hidden), f32), pltpu.SemaphoreType.DMA((1,))],
        compiler_params=params(38),
        cost_estimate=SHORT,
    )(normed, gate_pre, *operands)


def ffn_backward(branch, gate_pre, up_pre, weights, held):
    rows, width = branch.shape
    operands = weight_operands(*weights)
    hidden = weights[2].shape[0]
    shapes = [((rows, hidden), bf16), ((rows, hidden), bf16), ((rows, width), bf16)]
    return pl.pallas_call(
        ffn_backward_kernel,
        grid=(1,),
        in_specs=[whole(rows, width)] + [UNREAD] * (2 + len(operands) + len(held)),
        out_specs=[whole(*shape) for shape, _ in shapes],
        out_shape=[jax.ShapeDtypeStruct(*entry) for entry in shapes],
        scratch_shapes=WEIGHT_SCRATCH
        + [pltpu.VMEM((rows, hidden), f32)] * 2
        + [pltpu.SemaphoreType.DMA((2,))],
        compiler_params=params(44),
        cost_estimate=SHORT,
    )(branch, gate_pre, up_pre, *operands, *held)


def hidden_tile(rows):
    return pl.BlockSpec((rows, TILE), lambda i: (0, i))


def projection_kernel(n_own, n_other, wq, wk, wv, one, two, *rest):
    out_ref = rest[-1]
    own = n_own[...]
    first, second = n_other[:, :384], n_other[:, 384:]
    rows = own.shape[0]
    for p in range(2):
        place = pl.ds(p * rows, rows)
        q_at, kv_at = slice(p * 384, p * 384 + 384), slice(p * 128, p * 128 + 128)
        for weight, own_at, at, out_at in (
            (wq, q_at, p * 384, slice(0, 384)),
            (wk, kv_at, 768 + p * 128, slice(384, 512)),
            (wv, kv_at, 1024 + p * 128, slice(512, 640)),
        ):
            there = slice(at, at + out_at.stop - out_at.start)
            out_ref[place, out_at] = (
                dot(own, weight[:, own_at])
                + dot(first, one[:, there])
                + dot(second, two[:, there])
            ).astype(bf16)


def projection_backward_kernel(colour, g_ref, wq, wk, wv, one, two, *rest):
    out_ref = rest[-1]
    grad = jnp.concatenate(
        [
            g_ref[:, a:b]
            for a, b in ((0, 384), (640, 1024), (384, 512), (1024, 1152), (512, 640), (1152, 1280))
        ],
        axis=1,
    )
    out_ref[:, 0:768] = (
        dot_nt(grad[:, 0:768], wq[...])
        + dot_nt(grad[:, 768:1024], wk[...])
        + dot_nt(grad[:, 1024:1280], wv[...])
    ).astype(bf16)
    first = dot_nt(grad, one[...]).astype(bf16)
    second = dot_nt(grad, two[...]).astype(bf16)

    @pl.when(colour[0] == 0)
    def _():
        out_ref[:, 768:1152] = first
        out_ref[:, 1152:1536] = second

    @pl.when(colour[0] != 0)
    def _():
        out_ref[:, 768:1152] = second
        out_ref[:, 1152:1536] = first


def projection_backward(colour, held, *operands):
    rows = operands[0].shape[0]
    return pl.pallas_call(
        projection_backward_kernel,
        grid=(1,),
        in_specs=[SMEM] + [whole(*operand.shape) for operand in operands] + [UNREAD] * len(held),
        out_specs=whole(rows, 1536),
        out_shape=jax.ShapeDtypeStruct((rows, 1536), bf16),
        compiler_params=params(),
        cost_estimate=SHORT,
    )(colour.reshape(1), *operands, *held)


def out_blocks(pieces):
    operands = [piece for piece in pieces for _ in range(2)]
    specs = [pl.BlockSpec((192, 384), lambda i, k=k: (0, k)) for k in (5, 6)] * 4
    return operands, specs


def out_columns(refs):
    return jnp.concatenate([ref[...] for ref in refs], axis=0)


def out_projection_kernel(back_ref, w_ref, *refs):
    part_ref, attended_ref = refs[-2:]
    rows = attended_ref.shape[0]
    attended = jnp.concatenate([back_ref[0:rows], back_ref[rows : 2 * rows]], axis=1)
    attended_ref[...] = attended
    part_ref[:, 0:768] = dot(attended, w_ref[...]).astype(bf16)
    part_ref[:, 768:1152] = dot(attended, out_columns(refs[0:4])).astype(bf16)
    part_ref[:, 1152:1536] = dot(attended, out_columns(refs[4:8])).astype(bf16)


def out_projection(back, w_out, pieces, held):
    rows = back.shape[0] // 2
    operands, specs = out_blocks(pieces)
    return pl.pallas_call(
        out_projection_kernel,
        grid=(1,),
        in_specs=[whole(*back.shape), whole(*w_out.shape)] + specs + [UNREAD] * len(held),
        out_specs=(whole(rows, 1536), whole(rows, 768)),
        out_shape=(
            jax.ShapeDtypeStruct((rows, 1536), bf16),
            jax.ShapeDtypeStruct((rows, 768), bf16),
        ),
        compiler_params=params(),
        cost_estimate=SHORT,
    )(back, w_out, *operands, *held)


def out_backward_kernel(b_ref, w_ref, *refs):
    out_ref = refs[-1]
    rows = b_ref.shape[0]
    grad = (
        dot_nt(b_ref[:, 0:768], w_ref[...])
        + dot_nt(b_ref[:, 768:1152], out_columns(refs[0:4]))
        + dot_nt(b_ref[:, 1152:1536], out_columns(refs[4:8]))
    ).astype(bf16)
    out_ref[0:rows] = grad[:, 0:384]
    out_ref[rows : 2 * rows] = grad[:, 384:768]


def out_backward(branch, w_out, pieces):
    rows = branch.shape[0]
    operands, specs = out_blocks(pieces)
    return pl.pallas_call(
        out_backward_kernel,
        grid=(1,),
        in_specs=[whole(*branch.shape), whole(*w_out.shape)] + specs,
        out_specs=whole(2 * rows, 384),
        out_shape=jax.ShapeDtypeStruct((2 * rows, 384), bf16),
        compiler_params=params(),
        cost_estimate=SHORT,
    )(branch, w_out, *operands)


def projection(*operands):
    rows = operands[0].shape[0]
    return pl.pallas_call(
        projection_kernel,
        in_specs=[pl.BlockSpec(memory_space=pltpu.VMEM)] * 7 + [UNREAD] * (len(operands) - 7),
        out_shape=jax.ShapeDtypeStruct((2 * rows, 640), bf16),
        compiler_params=params(),
        cost_estimate=SHORT,
    )(*operands)


def merge_kernel(q_ref, own, newer, older, *rest):
    out_ref = rest[-1]
    out_ref[:, 0:384] = q_ref[...]
    out_ref[:, 384:640] = (
        own[...] + newer[...].astype(f32) + older[...].astype(f32)
    ).astype(bf16)


def merge(grad_queries, own, newer, older, held):
    operands = (grad_queries, own, newer, older)
    return pl.pallas_call(
        merge_kernel,
        grid=(1,),
        in_specs=[whole(*operand.shape) for operand in operands] + [UNREAD] * len(held),
        out_specs=whole(512, 640),
        out_shape=jax.ShapeDtypeStruct((512, 640), bf16),
        compiler_params=params(),
        cost_estimate=SHORT,
    )(*operands, *held)


def ffn_gradients_kernel(normed, branch, gate, up, act, m_one, m_two, l_one, l_two, *rest):
    out_ref, n_all, b_all, gate_all, up_all, act_all, total, in_sems, out_sems = rest[-9:]
    rows, width, hidden = 256, 768, 1920
    copies = {}
    for name, own, received, at, target in (
        ("normed", normed, (m_one, m_two), 0, n_all),
        ("gate", gate, (l_one, l_two), width, gate_all),
        ("up", up, (l_one, l_two), width + hidden, up_all),
        ("act", act, (m_one, m_two), width, act_all),
        ("branch", branch, (l_one, l_two), 0, b_all),
    ):
        columns = target.shape[1]
        parts = [(own.at[:, pl.ds(0, columns)], target.at[pl.ds(0, rows), :])]
        for k, part in enumerate(received):
            parts.append(
                (
                    part.at[:, pl.ds(at, columns)],
                    target.at[pl.ds(rows + 128 * k, 128), :],
                )
            )
        base = 3 * len(copies)
        copies[name] = [
            pltpu.make_async_copy(source, place, in_sems.at[base + k])
            for k, (source, place) in enumerate(parts)
        ]
        for copy in copies[name]:
            copy.start()

    def send(k):
        place = pl.ds(k * width, width)
        copy = pltpu.make_async_copy(total.at[place, :], out_ref.at[place, :], out_sems.at[k])
        copy.start()
        return copy

    wait_all(copies["normed"])
    wait_all(copies["gate"])
    for a, b in CHUNKS:
        total[0:width, a:b] = dot_tn(n_all[...], gate_all[:, a:b]).astype(bf16)
    sent = [send(0)]
    wait_all(copies["up"])
    for a, b in CHUNKS:
        total[width : 2 * width, a:b] = dot_tn(n_all[...], up_all[:, a:b]).astype(bf16)
    sent.append(send(1))
    wait_all(copies["act"])
    wait_all(copies["branch"])
    for a, b in CHUNKS:
        down = dot_tn(act_all[:, a:b], b_all[...]).astype(bf16)
        for r in range(width // 128):
            for c in range((b - a) // 128):
                total[
                    2 * width + r * 128 : 2 * width + r * 128 + 128, a + c * 128 : a + c * 128 + 128
                ] = down[c * 128 : c * 128 + 128, r * 128 : r * 128 + 128]
    sent.append(send(2))
    wait_all(sent)


def ffn_gradients(normed, branch, gate, up, act, middle, late, held):
    operands = (normed, branch, gate, up, act, *middle, *late, *held)
    return pl.pallas_call(
        ffn_gradients_kernel,
        grid=(1,),
        in_specs=[UNREAD] * len(operands),
        out_specs=pl.BlockSpec(memory_space=pltpu.HBM),
        out_shape=jax.ShapeDtypeStruct((2304, 1920), bf16),
        scratch_shapes=[pltpu.VMEM((512, 768), bf16)] * 2
        + [pltpu.VMEM((512, 1920), bf16)] * 3
        + [
            pltpu.VMEM((2304, 1920), bf16),
            pltpu.SemaphoreType.DMA((15,)),
            pltpu.SemaphoreType.DMA((3,)),
        ],
        compiler_params=params(40),
        cost_estimate=SHORT,
    )(*operands)


CHANNELS = (0, 640, 1152, 1664, 2176)


def attention_gradients_kernel(bits, *refs):
    normed, projected, attended, branch = refs[0:4]
    early, last, branch_moved = refs[4:6], refs[6:8], refs[8:10]
    outs, total = refs[11:-1], refs[-1]
    total[:, 2048:2176] = refs[10][...]

    def rows_of(own, received, at, width):
        parts = [own[:, :width]] + [ref[:, at : at + width] for ref in received]
        return jnp.concatenate(parts, axis=0)

    total[:, 0:768] = dot_tn(
        rows_of(attended, early, 768, 768), rows_of(branch, branch_moved, 0, 768)
    ).astype(bf16)
    total[:, 768:2048] = dot_tn(
        rows_of(normed, early, 0, 768), rows_of(projected, last, 0, 1280)
    ).astype(bf16)
    for c in range(4):
        columns = slice(CHANNELS[c], CHANNELS[c + 1])
        keep = pl.multiple_of(bits[c] * 384, 384)
        send = pl.multiple_of(384 - bits[c] * 384, 384)
        outs[2 * c][...] = total[pl.ds(keep, 384), columns]
        outs[2 * c + 1][...] = total[pl.ds(send, 384), columns]


def attention_gradients(bits, *operands):
    widths = [b - a for a, b in zip(CHANNELS[:-1], CHANNELS[1:]) for _ in range(2)]
    return list(
        pl.pallas_call(
            attention_gradients_kernel,
            grid=(1,),
            in_specs=[SMEM] + [whole(*operand.shape) for operand in operands],
            out_specs=[whole(384, w) for w in widths],
            out_shape=[jax.ShapeDtypeStruct((384, w), bf16) for w in widths],
            scratch_shapes=[pltpu.VMEM((768, 2176), bf16)],
            compiler_params=params(),
            cost_estimate=SHORT,
        )(bits, *operands)
    )


def ffn_results_kernel(one, two, total_hbm, *refs):
    outs, total, f_gate, f_up, f_down, in_sems, out_sems = refs[0:3], *refs[3:]
    width, hidden = 768, 1920
    targets = (f_gate, f_up, f_down)
    chunks = []
    for m in range(2):
        for r in range(2):
            place = pl.ds(m * width + r * 384, 384)
            chunks.append((m, r, (place, pl.ds(0, hidden)), (pl.ds(r * 384, 384), pl.ds(0, hidden))))
    for r, (a, b) in enumerate(CHUNKS):
        place = (pl.ds(2 * width, width), pl.ds(a, b - a))
        chunks.append((2, r, place, (pl.ds(a, b - a), pl.ds(0, width))))
    arriving, leaving = [], []
    for k, (_, _, place, _) in enumerate(chunks):
        arriving.append(
            pltpu.make_async_copy(total_hbm.at[place], total.at[place], in_sems.at[k])
        )
        arriving[-1].start()
    scale = TOKENS / count_of(one, two)
    for k, (m, r, _, there) in enumerate(chunks):
        arriving[k].wait()
        if m < 2:
            rows = slice(r * 384, r * 384 + 384)
            source = slice(m * width + r * 384, m * width + r * 384 + 384)
            targets[m][rows] = total[source].astype(f32) * scale
        else:
            a, b = CHUNKS[r]
            for p in range(a // 128, b // 128):
                for q in range(width // 128):
                    f_down[p * 128 : p * 128 + 128, q * 128 : q * 128 + 128] = (
                        total[
                            2 * width + q * 128 : 2 * width + q * 128 + 128,
                            p * 128 : p * 128 + 128,
                        ].astype(f32)
                        * scale
                    )
        leaving.append(
            pltpu.make_async_copy(targets[m].at[there], outs[m].at[there], out_sems.at[k])
        )
        leaving[-1].start()
    wait_all(leaving)


def ffn_results(pair, total):
    width, hidden = total.shape[0] // 3, total.shape[1]
    shapes = ((width, hidden), (width, hidden), (hidden, width))
    hbm = pl.BlockSpec(memory_space=pltpu.HBM)
    return pl.pallas_call(
        ffn_results_kernel,
        grid=(1,),
        in_specs=[whole(*value.shape) for value in pair] + [hbm],
        out_specs=[hbm] * 3,
        out_shape=[jax.ShapeDtypeStruct(shape, f32) for shape in shapes],
        scratch_shapes=[pltpu.VMEM(total.shape, bf16)]
        + [pltpu.VMEM(shape, f32) for shape in shapes]
        + [pltpu.SemaphoreType.DMA((6,)), pltpu.SemaphoreType.DMA((6,))],
        compiler_params=params(58),
        cost_estimate=SHORT,
    )(*pair, total)


PLACES = (
    (0, 0, 640, 3, 0),
    (1, 0, 128, 3, 640),
    (1, 128, 384, 0, 0),
    (2, 0, 128, 1, 0),
    (2, 128, 128, 2, 0),
    (2, 256, 256, 0, 384),
    (3, 0, 128, 0, 640),
    (3, 128, 128, 1, 128),
    (3, 256, 128, 2, 128),
)


def count_of(ref_one, ref_two):
    total = None
    for ref in (ref_one, ref_two):
        for lane in (32, 96):
            part = jnp.sum(ref[:, 384 + lane : 385 + lane].astype(f32), axis=0, keepdims=True)
            total = part if total is None else total + part
    return total


def attention_results_kernel(bits, *refs):
    outs, rows_ref, tile = refs[8:12], refs[12], refs[13]
    count = count_of(refs[6], refs[7])
    scale = TOKENS / count
    for c, at, width, out, there in PLACES:
        for side in range(2):
            first = bits[c] * 384 if side == 0 else 384 - bits[c] * 384
            outs[out][pl.ds(pl.multiple_of(first, 384), 384), there : there + width] = (
                refs[2 * c + side][:, at : at + width].astype(f32) * scale
            )
    for side in range(2):
        first = bits[3] * 384 if side == 0 else 384 - bits[3] * 384
        tile[pl.ds(pl.multiple_of(first, 384), 384), :] = refs[6 + side][:, 384:512].astype(f32)
    lines = jnp.transpose(tile[...])
    rows_ref[0:1] = (lines[0:1] + lines[72:73]) * scale
    rows_ref[1:2] = (lines[16:17] + lines[88:89]) * scale
    squares = jnp.sum(lines[40:41] + lines[104:105], axis=1, keepdims=True)
    rows_ref[2:3] = jnp.broadcast_to(squares / count, (1, 768))
    rows_ref[3:4] = jnp.broadcast_to(scale, (1, 768))


def attention_results(bits, pairs):
    operands = [value for pair in pairs for value in pair]
    widths = (768, 256, 256, 768)
    return pl.pallas_call(
        attention_results_kernel,
        grid=(1,),
        in_specs=[SMEM] + [whole(*operand.shape) for operand in operands],
        out_specs=[whole(768, width) for width in widths] + [whole(8, 768)],
        out_shape=[jax.ShapeDtypeStruct((768, width), f32) for width in widths]
        + [jax.ShapeDtypeStruct((8, 768), f32)],
        scratch_shapes=[pltpu.VMEM((768, 128), f32)],
        compiler_params=params(),
        cost_estimate=SHORT,
    )(bits, *operands)


def local(
    tokens,
    w_query,
    key_projection_weight,
    value_projection_weight,
    w_out,
    w_gate,
    w_up,
    w_down,
    norm_attn,
    norm_ffn,
    doc_lengths,
    valid_mask,
    teacher,
):
    seq_count, row_count, width = tokens.shape
    rows = seq_count * row_count
    half = width // 2
    quarter = width // 4
    dp = lax.axis_index("dp")
    colour = (lax.axis_index("x") + lax.axis_index("y")) % 2
    y_index = lax.axis_index("y")
    group_index = lax.axis_index("x") * 2 + lax.axis_index("z_hi")

    def to_local(value):
        own = jnp.where(dp == 0, value[..., :half], value[..., half:])
        other = jnp.where(dp == 0, value[..., half:], value[..., :half])
        first = jnp.where(colour == 0, other[..., :quarter], other[..., quarter:])
        second = jnp.where(colour == 0, other[..., quarter:], other[..., :quarter])
        return jnp.concatenate([own, first, second], axis=-1)

    def other_half_of(first, second):
        return jnp.concatenate(
            [jnp.where(colour == 0, first, second), jnp.where(colour == 0, second, first)], axis=-1
        )

    def other_half(value):
        return other_half_of(value[..., half : half + quarter], value[..., half + quarter :])

    def from_local(value):
        own, other = value[..., :half], other_half(value)
        return jnp.concatenate(
            [jnp.where(dp == 0, own, other), jnp.where(dp == 0, other, own)], axis=-1
        )

    def two_ways(first, second):
        return z_move(first, 1), z_move(second, -1)

    def over_x(one, two):
        return ring_move(one, "x", 1), ring_move(two, "x", -1)

    def over_y(one, two):
        return ring_move(one, "y", 1), ring_move(two, "y", -1)

    def to_neighbours(value):
        return two_ways(value[:row_count], value[row_count:])

    gains = jnp.stack([norm_attn, norm_ffn])
    gains_other = swap(gains, "dp")
    gains_first = jnp.where(colour == 0, gains_other[:, :quarter], gains_other[:, quarter:])
    gains_second = jnp.where(colour == 0, gains_other[:, quarter:], gains_other[:, :quarter])
    gains_full = jnp.concatenate([gains, gains_first, gains_second], axis=1).astype(f32)
    gain_one, gain_two = gains_full[0], gains_full[1]

    kv = key_projection_weight.shape[1]
    ff = w_gate.shape[1]
    sent = copy_blocks(
        colour,
        [
            [
                (w_query, (quarter, half), lambda c, k=k: (k, 0), 0, 0),
                (key_projection_weight, (quarter, kv), lambda c, k=k: (k, 0), 0, half),
                (value_projection_weight, (quarter, kv), lambda c, k=k: (k, 0), 0, half + kv),
            ]
            for k in range(2)
        ],
        [(quarter, half + 2 * kv)] * 2,
        (gains_other,),
    )
    qkv_one, qkv_two = two_ways(*sent)
    mask_values = valid_mask.reshape(rows).astype(f32)
    blocks = [
        [
            (w_gate, (192, ff), lambda c, k=k: (2 * c + k, 0), 0, 0),
            (w_out, (192, quarter), lambda c, k=k: (2 * k, c), 0, ff),
            (w_out, (192, quarter), lambda c, k=k: (2 * k + 1, c), 0, ff + quarter),
        ]
        for k in range(2)
    ]
    first_sent = copy_blocks(colour, blocks, [(192, ff + 2 * quarter)] * 2, (gains_other,))
    first_z = two_ways(*first_sent)

    residual_in = to_local(tokens.reshape(rows, width)).astype(f32)
    inverse_one = inverse_rms(residual_in)
    normed_one = (residual_in * inverse_one * gain_one).astype(bf16)
    normed_one_other = other_half(normed_one)
    projected = projection(
        normed_one[:, :half],
        normed_one_other,
        w_query,
        key_projection_weight,
        value_projection_weight,
        qkv_one,
        qkv_two,
        *first_sent,
    )
    mine = lax.all_to_all(projected, "y", 0, 0, tiled=True)
    queries, key_values = copy_blocks(
        colour,
        [
            [(mine, (512, 128), lambda c, k=k: (0, k), 0, 128 * (k - first)) for k in range(first, last)]
            for first, last in ((0, 3), (3, 5))
        ],
        [(512, 384), (512, 256)],
        (),
    )
    pieces = (group_move(key_values, 2), group_move(key_values, 1), key_values)
    blocks = [
        [(w_up, (192, ff), lambda c, k=k: (2 * c + k, 0), 0, 0)]
        + [
            (w_down, (192, quarter), lambda c, k=k, b=b: (5 * k + b, c), 0, ff + quarter * b)
            for b in range(5)
        ]
        for k in range(2)
    ]
    second_z = two_ways(*copy_blocks(colour, blocks, [(192, 2 * ff)] * 2, pieces[:2]))
    first = (first_z, over_x(*hold(first_z, pieces[0])))
    bounds = jnp.cumsum(lax.dynamic_index_in_dim(doc_lengths, y_index % 2, 0, keepdims=False))
    scalars = jnp.concatenate([(group_index * 512)[None], bounds]).astype(jnp.int32)
    attended_mine, logs = attention_forward(scalars, queries, pieces, ())
    returned = lax.all_to_all(attended_mine, "y", 0, 0, tiled=True)
    out_pieces = (*first[0], *first[1])
    attn_part, attended = out_projection(returned, w_out, out_pieces, ())
    split = copy_blocks(
        colour,
        [[(v, (192, ff), lambda c, k=k: (0, k), 0, 0)] for k in range(2) for v in second_z],
        [(192, ff)] * 4,
        (attn_part,),
    )
    second = (second_z, over_x(*split[:2]), over_y(*split[2:]))
    early = to_neighbours(jnp.concatenate([normed_one_other, attended], axis=1))
    weights = (w_gate, w_up, w_down, first, second)
    hidden_state, normed_two, inverse_two, gate_pre = gate_forward(
        residual_in, attn_part, swap(attn_part, "tensor"), gain_two, w_gate, first
    )
    up_pre, activated, ffn_part = ffn_forward(normed_two, gate_pre, weights)
    middle = to_neighbours(jnp.concatenate([other_half(normed_two), activated], axis=1))

    final_state = hidden_state + branch_scale * core_sum(ffn_part)
    deviation = final_state - to_local(teacher.reshape(rows, width)).astype(f32)
    row_squares = mask_values * jnp.mean(deviation * deviation, axis=-1)
    grad_final = deviation * mask_values[:, None]
    branch_two = (branch_scale * grad_final).astype(bf16)
    grad_gate_pre, grad_up_pre, part = ffn_backward(branch_two, gate_pre, up_pre, weights, early[1:])
    late = to_neighbours(
        jnp.concatenate([other_half(branch_two), grad_gate_pre, grad_up_pre], axis=1)
    )
    grad_normed_two = core_sum(part)

    grad_from_norm, gain_terms_two = norm_backward(
        hidden_state, inverse_two, gain_two, grad_normed_two
    )
    grad_hidden = grad_final + grad_from_norm
    branch_one = (branch_scale * grad_hidden).astype(bf16)
    grad_attended = out_backward(branch_one, w_out, out_pieces)
    branch_moved = to_neighbours(other_half(branch_one))
    grad_mine = lax.all_to_all(grad_attended, "y", 0, 0, tiled=True)
    grad_queries, grad_older, grad_newer, grad_own = attention_backward(
        scalars, queries, grad_mine, logs, pieces, ()
    )
    ffn_grads = ffn_gradients(
        normed_two, branch_two, grad_gate_pre, grad_up_pre, activated, middle, late, (grad_older,)
    )
    ffn_share = lax.psum_scatter(ffn_grads, ("x", "y"), scatter_dimension=0, tiled=True)
    older = group_move(grad_older, -2)
    newer = group_move(grad_newer, -1)
    grad_projected = lax.all_to_all(
        merge(grad_queries, grad_own, newer, older, branch_moved), "y", 0, 0, tiled=True
    )
    grad_projected = jnp.concatenate([grad_projected[:rows], grad_projected[rows:]], axis=1)
    last = to_neighbours(grad_projected)
    grad_normed_one = core_sum(
        projection_backward(
            colour,
            early[:1],
            grad_projected,
            w_query,
            key_projection_weight,
            value_projection_weight,
            qkv_one,
            qkv_two,
        )
    )
    gradient_via_first_norm, gain_terms_one = norm_backward(
        residual_in, inverse_one, gain_one, grad_normed_one
    )
    grad_tokens = from_local(grad_hidden + gradient_via_first_norm)

    ones = jnp.ones((rows, 128), f32)

    def column_sums(terms):
        return lax.dot_general(
            terms, ones, (((0,), (0,)), ((), ())), precision=lax.Precision.HIGHEST
        )

    def on_rows(values):
        return jnp.pad(jnp.broadcast_to(values[:, None], (rows, 128)), ((0, half - rows), (0, 0)))

    entries = [
        column_sums(gain_terms_one[:, :half]),
        column_sums(other_half(gain_terms_one)),
        column_sums(gain_terms_two[:, :half]),
        column_sums(other_half(gain_terms_two)),
        on_rows(mask_values),
        on_rows(row_squares),
    ]
    slot = lax.broadcasted_iota(jnp.int32, (half, 128), 1) // 8
    tile = jnp.zeros((half, 128), f32)
    for k, entry in enumerate(entries):
        tile = jnp.where(slot == k, entry, tile)
    bits = jnp.stack([pair_bit(steps[0]) for steps in FIRST]).astype(jnp.int32)
    cut_rows = attention_gradients(
        bits,
        normed_one,
        grad_projected,
        attended,
        branch_one,
        *early,
        *last,
        *branch_moved,
        tile.astype(bf16),
    )
    channels = [
        add_moved(cut_rows[2 * k], cut_rows[2 * k + 1], FIRST[k][0]) for k in range(4)
    ]
    (ffn_share,) = hold([ffn_share], *channels)
    channels = reduce_second(channels)
    pairs = [
        copy_blocks(
            colour,
            [
                [
                    (left, left.shape, lambda c: (0, 0), 0, 0),
                    (right, right.shape, lambda c: (0, 0), 0, left.shape[1]),
                ]
            ],
            [(left.shape[0], left.shape[1] + right.shape[1])],
            held,
        )[0]
        for left, right, held in (
            (channels[0], channels[1], (ffn_share,)),
            (channels[2], channels[3], (ffn_share,)),
        )
    ]
    ffn_share = z_sum(ffn_share)
    pairs = reduce_pairs(pairs, 0)
    (ffn_share,) = hold([ffn_share], *pairs)
    ffn_total_grads = lax.all_gather(ffn_share, ("x", "y"), axis=0, tiled=True)
    pairs = reduce_pairs(pairs, 1)
    pairs = reduce_rest(pairs, [c.shape[1] for c in channels])
    *attn_results, small = attention_results(bits, pairs)
    scale = small[3, 0]

    layer_out = from_local(final_state.astype(bf16)).reshape(seq_count, row_count, width)
    return (
        layer_out,
        small[2, 0],
        (grad_tokens * scale).reshape(seq_count, row_count, width),
        *attn_results,
        *ffn_results(pairs[3], ffn_total_grads),
        small[0],
        small[1],
    )


def solution(mesh):
    fine = Mesh(mesh.devices.reshape(2, 4, 2, 4, 2), ("dp", "x", "z_hi", "y", "tensor"))
    ctx = ("x", "z_hi", "y")
    return jax.shard_map(
        local,
        mesh=fine,
        in_specs=(
            P("dp", ctx, None),
            P("dp", "tensor"),
            P("dp", "tensor"),
            P("dp", "tensor"),
            P("tensor", "dp"),
            P("dp", "tensor"),
            P("dp", "tensor"),
            P("tensor", "dp"),
            P("dp"),
            P("dp"),
            P("dp", None),
            P("dp", ctx),
            P("dp", ctx, None),
        ),
        out_specs=(
            P("dp", ctx, None),
            P(),
            P("dp", ctx, None),
            P("dp", "tensor"),
            P("dp", "tensor"),
            P("dp", "tensor"),
            P("tensor", "dp"),
            P("dp", "tensor"),
            P("dp", "tensor"),
            P("tensor", "dp"),
            P("dp"),
            P("dp"),
        ),
        check_vma=False,
    )
```

```python
import math

import jax
import jax.numpy as jnp
from jax import lax
from jax.experimental import pallas as pl
from jax.experimental.pallas import tpu as pltpu
from jax.sharding import Mesh
from jax.sharding import PartitionSpec as P

HEAD = 64
WINDOW = 1024
BLOCK = 128
GROUP = 3
SPAN = WINDOW + BLOCK

branch_scale = 1.4 / math.sqrt(52.0)
norm_epsilon = 1e-05
masked_score = -1e30
scale_factor = 1.0 / math.sqrt(HEAD)
bf16 = jnp.bfloat16
f32 = jnp.float32


def dot(left, right):
    return jnp.dot(left, right, preferred_element_type=f32)


def dot_nt(left, right):
    return lax.dot_general(left, right, (((1,), (1,)), ((), ())), preferred_element_type=f32)


def dot_tn(left, right):
    return lax.dot_general(left, right, (((0,), (0,)), ((), ())), preferred_element_type=f32)


def z_move(value, distance):
    route = []
    for dp in range(2):
        for hi in range(2):
            z = (hi * 2 + dp + distance) % 4
            route.append((dp * 2 + hi, (z % 2) * 2 + z // 2))
    return lax.ppermute(value, ("dp", "z_hi"), route)


def ring_move(value, axis, distance):
    size = lax.axis_size(axis)
    return lax.ppermute(value, axis, [(i, (i + distance) % size) for i in range(size)])


def group_move(value, distance):
    return lax.ppermute(
        value, ("x", "z_hi"), [(i, i + distance) for i in range(8) if 0 <= i + distance < 8]
    )


def swap(value, axis):
    return lax.ppermute(value, axis, [(0, 1), (1, 0)])


PAIRS = {"even": ((0, 1), (1, 0), (2, 3), (3, 2)), "odd": ((0, 3), (3, 0), (1, 2), (2, 1))}


def pair_move(value, step):
    return lax.ppermute(value, step[0], PAIRS[step[1]])


def pair_bit(step):
    index = lax.axis_index(step[0])
    return (index // 2 + index) % 2 if step[1] == "even" else index // 2


def core_sum(part):
    return part.astype(f32) + swap(part, "tensor").astype(f32)


def z_sum(value):
    return (value.astype(f32) + swap(value, "z_hi").astype(f32)).astype(bf16)


def halves(value, step):
    bit = pair_bit(step)
    half = value.shape[0] // 2
    return (
        lax.dynamic_slice_in_dim(value, bit * half, half, 0),
        lax.dynamic_slice_in_dim(value, (1 - bit) * half, half, 0),
    )


def add_moved(keep, send, step):
    return (keep.astype(f32) + pair_move(send, step).astype(f32)).astype(bf16)


def halve(value, step):
    return add_moved(*halves(value, step), step)


def double(value, step):
    other = pair_move(value, step)
    return jnp.where(
        pair_bit(step) == 0,
        jnp.concatenate([value, other], axis=0),
        jnp.concatenate([other, value], axis=0),
    )


FIRST = (
    (("x", "even"), ("x", "odd")),
    (("x", "odd"), ("x", "even")),
    (("y", "even"), ("y", "odd")),
    (("y", "odd"), ("y", "even")),
)
SECOND = ((("y", "even"), ("y", "odd")), (("x", "even"), ("x", "odd")))


def reduce_second(channels):
    return [halve(c, FIRST[i][1]) for i, c in enumerate(channels)]


def reduce_pairs(pairs, level):
    return [halve(c, SECOND[i][level]) for i, c in enumerate(pairs)]


def reduce_rest(pairs, widths):
    at = widths[0] + widths[1]
    rows = pairs[0].shape[0]
    (total,) = copy_blocks(
        jnp.zeros((), jnp.int32),
        [
            [
                (pair, pair.shape, lambda c: (0, 0), 0, first)
                for pair, first in zip(pairs, (0, at))
            ]
        ],
        [(rows, sum(widths))],
        (),
    )
    tile = total[:, -128:]
    beside = z_move(tile, 1).astype(f32) + z_move(tile, -1).astype(f32)
    beside = jnp.concatenate([beside[:, 64:], beside[:, :64]], axis=1).astype(bf16)
    total = z_sum(total)
    total = jnp.concatenate([total[:, :-128], total[:, -128:] + beside], axis=1)
    pairs = [total[:, :at], total[:, at:]]
    for level in (1, 0):
        pairs = [double(c, SECOND[i][level]) for i, c in enumerate(pairs)]
    channels = [
        pairs[0][:, : widths[0]],
        pairs[0][:, widths[0] :],
        pairs[1][:, : widths[2]],
        pairs[1][:, widths[2] :],
    ]
    channels = [double(c, FIRST[i][1]) for i, c in enumerate(channels)]
    return [(c, pair_move(c, FIRST[i][0])) for i, c in enumerate(channels)]


def inverse_rms(source):
    return lax.rsqrt(jnp.mean(source * source, axis=-1, keepdims=True) + norm_epsilon)


def norm_backward(source, inverse, gain_vec, grad_normed):
    weighted = grad_normed * gain_vec
    grad_source = inverse * weighted - source * (inverse * inverse * inverse) * jnp.mean(
        source * weighted, axis=-1, keepdims=True
    )
    return (grad_source, grad_normed * source * inverse)


def allowed_keys(scalars, r):
    shape = (BLOCK, SPAN)
    query_pos = scalars[0] + r * BLOCK + lax.broadcasted_iota(jnp.int32, shape, 0)
    key_pos = scalars[0] + r * BLOCK - WINDOW + lax.broadcasted_iota(jnp.int32, shape, 1)
    lowest = jnp.maximum(query_pos - (WINDOW - 1), 0)
    for d in range(1, 5):
        lowest = jnp.maximum(lowest, jnp.where(query_pos >= scalars[d], scalars[d], 0))
    allowed = (key_pos >= lowest) & (key_pos <= query_pos)
    return jnp.concatenate([allowed] * (2 * GROUP), axis=0)


def low_half():
    return lax.broadcasted_iota(jnp.int32, (BLOCK, 128), 1) < HEAD


def head_rows(ref, factor):
    parts = []
    for h in range(2 * GROUP):
        g = h // GROUP
        lanes = low_half() if g == 0 else jnp.logical_not(low_half())
        columns = ref[:, h // 2 * 128 : h // 2 * 128 + 128].astype(f32)
        if h % 2 != g:
            columns = pltpu.roll(columns, HEAD, 1)
        parts.append(jnp.where(lanes, columns * factor, 0.0).astype(bf16))
    return jnp.concatenate(parts, axis=0)


def put_heads(ref, results):
    sides = []
    for h in range(2 * GROUP):
        columns = results[h * BLOCK : (h + 1) * BLOCK]
        sides.append(pltpu.roll(columns, HEAD, 1) if h % 2 != h // GROUP else columns)
    for t in range(GROUP):
        ref[:, t * 128 : (t + 1) * 128] = jnp.where(
            low_half(), sides[2 * t], sides[2 * t + 1]
        ).astype(ref.dtype)


def fill_window(window, older, newer, own):
    window[0:512] = older[...]
    window[512:1024] = newer[...]
    window[1024:1536] = own[...]


def attention_forward_kernel(scalars, q_ref, older, newer, own, *rest):
    out_ref, log_ref, window = rest[-3:]
    r = pl.program_id(0)

    @pl.when(r == 0)
    def _():
        fill_window(window, older, newer, own)

    span = pl.ds(pl.multiple_of(r * BLOCK, BLOCK), SPAN)
    keys = window[span, 0:128]
    values = window[span, 128:256]
    allowed = allowed_keys(scalars, r)
    scores = jnp.where(allowed, dot_nt(head_rows(q_ref, scale_factor), keys), masked_score)
    top = jnp.max(scores, axis=-1, keepdims=True)
    weights = jnp.exp(scores - top)
    total = jnp.sum(weights, axis=-1, keepdims=True)
    log_ref[0] = top + jnp.log(total)
    put_heads(out_ref, dot((weights * (1.0 / total)).astype(bf16), values))


def attention_backward_kernel(scalars, q_ref, g_ref, log_ref, older, newer, own, *rest):
    dq_ref, older_ref, newer_ref, own_ref, window, sums = rest[-6:]
    r = pl.program_id(0)

    @pl.when(r == 0)
    def _():
        fill_window(window, older, newer, own)
        sums[...] = jnp.zeros_like(sums)

    span = pl.ds(pl.multiple_of(r * BLOCK, BLOCK), SPAN)
    keys = window[span, 0:128]
    values = window[span, 128:256]
    allowed = allowed_keys(scalars, r)
    q6 = head_rows(q_ref, scale_factor)
    g6 = head_rows(g_ref, 1.0)
    scores = jnp.where(allowed, dot_nt(q6, keys), masked_score)
    probs = jnp.exp(scores - log_ref[0])
    grad_probs = dot_nt(g6, values)
    inner = jnp.sum(grad_probs * probs, axis=-1, keepdims=True)
    grad_scores = (probs * (grad_probs - inner)).astype(bf16)
    put_heads(dq_ref, dot(grad_scores, keys) * scale_factor)
    sums[span, 0:128] += dot_tn(grad_scores, q6)
    sums[span, 128:256] += dot_tn(probs.astype(bf16), g6)

    @pl.when(r == 3)
    def _():
        for part, ref in enumerate((older_ref, newer_ref, own_ref)):
            rows = slice(part * 512, (part + 1) * 512)
            ref[:, 0:128] = sums[rows, 0:128].astype(ref.dtype)
            ref[:, 128:256] = sums[rows, 128:256].astype(ref.dtype)


SMEM = pl.BlockSpec(memory_space=pltpu.SMEM)
UNREAD = pl.BlockSpec(memory_space=pl.ANY)
SHORT = pl.CostEstimate(flops=1000, bytes_accessed=1000, transcendentals=0)


def whole(*shape):
    return pl.BlockSpec(shape, lambda i: (0,) * len(shape))


def params(mebibytes=24):
    return pltpu.CompilerParams(vmem_limit_bytes=mebibytes * 1024 * 1024)


def copy_blocks(index, outputs, shapes, held):
    blocks = [block for output in outputs for block in output]

    def kernel(index_ref, *refs):
        outs = refs[len(blocks) + len(held) :]
        at = 0
        for output, out in zip(outputs, outs):
            for _, shape, _, row, column in output:
                out[row : row + shape[0], column : column + shape[1]] = refs[at][...]
                at += 1

    return pl.pallas_call(
        kernel,
        grid_spec=pltpu.PrefetchScalarGridSpec(
            num_scalar_prefetch=1,
            grid=(1,),
            in_specs=[
                pl.BlockSpec(block[1], lambda i, ref, place=block[2]: place(ref[0]))
                for block in blocks
            ]
            + [UNREAD] * len(held),
            out_specs=[pl.BlockSpec(shape, lambda i, ref: (0, 0)) for shape in shapes],
        ),
        out_shape=[
            jax.ShapeDtypeStruct(shape, output[0][0].dtype)
            for shape, output in zip(shapes, outputs)
        ],
        compiler_params=params(20),
        cost_estimate=SHORT,
    )(index.reshape(1), *[block[0] for block in blocks], *held)


def hold(values, *held):
    return copy_blocks(
        jnp.zeros((), jnp.int32),
        [[(v, v.shape, lambda c: (0, 0), 0, 0)] for v in values],
        [v.shape for v in values],
        held,
    )


def attention_forward(scalars, queries, pieces, held):
    return pl.pallas_call(
        attention_forward_kernel,
        grid=(4,),
        in_specs=[SMEM, pl.BlockSpec((BLOCK, 384), lambda i: (i, 0))]
        + [whole(512, 256)] * 3
        + [UNREAD] * len(held),
        out_specs=(
            pl.BlockSpec((BLOCK, 384), lambda i: (i, 0)),
            pl.BlockSpec((1, 2 * GROUP * BLOCK, 1), lambda i: (i, 0, 0)),
        ),
        out_shape=(
            jax.ShapeDtypeStruct((512, 384), bf16),
            jax.ShapeDtypeStruct((4, 2 * GROUP * BLOCK, 1), f32),
        ),
        scratch_shapes=[pltpu.VMEM((1536, 256), bf16)],
        compiler_params=params(32),
        cost_estimate=SHORT,
    )(scalars, queries, *pieces, *held)


def attention_backward(scalars, queries, grads, logs, pieces, held):
    return pl.pallas_call(
        attention_backward_kernel,
        grid=(4,),
        in_specs=[
            SMEM,
            pl.BlockSpec((BLOCK, 384), lambda i: (i, 0)),
            pl.BlockSpec((BLOCK, 384), lambda i: (i, 0)),
            pl.BlockSpec((1, 2 * GROUP * BLOCK, 1), lambda i: (i, 0, 0)),
        ]
        + [whole(512, 256)] * 3
        + [UNREAD] * len(held),
        out_specs=(
            pl.BlockSpec((BLOCK, 384), lambda i: (i, 0)),
            whole(512, 256),
            whole(512, 256),
            whole(512, 256),
        ),
        out_shape=(
            jax.ShapeDtypeStruct((512, 384), bf16),
            jax.ShapeDtypeStruct((512, 256), bf16),
            jax.ShapeDtypeStruct((512, 256), bf16),
            jax.ShapeDtypeStruct((512, 256), f32),
        ),
        scratch_shapes=[pltpu.VMEM((1536, 256), bf16), pltpu.VMEM((1536, 256), f32)],
        compiler_params=params(32),
        cost_estimate=SHORT,
    )(scalars, queries, grads, logs, *pieces, *held)


TILE = 384
TOKENS = 16384
CHUNKS = ((0, 1024), (1024, 1920))


def weight_copies(refs, gate, up, down, sems):
    copies = {"gate": [], "up": [], "down": []}

    def add(group, source, target):
        count = sum(len(entries) for entries in copies.values())
        copies[group].append(pltpu.make_async_copy(source, target, sems.at[count]))

    for group, target, at in (("gate", gate, 0), ("up", up, 5)):
        if target is None:
            continue
        add(group, refs[at], target.at[pl.ds(0, 768), :])
        for k in range(4):
            add(
                group,
                refs[at + 1 + k].at[:, pl.ds(0, 1920)],
                target.at[pl.ds(768 + 192 * k, 192), :],
            )
    add("down", refs[10], down.at[:, pl.ds(0, 768)])
    for side in range(2):
        for b in range(5):
            rows = pl.ds(960 * side + 192 * b, 192)
            add(
                "down",
                refs[6 + side].at[:, pl.ds(1920 + 384 * b, 384)],
                down.at[rows, pl.ds(768, 384)],
            )
            add(
                "down",
                refs[11 + side].at[:, pl.ds(384 * b, 384)],
                down.at[rows, pl.ds(1152, 384)],
            )
    return copies


def weight_operands(w_gate, w_up, w_down, one, two):
    return [w_gate, *one[0], *one[1], w_up, *two[0], *two[1], w_down, *two[2]]


WEIGHT_SCRATCH = [
    pltpu.VMEM((1536, 1920), bf16),
    pltpu.VMEM((1536, 1920), bf16),
    pltpu.VMEM((1920, 1536), bf16),
    pltpu.SemaphoreType.DMA((31,)),
]


def start_all(copies, order):
    for group in order:
        for copy in copies[group]:
            copy.start()


def wait_all(copies):
    for copy in copies:
        copy.wait()


def gate_kernel(x_ref, own, moved, gain, *refs):
    h_ref, n_ref, r_ref, g_ref, gate, sems = refs[5:]
    copies = [pltpu.make_async_copy(refs[0], gate.at[pl.ds(0, 768), :], sems.at[0])]
    for k in range(4):
        copies.append(
            pltpu.make_async_copy(
                refs[1 + k].at[:, pl.ds(0, 1920)],
                gate.at[pl.ds(768 + 192 * k, 192), :],
                sems.at[1 + k],
            )
        )
    for copy in copies:
        copy.start()
    hidden = x_ref[...] + branch_scale * (own[...].astype(f32) + moved[...].astype(f32))
    inverse = inverse_rms(hidden)
    h_ref[...] = hidden
    r_ref[...] = inverse
    n_ref[...] = (hidden * inverse * gain[...]).astype(bf16)
    wait_all(copies)
    for a, b in CHUNKS:
        g_ref[:, a:b] = dot(n_ref[...], gate[:, a:b])


def ffn_forward_kernel(n_ref, g_hbm, *refs):
    u_ref, a_ref, out_ref, up, down, sems, g_ref, more = refs[13:]
    copies = weight_copies(refs[:13], None, up, down, sems)
    copies["pre"] = [pltpu.make_async_copy(g_hbm, g_ref, more.at[0])]
    start_all(copies, ("up", "pre", "down"))
    wait_all(copies["up"])
    wait_all(copies["pre"])
    for a, b in CHUNKS:
        up_pre = dot(n_ref[...], up[:, a:b])
        u_ref[:, a:b] = up_pre
        gate_pre = g_ref[:, a:b]
        a_ref[:, a:b] = (gate_pre * jax.nn.sigmoid(gate_pre) * up_pre).astype(bf16)
    wait_all(copies["down"])
    out_ref[...] = dot(a_ref[...], down[...]).astype(bf16)


def ffn_backward_kernel(b_ref, g_hbm, u_hbm, *refs):
    weights = refs[:13]
    gg_ref, gu_ref, out_ref, gate, up, down, sems, g_ref, u_ref, more = refs[-10:]
    copies = weight_copies(weights, gate, up, down, sems)
    copies["pre"] = [
        pltpu.make_async_copy(g_hbm, g_ref, more.at[0]),
        pltpu.make_async_copy(u_hbm, u_ref, more.at[1]),
    ]
    start_all(copies, ("down", "pre", "gate", "up"))
    wait_all(copies["down"])
    wait_all(copies["pre"])
    for a, b in CHUNKS:
        grad = dot_nt(b_ref[...], down[a:b, :]).astype(bf16).astype(f32)
        gate_pre, up_pre = g_ref[:, a:b], u_ref[:, a:b]
        sigmoid = jax.nn.sigmoid(gate_pre)
        gg_ref[:, a:b] = (
            grad * up_pre * sigmoid * (1.0 + gate_pre * (1.0 - sigmoid))
        ).astype(bf16)
        gu_ref[:, a:b] = (grad * gate_pre * sigmoid).astype(bf16)
    wait_all(copies["gate"])
    part = dot_nt(gg_ref[...], gate[...])
    wait_all(copies["up"])
    out_ref[...] = (part + dot_nt(gu_ref[...], up[...])).astype(bf16)


def gate_forward(residual, own, moved, gain, w_gate, first):
    rows, width = residual.shape
    hidden = w_gate.shape[1]
    operands = [w_gate, *first[0], *first[1]]
    shapes = [((rows, width), f32), ((rows, width), bf16), ((rows, 1), f32), ((rows, hidden), f32)]
    return pl.pallas_call(
        gate_kernel,
        grid=(1,),
        in_specs=[whole(rows, width)] * 3 + [whole(1, width)] + [UNREAD] * len(operands),
        out_specs=[whole(*shape) for shape, _ in shapes],
        out_shape=[jax.ShapeDtypeStruct(*entry) for entry in shapes],
        scratch_shapes=[pltpu.VMEM((1536, 1920), bf16), pltpu.SemaphoreType.DMA((5,))],
        compiler_params=params(24),
        cost_estimate=SHORT,
    )(residual, own, moved, gain.reshape(1, width), *operands)


def ffn_forward(normed, gate_pre, weights):
    rows, width = normed.shape
    operands = weight_operands(*weights)
    hidden = gate_pre.shape[1]
    shapes = [((rows, hidden), f32), ((rows, hidden), bf16), ((rows, width), bf16)]
    return pl.pallas_call(
        ffn_forward_kernel,
        grid=(1,),
        in_specs=[whole(rows, width)] + [UNREAD] * (1 + len(operands)),
        out_specs=[whole(*shape) for shape, _ in shapes],
        out_shape=[jax.ShapeDtypeStruct(*entry) for entry in shapes],
        scratch_shapes=WEIGHT_SCRATCH[1:]
        + [pltpu.VMEM((rows, hidden), f32), pltpu.SemaphoreType.DMA((1,))],
        compiler_params=params(38),
        cost_estimate=SHORT,
    )(normed, gate_pre, *operands)


def ffn_backward(branch, gate_pre, up_pre, weights, held):
    rows, width = branch.shape
    operands = weight_operands(*weights)
    hidden = weights[2].shape[0]
    shapes = [((rows, hidden), bf16), ((rows, hidden), bf16), ((rows, width), bf16)]
    return pl.pallas_call(
        ffn_backward_kernel,
        grid=(1,),
        in_specs=[whole(rows, width)] + [UNREAD] * (2 + len(operands) + len(held)),
        out_specs=[whole(*shape) for shape, _ in shapes],
        out_shape=[jax.ShapeDtypeStruct(*entry) for entry in shapes],
        scratch_shapes=WEIGHT_SCRATCH
        + [pltpu.VMEM((rows, hidden), f32)] * 2
        + [pltpu.SemaphoreType.DMA((2,))],
        compiler_params=params(44),
        cost_estimate=SHORT,
    )(branch, gate_pre, up_pre, *operands, *held)


def hidden_tile(rows):
    return pl.BlockSpec((rows, TILE), lambda i: (0, i))


def projection_kernel(n_own, n_other, wq, wk, wv, one, two, *rest):
    out_ref = rest[-1]
    own = n_own[...]
    first, second = n_other[:, :384], n_other[:, 384:]
    rows = own.shape[0]
    for p in range(2):
        place = pl.ds(p * rows, rows)
        q_at, kv_at = slice(p * 384, p * 384 + 384), slice(p * 128, p * 128 + 128)
        for weight, own_at, at, out_at in (
            (wq, q_at, p * 384, slice(0, 384)),
            (wk, kv_at, 768 + p * 128, slice(384, 512)),
            (wv, kv_at, 1024 + p * 128, slice(512, 640)),
        ):
            there = slice(at, at + out_at.stop - out_at.start)
            out_ref[place, out_at] = (
                dot(own, weight[:, own_at])
                + dot(first, one[:, there])
                + dot(second, two[:, there])
            ).astype(bf16)


def projection_backward_kernel(colour, g_ref, wq, wk, wv, one, two, *rest):
    out_ref = rest[-1]
    grad = jnp.concatenate(
        [
            g_ref[:, a:b]
            for a, b in ((0, 384), (640, 1024), (384, 512), (1024, 1152), (512, 640), (1152, 1280))
        ],
        axis=1,
    )
    out_ref[:, 0:768] = (
        dot_nt(grad[:, 0:768], wq[...])
        + dot_nt(grad[:, 768:1024], wk[...])
        + dot_nt(grad[:, 1024:1280], wv[...])
    ).astype(bf16)
    first = dot_nt(grad, one[...]).astype(bf16)
    second = dot_nt(grad, two[...]).astype(bf16)

    @pl.when(colour[0] == 0)
    def _():
        out_ref[:, 768:1152] = first
        out_ref[:, 1152:1536] = second

    @pl.when(colour[0] != 0)
    def _():
        out_ref[:, 768:1152] = second
        out_ref[:, 1152:1536] = first


def projection_backward(colour, held, *operands):
    rows = operands[0].shape[0]
    return pl.pallas_call(
        projection_backward_kernel,
        grid=(1,),
        in_specs=[SMEM] + [whole(*operand.shape) for operand in operands] + [UNREAD] * len(held),
        out_specs=whole(rows, 1536),
        out_shape=jax.ShapeDtypeStruct((rows, 1536), bf16),
        compiler_params=params(),
        cost_estimate=SHORT,
    )(colour.reshape(1), *operands, *held)


def out_blocks(pieces):
    operands = [piece for piece in pieces for _ in range(2)]
    specs = [pl.BlockSpec((192, 384), lambda i, k=k: (0, k)) for k in (5, 6)] * 4
    return operands, specs


def out_columns(refs):
    return jnp.concatenate([ref[...] for ref in refs], axis=0)


def out_projection_kernel(back_ref, w_ref, *refs):
    part_ref, attended_ref = refs[-2:]
    rows = attended_ref.shape[0]
    attended = jnp.concatenate([back_ref[0:rows], back_ref[rows : 2 * rows]], axis=1)
    attended_ref[...] = attended
    part_ref[:, 0:768] = dot(attended, w_ref[...]).astype(bf16)
    part_ref[:, 768:1152] = dot(attended, out_columns(refs[0:4])).astype(bf16)
    part_ref[:, 1152:1536] = dot(attended, out_columns(refs[4:8])).astype(bf16)


def out_projection(back, w_out, pieces, held):
    rows = back.shape[0] // 2
    operands, specs = out_blocks(pieces)
    return pl.pallas_call(
        out_projection_kernel,
        grid=(1,),
        in_specs=[whole(*back.shape), whole(*w_out.shape)] + specs + [UNREAD] * len(held),
        out_specs=(whole(rows, 1536), whole(rows, 768)),
        out_shape=(
            jax.ShapeDtypeStruct((rows, 1536), bf16),
            jax.ShapeDtypeStruct((rows, 768), bf16),
        ),
        compiler_params=params(),
        cost_estimate=SHORT,
    )(back, w_out, *operands, *held)


def out_backward_kernel(b_ref, w_ref, *refs):
    out_ref = refs[-1]
    rows = b_ref.shape[0]
    grad = (
        dot_nt(b_ref[:, 0:768], w_ref[...])
        + dot_nt(b_ref[:, 768:1152], out_columns(refs[0:4]))
        + dot_nt(b_ref[:, 1152:1536], out_columns(refs[4:8]))
    ).astype(bf16)
    out_ref[0:rows] = grad[:, 0:384]
    out_ref[rows : 2 * rows] = grad[:, 384:768]


def out_backward(branch, w_out, pieces):
    rows = branch.shape[0]
    operands, specs = out_blocks(pieces)
    return pl.pallas_call(
        out_backward_kernel,
        grid=(1,),
        in_specs=[whole(*branch.shape), whole(*w_out.shape)] + specs,
        out_specs=whole(2 * rows, 384),
        out_shape=jax.ShapeDtypeStruct((2 * rows, 384), bf16),
        compiler_params=params(),
        cost_estimate=SHORT,
    )(branch, w_out, *operands)


def projection(*operands):
    rows = operands[0].shape[0]
    return pl.pallas_call(
        projection_kernel,
        in_specs=[pl.BlockSpec(memory_space=pltpu.VMEM)] * 7 + [UNREAD] * (len(operands) - 7),
        out_shape=jax.ShapeDtypeStruct((2 * rows, 640), bf16),
        compiler_params=params(),
        cost_estimate=SHORT,
    )(*operands)


def merge_kernel(q_ref, own, newer, older, *rest):
    out_ref = rest[-1]
    out_ref[:, 0:384] = q_ref[...]
    out_ref[:, 384:640] = (
        own[...] + newer[...].astype(f32) + older[...].astype(f32)
    ).astype(bf16)


def merge(grad_queries, own, newer, older, held):
    operands = (grad_queries, own, newer, older)
    return pl.pallas_call(
        merge_kernel,
        grid=(1,),
        in_specs=[whole(*operand.shape) for operand in operands] + [UNREAD] * len(held),
        out_specs=whole(512, 640),
        out_shape=jax.ShapeDtypeStruct((512, 640), bf16),
        compiler_params=params(),
        cost_estimate=SHORT,
    )(*operands, *held)


def ffn_gradients_kernel(normed, branch, gate, up, act, m_one, m_two, l_one, l_two, *rest):
    out_ref, n_all, b_all, gate_all, up_all, act_all, total, in_sems, out_sems = rest[-9:]
    rows, width, hidden = 256, 768, 1920
    copies = {}
    for name, own, received, at, target in (
        ("normed", normed, (m_one, m_two), 0, n_all),
        ("gate", gate, (l_one, l_two), width, gate_all),
        ("up", up, (l_one, l_two), width + hidden, up_all),
        ("act", act, (m_one, m_two), width, act_all),
        ("branch", branch, (l_one, l_two), 0, b_all),
    ):
        columns = target.shape[1]
        parts = [(own.at[:, pl.ds(0, columns)], target.at[pl.ds(0, rows), :])]
        for k, part in enumerate(received):
            parts.append(
                (
                    part.at[:, pl.ds(at, columns)],
                    target.at[pl.ds(rows + 128 * k, 128), :],
                )
            )
        base = 3 * len(copies)
        copies[name] = [
            pltpu.make_async_copy(source, place, in_sems.at[base + k])
            for k, (source, place) in enumerate(parts)
        ]
        for copy in copies[name]:
            copy.start()

    def send(k):
        place = pl.ds(k * width, width)
        copy = pltpu.make_async_copy(total.at[place, :], out_ref.at[place, :], out_sems.at[k])
        copy.start()
        return copy

    wait_all(copies["normed"])
    wait_all(copies["gate"])
    for a, b in CHUNKS:
        total[0:width, a:b] = dot_tn(n_all[...], gate_all[:, a:b]).astype(bf16)
    sent = [send(0)]
    wait_all(copies["up"])
    for a, b in CHUNKS:
        total[width : 2 * width, a:b] = dot_tn(n_all[...], up_all[:, a:b]).astype(bf16)
    sent.append(send(1))
    wait_all(copies["act"])
    wait_all(copies["branch"])
    for a, b in CHUNKS:
        down = dot_tn(act_all[:, a:b], b_all[...]).astype(bf16)
        for r in range(width // 128):
            for c in range((b - a) // 128):
                total[
                    2 * width + r * 128 : 2 * width + r * 128 + 128, a + c * 128 : a + c * 128 + 128
                ] = down[c * 128 : c * 128 + 128, r * 128 : r * 128 + 128]
    sent.append(send(2))
    wait_all(sent)


def ffn_gradients(normed, branch, gate, up, act, middle, late, held):
    operands = (normed, branch, gate, up, act, *middle, *late, *held)
    return pl.pallas_call(
        ffn_gradients_kernel,
        grid=(1,),
        in_specs=[UNREAD] * len(operands),
        out_specs=pl.BlockSpec(memory_space=pltpu.HBM),
        out_shape=jax.ShapeDtypeStruct((2304, 1920), bf16),
        scratch_shapes=[pltpu.VMEM((512, 768), bf16)] * 2
        + [pltpu.VMEM((512, 1920), bf16)] * 3
        + [
            pltpu.VMEM((2304, 1920), bf16),
            pltpu.SemaphoreType.DMA((15,)),
            pltpu.SemaphoreType.DMA((3,)),
        ],
        compiler_params=params(40),
        cost_estimate=SHORT,
    )(*operands)


CHANNELS = (0, 640, 1152, 1664, 2176)


def attention_gradients_kernel(bits, *refs):
    normed, projected, attended, branch = refs[0:4]
    early, last, branch_moved = refs[4:6], refs[6:8], refs[8:10]
    outs, total = refs[11:-1], refs[-1]
    total[:, 2048:2176] = refs[10][...]

    def rows_of(own, received, at, width):
        parts = [own[:, :width]] + [ref[:, at : at + width] for ref in received]
        return jnp.concatenate(parts, axis=0)

    total[:, 0:768] = dot_tn(
        rows_of(attended, early, 768, 768), rows_of(branch, branch_moved, 0, 768)
    ).astype(bf16)
    total[:, 768:2048] = dot_tn(
        rows_of(normed, early, 0, 768), rows_of(projected, last, 0, 1280)
    ).astype(bf16)
    for c in range(4):
        columns = slice(CHANNELS[c], CHANNELS[c + 1])
        keep = pl.multiple_of(bits[c] * 384, 384)
        send = pl.multiple_of(384 - bits[c] * 384, 384)
        outs[2 * c][...] = total[pl.ds(keep, 384), columns]
        outs[2 * c + 1][...] = total[pl.ds(send, 384), columns]


def attention_gradients(bits, *operands):
    widths = [b - a for a, b in zip(CHANNELS[:-1], CHANNELS[1:]) for _ in range(2)]
    return list(
        pl.pallas_call(
            attention_gradients_kernel,
            grid=(1,),
            in_specs=[SMEM] + [whole(*operand.shape) for operand in operands],
            out_specs=[whole(384, w) for w in widths],
            out_shape=[jax.ShapeDtypeStruct((384, w), bf16) for w in widths],
            scratch_shapes=[pltpu.VMEM((768, 2176), bf16)],
            compiler_params=params(),
            cost_estimate=SHORT,
        )(bits, *operands)
    )


def ffn_results_kernel(one, two, total_hbm, *refs):
    outs, total, f_gate, f_up, f_down, in_sems, out_sems = refs[0:3], *refs[3:]
    width, hidden = 768, 1920
    targets = (f_gate, f_up, f_down)
    chunks = []
    for m in range(2):
        for r in range(2):
            place = pl.ds(m * width + r * 384, 384)
            chunks.append((m, r, (place, pl.ds(0, hidden)), (pl.ds(r * 384, 384), pl.ds(0, hidden))))
    for r, (a, b) in enumerate(CHUNKS):
        place = (pl.ds(2 * width, width), pl.ds(a, b - a))
        chunks.append((2, r, place, (pl.ds(a, b - a), pl.ds(0, width))))
    arriving, leaving = [], []
    for k, (_, _, place, _) in enumerate(chunks):
        arriving.append(
            pltpu.make_async_copy(total_hbm.at[place], total.at[place], in_sems.at[k])
        )
        arriving[-1].start()
    scale = TOKENS / count_of(one, two)
    for k, (m, r, _, there) in enumerate(chunks):
        arriving[k].wait()
        if m < 2:
            rows = slice(r * 384, r * 384 + 384)
            source = slice(m * width + r * 384, m * width + r * 384 + 384)
            targets[m][rows] = total[source].astype(f32) * scale
        else:
            a, b = CHUNKS[r]
            for p in range(a // 128, b // 128):
                for q in range(width // 128):
                    f_down[p * 128 : p * 128 + 128, q * 128 : q * 128 + 128] = (
                        total[
                            2 * width + q * 128 : 2 * width + q * 128 + 128,
                            p * 128 : p * 128 + 128,
                        ].astype(f32)
                        * scale
                    )
        leaving.append(
            pltpu.make_async_copy(targets[m].at[there], outs[m].at[there], out_sems.at[k])
        )
        leaving[-1].start()
    wait_all(leaving)


def ffn_results(pair, total):
    width, hidden = total.shape[0] // 3, total.shape[1]
    shapes = ((width, hidden), (width, hidden), (hidden, width))
    hbm = pl.BlockSpec(memory_space=pltpu.HBM)
    return pl.pallas_call(
        ffn_results_kernel,
        grid=(1,),
        in_specs=[whole(*value.shape) for value in pair] + [hbm],
        out_specs=[hbm] * 3,
        out_shape=[jax.ShapeDtypeStruct(shape, f32) for shape in shapes],
        scratch_shapes=[pltpu.VMEM(total.shape, bf16)]
        + [pltpu.VMEM(shape, f32) for shape in shapes]
        + [pltpu.SemaphoreType.DMA((6,)), pltpu.SemaphoreType.DMA((6,))],
        compiler_params=params(58),
        cost_estimate=SHORT,
    )(*pair, total)


PLACES = (
    (0, 0, 640, 3, 0),
    (1, 0, 128, 3, 640),
    (1, 128, 384, 0, 0),
    (2, 0, 128, 1, 0),
    (2, 128, 128, 2, 0),
    (2, 256, 256, 0, 384),
    (3, 0, 128, 0, 640),
    (3, 128, 128, 1, 128),
    (3, 256, 128, 2, 128),
)


def count_of(ref_one, ref_two):
    total = None
    for ref in (ref_one, ref_two):
        for lane in (32, 96):
            part = jnp.sum(ref[:, 384 + lane : 385 + lane].astype(f32), axis=0, keepdims=True)
            total = part if total is None else total + part
    return total


def attention_results_kernel(bits, *refs):
    outs, rows_ref, tile = refs[8:12], refs[12], refs[13]
    count = count_of(refs[6], refs[7])
    scale = TOKENS / count
    for c, at, width, out, there in PLACES:
        for side in range(2):
            first = bits[c] * 384 if side == 0 else 384 - bits[c] * 384
            outs[out][pl.ds(pl.multiple_of(first, 384), 384), there : there + width] = (
                refs[2 * c + side][:, at : at + width].astype(f32) * scale
            )
    for side in range(2):
        first = bits[3] * 384 if side == 0 else 384 - bits[3] * 384
        tile[pl.ds(pl.multiple_of(first, 384), 384), :] = refs[6 + side][:, 384:512].astype(f32)
    lines = jnp.transpose(tile[...])
    rows_ref[0:1] = (lines[0:1] + lines[72:73]) * scale
    rows_ref[1:2] = (lines[16:17] + lines[88:89]) * scale
    squares = jnp.sum(lines[40:41] + lines[104:105], axis=1, keepdims=True)
    rows_ref[2:3] = jnp.broadcast_to(squares / count, (1, 768))
    rows_ref[3:4] = jnp.broadcast_to(scale, (1, 768))


def attention_results(bits, pairs):
    operands = [value for pair in pairs for value in pair]
    widths = (768, 256, 256, 768)
    return pl.pallas_call(
        attention_results_kernel,
        grid=(1,),
        in_specs=[SMEM] + [whole(*operand.shape) for operand in operands],
        out_specs=[whole(768, width) for width in widths] + [whole(8, 768)],
        out_shape=[jax.ShapeDtypeStruct((768, width), f32) for width in widths]
        + [jax.ShapeDtypeStruct((8, 768), f32)],
        scratch_shapes=[pltpu.VMEM((768, 128), f32)],
        compiler_params=params(),
        cost_estimate=SHORT,
    )(bits, *operands)


def local(
    tokens,
    w_query,
    key_projection_weight,
    value_projection_weight,
    w_out,
    w_gate,
    w_up,
    w_down,
    norm_attn,
    norm_ffn,
    doc_lengths,
    valid_mask,
    teacher,
):
    seq_count, row_count, width = tokens.shape
    rows = seq_count * row_count
    half = width // 2
    quarter = width // 4
    dp = lax.axis_index("dp")
    colour = (lax.axis_index("x") + lax.axis_index("y")) % 2
    y_index = lax.axis_index("y")
    group_index = lax.axis_index("x") * 2 + lax.axis_index("z_hi")

    def to_local(value):
        own = jnp.where(dp == 0, value[..., :half], value[..., half:])
        other = jnp.where(dp == 0, value[..., half:], value[..., :half])
        first = jnp.where(colour == 0, other[..., :quarter], other[..., quarter:])
        second = jnp.where(colour == 0, other[..., quarter:], other[..., :quarter])
        return jnp.concatenate([own, first, second], axis=-1)

    def other_half_of(first, second):
        return jnp.concatenate(
            [jnp.where(colour == 0, first, second), jnp.where(colour == 0, second, first)], axis=-1
        )

    def other_half(value):
        return other_half_of(value[..., half : half + quarter], value[..., half + quarter :])

    def from_local(value):
        own, other = value[..., :half], other_half(value)
        return jnp.concatenate(
            [jnp.where(dp == 0, own, other), jnp.where(dp == 0, other, own)], axis=-1
        )

    def two_ways(first, second):
        return z_move(first, 1), z_move(second, -1)

    def over_x(one, two):
        return ring_move(one, "x", 1), ring_move(two, "x", -1)

    def over_y(one, two):
        return ring_move(one, "y", 1), ring_move(two, "y", -1)

    def to_neighbours(value):
        return two_ways(value[:row_count], value[row_count:])

    gains = jnp.stack([norm_attn, norm_ffn])
    gains_other = swap(gains, "dp")
    gains_first = jnp.where(colour == 0, gains_other[:, :quarter], gains_other[:, quarter:])
    gains_second = jnp.where(colour == 0, gains_other[:, quarter:], gains_other[:, :quarter])
    gains_full = jnp.concatenate([gains, gains_first, gains_second], axis=1).astype(f32)
    gain_one, gain_two = gains_full[0], gains_full[1]

    kv = key_projection_weight.shape[1]
    ff = w_gate.shape[1]
    sent = copy_blocks(
        colour,
        [
            [
                (w_query, (quarter, half), lambda c, k=k: (k, 0), 0, 0),
                (key_projection_weight, (quarter, kv), lambda c, k=k: (k, 0), 0, half),
                (value_projection_weight, (quarter, kv), lambda c, k=k: (k, 0), 0, half + kv),
            ]
            for k in range(2)
        ],
        [(quarter, half + 2 * kv)] * 2,
        (gains_other,),
    )
    qkv_one, qkv_two = two_ways(*sent)
    mask_values = valid_mask.reshape(rows).astype(f32)
    blocks = [
        [
            (w_gate, (192, ff), lambda c, k=k: (2 * c + k, 0), 0, 0),
            (w_out, (192, quarter), lambda c, k=k: (2 * k, c), 0, ff),
            (w_out, (192, quarter), lambda c, k=k: (2 * k + 1, c), 0, ff + quarter),
        ]
        for k in range(2)
    ]
    first_sent = copy_blocks(colour, blocks, [(192, ff + 2 * quarter)] * 2, (gains_other,))
    first_z = two_ways(*first_sent)

    residual_in = to_local(tokens.reshape(rows, width)).astype(f32)
    inverse_one = inverse_rms(residual_in)
    normed_one = (residual_in * inverse_one * gain_one).astype(bf16)
    normed_one_other = other_half(normed_one)
    projected = projection(
        normed_one[:, :half],
        normed_one_other,
        w_query,
        key_projection_weight,
        value_projection_weight,
        qkv_one,
        qkv_two,
        *first_sent,
    )
    mine = lax.all_to_all(projected, "y", 0, 0, tiled=True)
    queries, key_values = copy_blocks(
        colour,
        [
            [(mine, (512, 128), lambda c, k=k: (0, k), 0, 128 * (k - first)) for k in range(first, last)]
            for first, last in ((0, 3), (3, 5))
        ],
        [(512, 384), (512, 256)],
        (),
    )
    pieces = (group_move(key_values, 2), group_move(key_values, 1), key_values)
    blocks = [
        [(w_up, (192, ff), lambda c, k=k: (2 * c + k, 0), 0, 0)]
        + [
            (w_down, (192, quarter), lambda c, k=k, b=b: (5 * k + b, c), 0, ff + quarter * b)
            for b in range(5)
        ]
        for k in range(2)
    ]
    second_z = two_ways(*copy_blocks(colour, blocks, [(192, 2 * ff)] * 2, pieces[:2]))
    first = (first_z, over_x(*hold(first_z, pieces[0])))
    bounds = jnp.cumsum(lax.dynamic_index_in_dim(doc_lengths, y_index % 2, 0, keepdims=False))
    scalars = jnp.concatenate([(group_index * 512)[None], bounds]).astype(jnp.int32)
    attended_mine, logs = attention_forward(scalars, queries, pieces, ())
    returned = lax.all_to_all(attended_mine, "y", 0, 0, tiled=True)
    out_pieces = (*first[0], *first[1])
    attn_part, attended = out_projection(returned, w_out, out_pieces, ())
    split = copy_blocks(
        colour,
        [[(v, (192, ff), lambda c, k=k: (0, k), 0, 0)] for k in range(2) for v in second_z],
        [(192, ff)] * 4,
        (attn_part,),
    )
    second = (second_z, over_x(*split[:2]), over_y(*split[2:]))
    early = to_neighbours(jnp.concatenate([normed_one_other, attended], axis=1))
    weights = (w_gate, w_up, w_down, first, second)
    hidden_state, normed_two, inverse_two, gate_pre = gate_forward(
        residual_in, attn_part, swap(attn_part, "tensor"), gain_two, w_gate, first
    )
    up_pre, activated, ffn_part = ffn_forward(normed_two, gate_pre, weights)
    middle = to_neighbours(jnp.concatenate([other_half(normed_two), activated], axis=1))

    final_state = hidden_state + branch_scale * core_sum(ffn_part)
    deviation = final_state - to_local(teacher.reshape(rows, width)).astype(f32)
    row_squares = mask_values * jnp.mean(deviation * deviation, axis=-1)
    grad_final = deviation * mask_values[:, None]
    branch_two = (branch_scale * grad_final).astype(bf16)
    grad_gate_pre, grad_up_pre, part = ffn_backward(
        branch_two, gate_pre, up_pre, weights, (early[1][:16, :128],)
    )
    late = to_neighbours(
        jnp.concatenate([other_half(branch_two), grad_gate_pre, grad_up_pre], axis=1)
    )
    grad_normed_two = core_sum(part)

    grad_from_norm, gain_terms_two = norm_backward(
        hidden_state, inverse_two, gain_two, grad_normed_two
    )
    grad_hidden = grad_final + grad_from_norm
    branch_one = (branch_scale * grad_hidden).astype(bf16)
    grad_attended = out_backward(branch_one, w_out, out_pieces)
    branch_moved = to_neighbours(other_half(branch_one))
    grad_mine = lax.all_to_all(grad_attended, "y", 0, 0, tiled=True)
    grad_queries, grad_older, grad_newer, grad_own = attention_backward(
        scalars, queries, grad_mine, logs, pieces, ()
    )
    ffn_grads = ffn_gradients(
        normed_two, branch_two, grad_gate_pre, grad_up_pre, activated, middle, late, (grad_older,)
    )
    ffn_share = lax.psum_scatter(ffn_grads, ("x", "y"), scatter_dimension=0, tiled=True)
    older = group_move(grad_older, -2)
    newer = group_move(grad_newer, -1)
    grad_projected = lax.all_to_all(
        merge(grad_queries, grad_own, newer, older, branch_moved), "y", 0, 0, tiled=True
    )
    grad_projected = jnp.concatenate([grad_projected[:rows], grad_projected[rows:]], axis=1)
    last = to_neighbours(grad_projected)
    grad_normed_one = core_sum(
        projection_backward(
            colour,
            early[:1],
            grad_projected,
            w_query,
            key_projection_weight,
            value_projection_weight,
            qkv_one,
            qkv_two,
        )
    )
    gradient_via_first_norm, gain_terms_one = norm_backward(
        residual_in, inverse_one, gain_one, grad_normed_one
    )
    grad_tokens = from_local(grad_hidden + gradient_via_first_norm)

    ones = jnp.ones((rows, 128), f32)

    def column_sums(terms):
        return lax.dot_general(
            terms, ones, (((0,), (0,)), ((), ())), precision=lax.Precision.HIGHEST
        )

    def on_rows(values):
        return jnp.pad(jnp.broadcast_to(values[:, None], (rows, 128)), ((0, half - rows), (0, 0)))

    entries = [
        column_sums(gain_terms_one[:, :half]),
        column_sums(other_half(gain_terms_one)),
        column_sums(gain_terms_two[:, :half]),
        column_sums(other_half(gain_terms_two)),
        on_rows(mask_values),
        on_rows(row_squares),
    ]
    slot = lax.broadcasted_iota(jnp.int32, (half, 128), 1) // 8
    tile = jnp.zeros((half, 128), f32)
    for k, entry in enumerate(entries):
        tile = jnp.where(slot == k, entry, tile)
    bits = jnp.stack([pair_bit(steps[0]) for steps in FIRST]).astype(jnp.int32)
    cut_rows = attention_gradients(
        bits,
        normed_one,
        grad_projected,
        attended,
        branch_one,
        *early,
        *last,
        *branch_moved,
        tile.astype(bf16),
    )
    channels = [
        add_moved(cut_rows[2 * k], cut_rows[2 * k + 1], FIRST[k][0]) for k in range(4)
    ]
    (ffn_share,) = hold([ffn_share], *channels)
    channels = reduce_second(channels)
    pairs = [
        copy_blocks(
            colour,
            [
                [
                    (left, left.shape, lambda c: (0, 0), 0, 0),
                    (right, right.shape, lambda c: (0, 0), 0, left.shape[1]),
                ]
            ],
            [(left.shape[0], left.shape[1] + right.shape[1])],
            held,
        )[0]
        for left, right, held in (
            (channels[0], channels[1], (ffn_share,)),
            (channels[2], channels[3], (ffn_share,)),
        )
    ]
    ffn_share = z_sum(ffn_share)
    pairs = reduce_pairs(pairs, 0)
    (ffn_share,) = hold([ffn_share], *pairs)
    ffn_total_grads = lax.all_gather(ffn_share, ("x", "y"), axis=0, tiled=True)
    pairs = reduce_pairs(pairs, 1)
    pairs = reduce_rest(pairs, [c.shape[1] for c in channels])
    *attn_results, small = attention_results(bits, pairs)
    scale = small[3, 0]

    layer_out = from_local(final_state.astype(bf16)).reshape(seq_count, row_count, width)
    return (
        layer_out,
        small[2, 0],
        (grad_tokens * scale).reshape(seq_count, row_count, width),
        *attn_results,
        *ffn_results(pairs[3], ffn_total_grads),
        small[0],
        small[1],
    )


def solution(mesh):
    fine = Mesh(mesh.devices.reshape(2, 4, 2, 4, 2), ("dp", "x", "z_hi", "y", "tensor"))
    ctx = ("x", "z_hi", "y")
    return jax.shard_map(
        local,
        mesh=fine,
        in_specs=(
            P("dp", ctx, None),
            P("dp", "tensor"),
            P("dp", "tensor"),
            P("dp", "tensor"),
            P("tensor", "dp"),
            P("dp", "tensor"),
            P("dp", "tensor"),
            P("tensor", "dp"),
            P("dp"),
            P("dp"),
            P("dp", None),
            P("dp", ctx),
            P("dp", ctx, None),
        ),
        out_specs=(
            P("dp", ctx, None),
            P(),
            P("dp", ctx, None),
            P("dp", "tensor"),
            P("dp", "tensor"),
            P("dp", "tensor"),
            P("tensor", "dp"),
            P("dp", "tensor"),
            P("dp", "tensor"),
            P("tensor", "dp"),
            P("dp"),
            P("dp"),
        ),
        check_vma=False,
    )
```
